128 devices in a mesh: rx: 32 (over y, z, core), ry: 4 (over x).
Axes of the slice: x: 4, y: 4, z: 4, core: 2. Of those that a mesh axis runs over, the one named last changes fastest.
Arguments:
- matrix: float32 [524288, 256], P(('rx', 'ry')), may hold values from -6 to 6
- signs: int32 [524288], P(('rx', 'ry')), may hold values from -1 to 1, as said below
- indices: int32 [32768], P(('rx', 'ry')), may hold values from 0 to 4095, as said below
- counts: int32 [128], P(('rx', 'ry')), may hold values from 64 to 256, as said below
Outputs:
- sketch: float32 [32768, 256], P(('rx', 'ry'))
- gram_blocks: float32 [4, 128, 128], P('ry')
The draws below stay inside these ranges and needn't reach their ends.
Inputs may be any that keep to these rules, and one draw needn't show every extreme that they name: `signs`: each entry is -1 or 1. `indices`: local row numbers; repeats allowed; entries of dead slots are ignored. `counts`: some device has all 256 slots live.
All inputs are finite; a program needn't handle non-finite values.
Results may differ from the reference program's by a relative error of at most 0.00011.
Values sent between devices are 32-bit elements; how exact they have to be, the bound alone decides.
A program may use at most 64 MiB of HBM per device.

```python
import jax
import jax.numpy as jnp
from jax import lax

PANEL = 128
COLS = 256
BLK = 128
ROWS_DEV = 4096
CAP = 256
ROWS = 524288
SLOTS = 32768
N_RX = 32
N_RY = 4


def draw_signs(key, part):
    key = jax.random.fold_in(key, 11)
    return (2 * jax.random.randint(key, (ROWS,), 0, 2) - 1).astype(jnp.int32)


def draw_indices(key, part):
    key = jax.random.fold_in(key, 12)
    return jax.random.randint(key, (SLOTS,), 0, ROWS_DEV).astype(jnp.int32)


def draw_counts(key, part):
    key = jax.random.fold_in(key, 13)
    first, second = jax.random.split(key)
    values = jax.random.randint(first, (N_RX * N_RY,), CAP // 4, CAP + 1)
    fullest = jax.random.randint(second, (), 0, N_RX * N_RY)
    return values.at[fullest].set(CAP).astype(jnp.int32)


def levels(key, shape, cuts, least, largest):
    gain, own = 1.0, jax.random.fold_in(key, 6)
    for axis_at, shards_of in cuts:
        heights = jnp.exp(jax.random.uniform(jax.random.fold_in(own, axis_at), (shards_of,), jnp.float32, least / len(cuts), largest / len(cuts)))
        gain = gain * jnp.repeat(heights, shape[axis_at] // shards_of).reshape([-1 if axis == axis_at else 1 for axis in range(len(shape))])
    return gain


def normal_values(rng, dims, spread, limit, shards=(), kind=jnp.bfloat16):
    drawn = spread * jax.random.normal(rng, dims, jnp.float32)
    if shards:
        drawn = drawn * levels(rng, dims, shards, -0.22, 0.18)
    return jnp.clip(drawn, -limit, limit).astype(kind)


def setup_inputs(seed: int = 0) -> dict:
    seeds = jax.random.split(jax.random.key(seed), 5)
    return {
        "matrix": normal_values(seeds[0], (ROWS, COLS), 1.0, 6.0, ((0, 128),), jnp.float32),
        "signs": draw_signs(jax.random.fold_in(seeds[4], 71), 0),
        "indices": draw_indices(jax.random.fold_in(seeds[4], 71), 0),
        "counts": draw_counts(jax.random.fold_in(seeds[4], 71), 0),
    }


def hadamard(order):
    idx = jnp.arange(order, dtype=jnp.int32)
    both = jnp.bitwise_and(idx[:, None], idx[None, :])
    parity = jnp.zeros((order, order), jnp.int32)
    for shift in range(order.bit_length() - 1):
        parity = parity + jnp.bitwise_and(jnp.right_shift(both, shift), 1)
    return (1 - 2 * (parity % 2)).astype(jnp.float32)


def reference(matrix, signs, indices, counts):
    groups = N_RX * N_RY
    signed = matrix * signs[:, None].astype(jnp.float32)
    blocks = signed.reshape(ROWS // BLK, BLK, COLS)
    local = jnp.einsum("ij,bjc->bic", hadamard(BLK), blocks, precision=lax.Precision.HIGHEST)
    depth = groups.bit_length() - 1
    mixed = local.reshape((2,) * depth + (ROWS_DEV, COLS))
    for axis in range(depth):
        first = jnp.take(mixed, 0, axis)
        second = jnp.take(mixed, 1, axis)
        mixed = jnp.stack([first + second, first - second], axis)
    mixed = mixed.reshape(groups, ROWS_DEV, COLS) * (1.0 / (groups * BLK) ** 0.5)
    where_rows = indices.reshape(groups, CAP)
    live = jnp.arange(CAP, dtype=jnp.int32)[None, :] < counts[:, None]
    picked = jnp.take_along_axis(mixed, where_rows[:, :, None], axis=1)
    sketch = jnp.where(live[:, :, None], picked, jnp.float32(0.0)).reshape(groups * CAP, COLS)
    gram = jnp.dot(sketch.T, sketch, precision=lax.Precision.HIGHEST) * (1.0 / (groups * CAP))
    gram_blocks = gram.reshape(2, PANEL, 2, PANEL).transpose(0, 2, 1, 3).reshape(4, PANEL, PANEL)
    return sketch, gram_blocks
```

```python
import functools

import jax
import jax.numpy as jnp
from jax import lax
from jax.experimental import pallas as pl
from jax.experimental.pallas import tpu as pltpu
from jax.sharding import PartitionSpec as P

MESH = pl.DeviceIdType.MESH
BLK = 128
HALF = 64
PARTS = (
    (0, "y", "x", "z"),
    (0, "x", "z", "y"),
    (1, "y", "z", "x"),
    (1, "z", "x", "y"),
)


def coords():
    rx = lax.axis_index("rx")
    return {"y": rx // 8, "z": (rx // 2) % 4, "c": rx % 2, "x": lax.axis_index("ry")}


def device(at):
    return ((at["y"] * 4 + at["z"]) * 2 + at["c"], at["x"])


def moved(at, **to):
    return device({**at, **to})


def sign4(a, b):
    odd = (a % 2) * (b % 2) + (a // 2) * (b // 2)
    return (1 - 2 * (odd % 2)).astype(jnp.float32)


def hadamard(n):
    both = lax.broadcasted_iota(jnp.int32, (n, n), 0) & lax.broadcasted_iota(jnp.int32, (n, n), 1)
    both = both ^ (both >> 4)
    both = both ^ (both >> 2)
    both = both ^ (both >> 1)
    return (1 - 2 * (both & 1)).astype(jnp.float32)


def kernel(
    x_hbm, sg, idx, cnt, sk_out, gr_out,
    xm, xo, so, had, a, b, c, d0, d1, d2, d3, e, f, g, h,
    tile, ly, lz, pzy, pxy, pxz, szy, sxy, sxz, gp, rb, co, ob,
    loc_sem, core_s, core_r, st_s, st_r, ix_s, ix_r, sm_sem, rs_s, rs_r, ag_s, ag_r,
):
    me = coords()
    done = (d0, d1, d2, d3)
    lane = lax.broadcasted_iota(jnp.int32, (1, 128), 1) < HALF
    other = moved(me, c=1 - me["c"])

    def local(panel):
        cols = pl.ds(panel * 128, 128)
        return pltpu.make_async_copy(x_hbm.at[:, cols], xm.at[:, cols], loc_sem.at[panel])

    def remote(src, dst, send, recv, to):
        return pltpu.make_async_remote_copy(
            src_ref=src, dst_ref=dst, send_sem=send, recv_sem=recv, device_id=to, device_id_type=MESH
        )

    for panel in range(2):
        local(panel).start()

    barrier = pltpu.get_barrier_semaphore()

    def greet(o, _):
        to = moved(me, y=(me["y"] + o // 16) % 4, z=(me["z"] + (o // 4) % 4) % 4, x=(me["x"] + o % 4) % 4)
        pl.semaphore_signal(barrier, inc=1, device_id=to, device_id_type=MESH)
        return 0

    pl.semaphore_signal(barrier, inc=1, device_id=other, device_id_type=MESH)
    lax.fori_loop(1, 64, greet, 0)

    had[...] = hadamard(BLK)
    rows = idx[...]
    tile[...] = jnp.zeros_like(tile)
    tile[pl.ds(0, 1), :] = rows[0:1, :]
    tile[pl.ds(1, 1), :] = rows[1:2, :] ^ 2048
    pl.semaphore_wait(barrier, 64)

    def core(i):
        if i == 2:
            return remote(sg, so, core_s.at[i], core_r.at[i], other)
        cols = pl.ds(i * 128, 128)
        return remote(x_hbm.at[:, cols], xo.at[:, cols], core_s.at[i], core_r.at[i], other)

    core(2).start()
    core(0).start()
    core(1).start()

    def line(buf, axis, n, dist):
        at = (me[axis] + dist) % 4
        mine = pl.ds(pl.multiple_of(me[axis] * 8, 8), 8)
        i = n * 3 + dist - 1
        return remote(tile, buf.at[mine, :], ix_s.at[i], ix_r.at[i], moved(me, **{axis: at}))

    def plane(src, buf, axis, n, dist):
        at = (me[axis] + dist) % 4
        mine = pl.ds(pl.multiple_of(me[axis] * 32, 32), 32)
        i = 6 + n * 3 + dist - 1
        return remote(src, buf.at[mine, :], ix_s.at[i], ix_r.at[i], moved(me, **{axis: at}))

    lines = ((ly, "y", 0), (lz, "z", 1))
    planes = ((ly, pzy, "z", 0), (ly, pxy, "x", 1), (lz, pxz, "x", 2))
    for buf, axis, n in lines:
        for dist in (1, 2, 3):
            line(buf, axis, n, dist).start()
        buf[pl.ds(pl.multiple_of(me[axis] * 8, 8), 8), :] = tile[...]

    def exchange(stage, part, dist):
        axis = PARTS[part][1 if stage < 2 else stage]
        at = (me[axis] + dist) % 4
        src, dst = ((a, b), (c, None), (e, f), (g, h))[stage]
        size = 128 if stage == 3 else 512
        i = (stage * 4 + part) * 3 + dist - 1
        mine = pl.ds(pl.multiple_of(me[axis] * size, size), size)
        return remote(
            src.at[part, pl.ds(pl.multiple_of(at * size, size), size), :],
            done[part].at[mine, :] if stage == 1 else dst.at[part, mine, :],
            st_s.at[i], st_r.at[i], moved(me, **{axis: at}),
        )

    def send(stage, part):
        for dist in (1, 2, 3):
            exchange(stage, part, dist).start()

    def arrive(stage, part):
        for dist in (1, 2, 3):
            exchange(stage, part, dist).wait_recv()

    def start_part(panel):
        sign = (1 - 2 * me["c"]).astype(jnp.float32)
        cols = pl.ds(panel * 128, 128)

        def block(at):
            place = pl.ds(pl.multiple_of(at * BLK, BLK), BLK)
            s0 = sg[pl.ds(at, 1), :].astype(jnp.float32) * sign
            s1 = so[pl.ds(at, 1), :].astype(jnp.float32)
            hm = had[...]
            left = jnp.concatenate([hm * s0, hm * s1], axis=1).astype(jnp.bfloat16)
            both = jnp.concatenate([xm[place, cols], xo[place, cols]], axis=0)
            hi = both.astype(jnp.bfloat16)
            lo = (both - hi.astype(jnp.float32)).astype(jnp.bfloat16)
            out = jnp.dot(left, jnp.concatenate([hi, lo], axis=1), preferred_element_type=jnp.float32)
            return out[:, :128] + out[:, 128:]

        def pair(i, _):
            lo, hi = block(i), block(i + 16)
            place = pl.ds(pl.multiple_of(i * BLK, BLK), BLK)
            a[2 * panel, place, :] = jnp.where(lane, lo, pltpu.roll(hi, HALF, 1))
            a[2 * panel + 1, place, :] = jnp.where(lane, pltpu.roll(lo, HALF, 1), hi)
            return 0

        lax.fori_loop(0, 16, pair, 0)

    def own(axis, size):
        return pl.ds(pl.multiple_of(me[axis] * size, size), size)

    def transform(part):
        def step(i, _):
            v = [b[part, pl.ds(pl.multiple_of(q * 512 + i * 32, 32), 32), :] for q in range(4)]
            s, t, u, w = v[0] + v[1], v[0] - v[1], v[2] + v[3], v[2] - v[3]
            for q, out in enumerate((s + u, t + w, s - u, t - w)):
                c[part, pl.ds(pl.multiple_of(q * 512 + i * 32, 32), 32), :] = out
            return 0

        lax.fori_loop(0, 16, step, 0)

    def whole(part):
        axis = PARTS[part][1]
        b[part, own(axis, 512), :] = a[part, own(axis, 512), :]
        arrive(0, part)
        transform(part)
        send(1, part)
        done[part][own(axis, 512), :] = c[part, own(axis, 512), :]

    def gather(part, m, dst):
        table, swap = ((sxz, False), (szy, False), (sxz, True), (sxy, False))[part]
        rows = done[part]

        def some(i, _):
            l, k0 = i // 8, (i % 8) * 16
            row = ((l * 4 + m) if swap else (m * 4 + l)) * 8
            for u in range(16):
                lo = rows[pl.ds(table[row, k0 + u], 1), :]
                hi = rows[pl.ds(table[row + 1, k0 + u], 1), :]
                dst[part, pl.ds(m * 512 + i * 16 + u, 1), :] = jnp.where(lane, lo, hi)
            return 0

        lax.fori_loop(0, 32, some, 0)

    def pruned(part):
        axis = PARTS[part][2]
        arrive(1, part)

        def turn(i, _):
            v = done[part][pl.ds(pl.multiple_of(i * 64, 64), 64), :]
            done[part][pl.ds(pl.multiple_of(2048 + i * 64, 64), 64), :] = pltpu.roll(v, HALF, 1)
            return 0

        lax.fori_loop(0, 32, turn, 0)
        for dist in (1, 2, 3):
            gather(part, (me[axis] + dist) % 4, e)
            exchange(2, part, dist).start()
        gather(part, me[axis], f)

    def add_up(part, src, size, axis):
        signs = [sign4(me[axis], jnp.int32(q)) for q in range(4)]

        def at(start, count):
            total = src[part, pl.ds(start, count), :]
            for q in range(1, 4):
                total = total + signs[q] * src[part, pl.ds(pl.multiple_of(q * size + start, 8), count), :]
            return total

        return at

    def last(part):
        axis = PARTS[part][3]
        arrive(2, part)
        sums = add_up(part, f, 512, PARTS[part][2])

        def step(i, _):
            start = pl.multiple_of(i * 32, 32)
            g[part, pl.ds(start, 32), :] = sums(start, 32)
            return 0

        lax.fori_loop(0, 16, step, 0)
        send(3, part)
        h[part, own(axis, 128), :] = g[part, own(axis, 128), :]

    def final(part):
        arrive(3, part)
        return add_up(part, h, 128, PARTS[part][3])(0, 128)

    local(0).wait()
    core(2).wait_recv()
    core(0).wait_recv()
    start_part(0)
    send(0, 0)
    send(0, 1)
    local(1).wait()
    core(1).wait_recv()
    start_part(1)
    send(0, 3)
    send(0, 2)

    for buf, axis, n in lines:
        for dist in (1, 2, 3):
            line(buf, axis, n, dist).wait_recv()
    for src, buf, axis, n in planes:
        for dist in (1, 2, 3):
            plane(src, buf, axis, n, dist).start()
        buf[pl.ds(pl.multiple_of(me[axis] * 32, 32), 32), :] = src[...]

    whole(1)
    whole(0)
    whole(3)
    for i, (src, buf, axis, n) in enumerate(planes):
        for dist in (1, 2, 3):
            plane(src, buf, axis, n, dist).wait_recv()
        pltpu.make_async_copy(buf, (szy, sxy, sxz)[i], sm_sem.at[i]).start()
    whole(2)
    for i, (src, buf, axis, n) in enumerate(planes):
        pltpu.make_async_copy(buf, (szy, sxy, sxz)[i], sm_sem.at[i]).wait()

    pruned(1)
    pruned(3)
    pruned(0)
    last(1)
    last(3)
    pruned(2)
    last(0)
    last(2)

    scale = 1.0 / (128 * BLK) ** 0.5
    slot = lax.broadcasted_iota(jnp.int32, (128, 1), 0)
    count = cnt[0]
    for panel in range(2):
        p1 = final(2 * panel + 1)
        p0 = final(2 * panel)
        cols = pl.ds(panel * 128, 128)
        lo = jnp.where(lane, p0, pltpu.roll(p1, HALF, 1)) * scale
        hi = jnp.where(lane, pltpu.roll(p0, HALF, 1), p1) * scale
        sk_out[pl.ds(0, 128), cols] = jnp.where(slot < count, lo, 0.0)
        sk_out[pl.ds(128, 128), cols] = jnp.where(slot + 128 < count, hi, 0.0)

    sk = sk_out[...]
    hi = sk.astype(jnp.bfloat16)
    lo = (sk - hi.astype(jnp.float32)).astype(jnp.bfloat16)

    def dot_t(p, q):
        return lax.dot_general(p, q, (((0,), (0,)), ((), ())), preferred_element_type=jnp.float32)

    gram = dot_t(hi, hi) + dot_t(hi, lo) + dot_t(lo, hi)
    for i in range(4):
        gp[pl.ds(i * 128, 128), :] = gram[i // 2 * 128 : i // 2 * 128 + 128, i % 2 * 128 : i % 2 * 128 + 128]

    here = me["y"] * 4 + me["z"]

    def piece(o):
        to = {"y": (me["y"] + o // 16) % 4, "z": (me["z"] + (o // 4) % 4) % 4, "x": (me["x"] + o % 4) % 4}
        src = pl.multiple_of(to["x"] * 128 + (to["y"] * 4 + to["z"]) * 8, 8)
        dst = pl.multiple_of((here * 4 + me["x"]) * 8, 8)
        return remote(gp.at[pl.ds(src, 8), :], rb.at[pl.ds(dst, 8), :], rs_s.at[o], rs_r.at[o], moved(me, **to))

    lax.fori_loop(1, 64, lambda o, _: (piece(o).start(), 0)[1], 0)
    rb[pl.ds(pl.multiple_of((here * 4 + me["x"]) * 8, 8), 8), :] = gp[
        pl.ds(pl.multiple_of(me["x"] * 128 + here * 8, 8), 8), :
    ]
    lax.fori_loop(1, 64, lambda o, _: (piece(o).wait_recv(), 0)[1], 0)
    co[pl.ds(0, 8), :] = rb[...].reshape(64, 8, 128).sum(0)
    swap = remote(co.at[pl.ds(0, 8), :], co.at[pl.ds(8, 8), :], core_s.at[3], core_r.at[3], other)
    swap.start()
    swap.wait_recv()
    mine = pl.ds(pl.multiple_of(here * 8, 8), 8)
    ob[mine, :] = (co[pl.ds(0, 8), :] + co[pl.ds(8, 8), :]) * (1.0 / (128 * 256))

    def share(o):
        to = {"y": (me["y"] + o // 4) % 4, "z": (me["z"] + o % 4) % 4}
        return remote(ob.at[mine, :], ob.at[mine, :], ag_s.at[o], ag_r.at[o], moved(me, **to))

    lax.fori_loop(1, 16, lambda o, _: (share(o).start(), 0)[1], 0)
    lax.fori_loop(1, 16, lambda o, _: (share(o).wait_recv(), 0)[1], 0)
    gr_out[...] = ob[...]

    lax.fori_loop(1, 16, lambda o, _: (share(o).wait_send(), 0)[1], 0)
    swap.wait_send()
    lax.fori_loop(1, 64, lambda o, _: (piece(o).wait_send(), 0)[1], 0)
    for i in range(3):
        core(i).wait_send()
    for dist in (1, 2, 3):
        for buf, axis, n in lines:
            line(buf, axis, n, dist).wait_send()
        for src, buf, axis, n in planes:
            plane(src, buf, axis, n, dist).wait_send()
        for stage in range(4):
            for part in range(4):
                exchange(stage, part, dist).wait_send()


def local(matrix, signs, indices, counts):
    f32, i32 = jnp.float32, jnp.int32
    vmem, smem, dma = pltpu.VMEM, pltpu.SMEM, pltpu.SemaphoreType.DMA
    in_vmem = pl.BlockSpec(memory_space=vmem)
    sketch, gram = pl.pallas_call(
        kernel,
        name="sketch_gram",
        out_shape=(jax.ShapeDtypeStruct((256, 256), f32), jax.ShapeDtypeStruct((128, 128), f32)),
        in_specs=[pl.BlockSpec(memory_space=pl.ANY), in_vmem, in_vmem, pl.BlockSpec(memory_space=smem)],
        out_specs=(in_vmem, in_vmem),
        scratch_shapes=[
            vmem((4096, 256), f32), vmem((4096, 256), f32), vmem((32, 128), i32), vmem((128, 128), f32),
            vmem((4, 2048, 128), f32), vmem((4, 2048, 128), f32), vmem((4, 2048, 128), f32),
            *[vmem((4096, 128), f32)] * 4, vmem((4, 2048, 128), f32), vmem((4, 2048, 128), f32),
            vmem((4, 512, 128), f32), vmem((4, 512, 128), f32),
            vmem((8, 128), i32), vmem((32, 128), i32), vmem((32, 128), i32),
            vmem((128, 128), i32), vmem((128, 128), i32), vmem((128, 128), i32),
            smem((128, 128), i32), smem((128, 128), i32), smem((128, 128), i32),
            vmem((512, 128), f32), vmem((512, 128), f32), vmem((16, 128), f32), vmem((128, 128), f32),
            dma((2,)), dma((4,)), dma((4,)), dma((48,)), dma((48,)), dma((15,)), dma((15,)), dma((3,)),
            dma((64,)), dma((64,)), dma((16,)), dma((16,)),
        ],
        compiler_params=pltpu.CompilerParams(
            collective_id=0, has_side_effects=True, vmem_limit_bytes=56 * 2**20
        ),
    )(matrix, signs.reshape(32, 128), indices.reshape(2, 128), counts)
    return sketch, gram[None]


def solution(mesh):
    in_specs = (P(("rx", "ry"), None), P(("rx", "ry")), P(("rx", "ry")), P(("rx", "ry")))
    out_specs = (P(("rx", "ry"), None), P("ry", None, None))
    return jax.shard_map(local, mesh=mesh, in_specs=in_specs, out_specs=out_specs, check_vma=False)
```

```python
import functools

import jax
import jax.numpy as jnp
from jax import lax
from jax.experimental import pallas as pl
from jax.experimental.pallas import tpu as pltpu
from jax.sharding import PartitionSpec as P

MESH = pl.DeviceIdType.MESH
BLK = 128
HALF = 64
PARTS = (("y", "x", "z"), ("x", "z", "y"), ("y", "z", "x"), ("z", "x", "y"))


def coords():
    rx = lax.axis_index("rx")
    return {"y": rx // 8, "z": (rx // 2) % 4, "c": rx % 2, "x": lax.axis_index("ry")}


def device(at):
    return ((at["y"] * 4 + at["z"]) * 2 + at["c"], at["x"])


def moved(at, **to):
    return device({**at, **to})


def sign4(a, b):
    odd = (a % 2) * (b % 2) + (a // 2) * (b // 2)
    return (1 - 2 * (odd % 2)).astype(jnp.float32)


def hadamard(n):
    both = lax.broadcasted_iota(jnp.int32, (n, n), 0) & lax.broadcasted_iota(jnp.int32, (n, n), 1)
    both = both ^ (both >> 4)
    both = both ^ (both >> 2)
    both = both ^ (both >> 1)
    return (1 - 2 * (both & 1)).astype(jnp.float32)


def kernel(
    x_hbm, sg, idx, cnt, sk_out, gr_out,
    xm, xo, so, had, ry, ro, sy, syo, cy, dy, r, a, b, c, d1, d3, e, f, g, h,
    tile, ly, lz, pzy, pxy, pxz, szy, sxy, sxz, gp, rb, co, ob,
    loc_sem, core_s, core_r, y_s, y_r, st_s, st_r, ix_s, ix_r, sm_sem, rs_s, rs_r, ag_s, ag_r,
):
    me = coords()
    done = {1: d1, 3: d3}
    lane = lax.broadcasted_iota(jnp.int32, (1, 128), 1) < HALF
    other = moved(me, c=1 - me["c"])

    def rows(start, size):
        return pl.ds(pl.multiple_of(start, 8), size)

    def remote(src, dst, send, recv, to):
        return pltpu.make_async_remote_copy(
            src_ref=src, dst_ref=dst, send_sem=send, recv_sem=recv, device_id=to, device_id_type=MESH
        )

    load = pltpu.make_async_copy(x_hbm.at[:, pl.ds(128, 128)], xm, loc_sem.at[0])
    keep = pltpu.make_async_copy(
        x_hbm.at[rows(me["y"] * 1024, 1024), pl.ds(0, 128)], ry.at[me["y"]], loc_sem.at[1]
    )
    load.start()
    keep.start()

    barrier = pltpu.get_barrier_semaphore()

    def greet(o, _):
        to = moved(me, y=(me["y"] + o // 16) % 4, z=(me["z"] + (o // 4) % 4) % 4, x=(me["x"] + o % 4) % 4)
        pl.semaphore_signal(barrier, inc=1, device_id=to, device_id_type=MESH)
        return 0

    pl.semaphore_signal(barrier, inc=1, device_id=other, device_id_type=MESH)
    lax.fori_loop(1, 64, greet, 0)

    had[...] = hadamard(BLK)
    slots = idx[...]
    tile[...] = jnp.zeros_like(tile)
    tile[pl.ds(0, 1), :] = slots[0:1, :]
    tile[pl.ds(1, 1), :] = slots[1:2, :] ^ 2048
    tile[pl.ds(2, 1), :] = slots[1:2, :]
    pl.semaphore_wait(barrier, 64)

    def core(i):
        if i == 8:
            return remote(sg, so, core_s.at[i], core_r.at[i], other)
        place = pl.ds(i % 2 * 2048 + i // 2 * 512, 512)
        return remote(x_hbm.at[place, pl.ds(128, 128)], xo.at[place, :], core_s.at[i], core_r.at[i], other)

    def out_y(k, dist):
        at = (me["y"] + dist) % 4
        i = k * 3 + dist - 1
        if k == 4:
            src, dst = sg.at[rows(at * 8, 8), :], sy.at[rows(me["y"] * 8, 8), :]
        else:
            src = x_hbm.at[rows(at * 1024 + k * 256, 256), pl.ds(0, 128)]
            dst = ry.at[me["y"], pl.ds(k * 256, 256), :]
        return remote(src, dst, y_s.at[i], y_r.at[i], moved(me, y=at))

    def back_y(k, dist):
        at = (me["y"] + dist) % 4
        i = 15 + k * 3 + dist - 1
        return remote(
            cy.at[at, pl.ds(k * 256, 256), :], dy.at[rows(me["y"] * 1024 + k * 256, 256), :],
            y_s.at[i], y_r.at[i], moved(me, y=at),
        )

    def core_y(k):
        i = 9 + k
        if k == 4:
            return remote(sy, syo, core_s.at[i], core_r.at[i], other)
        place = pl.ds(k * 256, 256)
        return remote(ry.at[:, place, :], ro.at[:, place, :], core_s.at[i], core_r.at[i], other)

    core(8).start()
    for i in range(2):
        core(i).start()
    for dist in (1, 2, 3):
        out_y(4, dist).start()
        out_y(0, dist).start()
    for i in range(2, 8):
        core(i).start()
    for k in range(1, 4):
        for dist in (1, 2, 3):
            out_y(k, dist).start()

    def line(buf, axis, n, dist):
        at = (me[axis] + dist) % 4
        i = n * 3 + dist - 1
        return remote(tile, buf.at[rows(me[axis] * 8, 8), :], ix_s.at[i], ix_r.at[i], moved(me, **{axis: at}))

    def plane(src, buf, axis, n, dist):
        at = (me[axis] + dist) % 4
        i = 6 + n * 3 + dist - 1
        return remote(src, buf.at[rows(me[axis] * 32, 32), :], ix_s.at[i], ix_r.at[i], moved(me, **{axis: at}))

    lines = ((ly, "y", 0), (lz, "z", 1))
    planes = ((ly, pzy, "z", 0), (ly, pxy, "x", 1), (lz, pxz, "x", 2))
    for buf, axis, n in lines:
        for dist in (1, 2, 3):
            line(buf, axis, n, dist).start()
        buf[rows(me[axis] * 8, 8), :] = tile[...]

    def exchange(stage, part, dist):
        axis = PARTS[part][max(stage - 1, 0)]
        at = (me[axis] + dist) % 4
        size = 128 if stage == 3 else 512
        i = (stage * 4 + part) * 3 + dist - 1
        src = (a, c, e, g)[stage].at[part // 2 if stage < 2 else part, rows(at * size, size), :]
        mine = rows(me[axis] * size, size)
        if stage == 1:
            dst = done[part].at[mine, :]
        else:
            dst = (b, None, f, h)[stage].at[part // 2 if stage < 2 else part, mine, :]
        return remote(src, dst, st_s.at[i], st_r.at[i], moved(me, **{axis: at}))

    def send(stage, part):
        for dist in (1, 2, 3):
            exchange(stage, part, dist).start()

    def arrive(stage, part):
        for dist in (1, 2, 3):
            exchange(stage, part, dist).wait_recv()

    sign = (1 - 2 * me["c"]).astype(jnp.float32)

    def mixed(s0, s1, x0, x1):
        hm = had[...]
        left = jnp.concatenate(
            [hm * (s0.astype(jnp.float32) * sign), hm * s1.astype(jnp.float32)], axis=1
        ).astype(jnp.bfloat16)
        both = jnp.concatenate([x0, x1], axis=0)
        hi = both.astype(jnp.bfloat16)
        lo = (both - hi.astype(jnp.float32)).astype(jnp.bfloat16)
        out = jnp.dot(left, jnp.concatenate([hi, lo], axis=1), preferred_element_type=jnp.float32)
        return out[:, :128] + out[:, 128:]

    def panel1(j):
        def block(at):
            place = rows(at * BLK, BLK)
            return mixed(sg[pl.ds(at, 1), :], so[pl.ds(at, 1), :], xm[place, :], xo[place, :])

        def pair(i, _):
            lo, hi = block(i), block(i + 16)
            place = rows(i * BLK, BLK)
            a[0, place, :] = jnp.where(lane, lo, pltpu.roll(hi, HALF, 1))
            a[1, place, :] = jnp.where(lane, pltpu.roll(lo, HALF, 1), hi)
            return 0

        lax.fori_loop(4 * j, 4 * j + 4, pair, 0)

    def four(v):
        s, t, u, w = v[0] + v[1], v[0] - v[1], v[2] + v[3], v[2] - v[3]
        return s + u, t + w, s - u, t - w

    def panel0(k):
        def step(n, _):
            at = k * 2 + n
            place = rows(at * BLK, BLK)
            v = [
                mixed(sy[pl.ds(q * 8 + at, 1), :], syo[pl.ds(q * 8 + at, 1), :], ry[q, place, :], ro[q, place, :])
                for q in range(4)
            ]
            for q, out in enumerate(four(v)):
                cy[q, place, :] = out
            return 0

        lax.fori_loop(0, 2, step, 0)
        for dist in (1, 2, 3):
            back_y(k, dist).start()
        dy[rows(me["y"] * 1024 + k * 256, 256), :] = cy[me["y"], pl.ds(k * 256, 256), :]

    def across(k):
        for dist in (1, 2, 3):
            out_y(k, dist).wait_recv()
        core_y(k).start()

    def own(axis, size):
        return rows(me[axis] * size, size)

    def whole(part):
        n, axis = part // 2, PARTS[part][0]
        b[n, own(axis, 512), :] = a[n, own(axis, 512), :]
        arrive(0, part)

        def step(i, _):
            for q, out in enumerate(four([b[n, rows(q * 512 + i * 32, 32), :] for q in range(4)])):
                c[n, rows(q * 512 + i * 32, 32), :] = out
            return 0

        lax.fori_loop(0, 16, step, 0)
        send(1, part)
        done[part][own(axis, 512), :] = c[n, own(axis, 512), :]

    def gather(part, m, dst):
        table, src = {1: szy, 3: sxy}[part], done[part]

        def some(i, _):
            row, k0 = (m * 4 + i // 2) * 8, (i % 2) * 64
            for u in range(64):
                lo = src[pl.ds(table[row, k0 + u], 1), :]
                hi = src[pl.ds(table[row + 1, k0 + u], 1), :]
                dst[part, pl.ds(m * 512 + i * 64 + u, 1), :] = jnp.where(lane, lo, hi)
            return 0

        lax.fori_loop(0, 8, some, 0)

    def pruned(part):
        axis = PARTS[part][1]
        arrive(1, part)

        def turn(i, _):
            done[part][rows(2048 + i * 64, 64), :] = pltpu.roll(done[part][rows(i * 64, 64), :], HALF, 1)
            return 0

        lax.fori_loop(0, 32, turn, 0)
        for dist in (1, 2, 3):
            gather(part, (me[axis] + dist) % 4, e)
            exchange(2, part, dist).start()
        gather(part, me[axis], f)

    def cells(xs, zs):
        def cell(n, _):
            x = (me["x"] + (xs[0] + n if len(xs) > 1 else xs[0])) % 4
            z = (me["z"] + (zs[0] + n if len(zs) > 1 else zs[0])) % 4
            row = (x * 4 + z) * 8

            def some(i, _):
                for u in range(32):
                    r[pl.ds(i * 32 + u, 1), :] = dy[pl.ds(sxz[row, i * 32 + u], 1), :]
                    r[pl.ds(128 + i * 32 + u, 1), :] = dy[pl.ds(sxz[row + 2, i * 32 + u], 1), :]
                return 0

            lax.fori_loop(0, 4, some, 0)
            lo, hi = r[pl.ds(0, 128), :], r[pl.ds(128, 128), :]
            e[0, rows(x * 512 + z * 128, 128), :] = jnp.where(lane, lo, pltpu.roll(hi, HALF, 1))
            e[2, rows(z * 512 + x * 128, 128), :] = jnp.where(lane, pltpu.roll(lo, HALF, 1), hi)
            return 0

        lax.fori_loop(0, max(len(xs), len(zs)), cell, 0)

    def pruned_y():
        for k in range(4):
            for dist in (1, 2, 3):
                back_y(k, dist).wait_recv()
        for dist in (1, 2, 3):
            cells((dist,), range(dist, 5))
            exchange(2, 0, dist).start()
            cells(range(dist + 1, 5), (dist,))
            exchange(2, 2, dist).start()
        cells((4,), (4,))
        for part in (0, 2):
            f[part, own(PARTS[part][1], 512), :] = e[part, own(PARTS[part][1], 512), :]

    def add_up(part, src, size, axis):
        signs = [sign4(me[axis], jnp.int32(q)) for q in range(4)]

        def at(start, count):
            total = src[part, pl.ds(start, count), :]
            for q in range(1, 4):
                total = total + signs[q] * src[part, rows(q * size + start, count), :]
            return total

        return at

    def last(part):
        axis = PARTS[part][2]
        arrive(2, part)
        sums = add_up(part, f, 512, PARTS[part][1])

        def step(i, _):
            start = pl.multiple_of(i * 32, 32)
            g[part, pl.ds(start, 32), :] = sums(start, 32)
            return 0

        lax.fori_loop(0, 16, step, 0)
        send(3, part)
        h[part, own(axis, 128), :] = g[part, own(axis, 128), :]

    def final(part):
        arrive(3, part)
        return add_up(part, h, 128, PARTS[part][2])(0, 128)

    load.wait()
    core(8).wait_recv()
    for j in range(4):
        core(2 * j).wait_recv()
        core(2 * j + 1).wait_recv()
        panel1(j)
        for part in (1, 3):
            axis = PARTS[part][0]

            @pl.when(me[axis] != j)
            def _():
                exchange(0, part, (j - me[axis] + 4) % 4).start()

    keep.wait()
    for dist in (1, 2, 3):
        out_y(4, dist).wait_recv()
    sy[own("y", 8), :] = sg[own("y", 8), :]
    core_y(4).start()
    across(0)
    for buf, axis, n in lines:
        for dist in (1, 2, 3):
            line(buf, axis, n, dist).wait_recv()
    for src, buf, axis, n in planes:
        for dist in (1, 2, 3):
            plane(src, buf, axis, n, dist).start()
        buf[rows(me[axis] * 32, 32), :] = src[...]
    core_y(4).wait_recv()
    core_y(0).wait_recv()
    panel0(0)
    across(1)
    core_y(1).wait_recv()
    panel0(1)
    across(2)
    whole(1)
    core_y(2).wait_recv()
    panel0(2)
    whole(3)
    across(3)
    core_y(3).wait_recv()
    panel0(3)
    for i, (src, buf, axis, n) in enumerate(planes):
        for dist in (1, 2, 3):
            plane(src, buf, axis, n, dist).wait_recv()
        pltpu.make_async_copy(buf, (szy, sxy, sxz)[i], sm_sem.at[i]).start()
    for i, (src, buf, axis, n) in enumerate(planes):
        pltpu.make_async_copy(buf, (szy, sxy, sxz)[i], sm_sem.at[i]).wait()

    pruned(1)
    pruned(3)
    pruned_y()
    last(1)
    last(3)
    last(0)
    last(2)

    scale = 1.0 / (128 * BLK) ** 0.5
    slot = lax.broadcasted_iota(jnp.int32, (128, 1), 0)
    count = cnt[0]
    for panel in (1, 0):
        p1 = final(3 if panel else 2)
        p0 = final(1 if panel else 0)
        cols = pl.ds(panel * 128, 128)
        lo = jnp.where(lane, p0, pltpu.roll(p1, HALF, 1)) * scale
        hi = jnp.where(lane, pltpu.roll(p0, HALF, 1), p1) * scale
        sk_out[pl.ds(0, 128), cols] = jnp.where(slot < count, lo, 0.0)
        sk_out[pl.ds(128, 128), cols] = jnp.where(slot + 128 < count, hi, 0.0)

    sk = sk_out[...]
    hi = sk.astype(jnp.bfloat16)
    lo = (sk - hi.astype(jnp.float32)).astype(jnp.bfloat16)

    def dot_t(p, q):
        return lax.dot_general(p, q, (((0,), (0,)), ((), ())), preferred_element_type=jnp.float32)

    gram = dot_t(hi, hi) + dot_t(hi, lo) + dot_t(lo, hi)
    for i in range(4):
        gp[pl.ds(i * 128, 128), :] = gram[i // 2 * 128 : i // 2 * 128 + 128, i % 2 * 128 : i % 2 * 128 + 128]

    here = me["y"] * 4 + me["z"]

    def piece(o):
        to = {"y": (me["y"] + o // 16) % 4, "z": (me["z"] + (o // 4) % 4) % 4, "x": (me["x"] + o % 4) % 4}
        src = pl.multiple_of(to["x"] * 128 + (to["y"] * 4 + to["z"]) * 8, 8)
        dst = pl.multiple_of((here * 4 + me["x"]) * 8, 8)
        return remote(gp.at[pl.ds(src, 8), :], rb.at[pl.ds(dst, 8), :], rs_s.at[o], rs_r.at[o], moved(me, **to))

    lax.fori_loop(1, 64, lambda o, _: (piece(o).start(), 0)[1], 0)
    rb[pl.ds(pl.multiple_of((here * 4 + me["x"]) * 8, 8), 8), :] = gp[
        pl.ds(pl.multiple_of(me["x"] * 128 + here * 8, 8), 8), :
    ]
    lax.fori_loop(1, 64, lambda o, _: (piece(o).wait_recv(), 0)[1], 0)
    co[pl.ds(0, 8), :] = rb[...].reshape(64, 8, 128).sum(0)
    swap = remote(co.at[pl.ds(0, 8), :], co.at[pl.ds(8, 8), :], core_s.at[14], core_r.at[14], other)
    swap.start()
    swap.wait_recv()
    mine = pl.ds(pl.multiple_of(here * 8, 8), 8)
    ob[mine, :] = (co[pl.ds(0, 8), :] + co[pl.ds(8, 8), :]) * (1.0 / (128 * 256))

    def share(o):
        to = {"y": (me["y"] + o // 4) % 4, "z": (me["z"] + o % 4) % 4}
        return remote(ob.at[mine, :], ob.at[mine, :], ag_s.at[o], ag_r.at[o], moved(me, **to))

    lax.fori_loop(1, 16, lambda o, _: (share(o).start(), 0)[1], 0)
    lax.fori_loop(1, 16, lambda o, _: (share(o).wait_recv(), 0)[1], 0)
    gr_out[...] = ob[...]

    lax.fori_loop(1, 16, lambda o, _: (share(o).wait_send(), 0)[1], 0)
    swap.wait_send()
    lax.fori_loop(1, 64, lambda o, _: (piece(o).wait_send(), 0)[1], 0)
    for i in range(9):
        core(i).wait_send()
    for k in range(5):
        core_y(k).wait_send()
    for dist in (1, 2, 3):
        for buf, axis, n in lines:
            line(buf, axis, n, dist).wait_send()
        for src, buf, axis, n in planes:
            plane(src, buf, axis, n, dist).wait_send()
        for k in range(5):
            out_y(k, dist).wait_send()
        for k in range(4):
            back_y(k, dist).wait_send()
        for stage in range(4):
            for part in (1, 3) if stage < 2 else range(4):
                exchange(stage, part, dist).wait_send()


def local(matrix, signs, indices, counts):
    f32, i32 = jnp.float32, jnp.int32
    vmem, smem, dma = pltpu.VMEM, pltpu.SMEM, pltpu.SemaphoreType.DMA
    in_vmem = pl.BlockSpec(memory_space=vmem)
    sketch, gram = pl.pallas_call(
        kernel,
        name="sketch_gram",
        out_shape=(jax.ShapeDtypeStruct((256, 256), f32), jax.ShapeDtypeStruct((128, 128), f32)),
        in_specs=[pl.BlockSpec(memory_space=pl.ANY), in_vmem, in_vmem, pl.BlockSpec(memory_space=smem)],
        out_specs=(in_vmem, in_vmem),
        scratch_shapes=[
            vmem((4096, 128), f32), vmem((4096, 128), f32), vmem((32, 128), i32), vmem((128, 128), f32),
            vmem((4, 1024, 128), f32), vmem((4, 1024, 128), f32), vmem((32, 128), i32), vmem((32, 128), i32),
            vmem((4, 1024, 128), f32), vmem((4096, 128), f32), vmem((256, 128), f32),
            vmem((2, 2048, 128), f32), vmem((2, 2048, 128), f32), vmem((2, 2048, 128), f32),
            vmem((4096, 128), f32), vmem((4096, 128), f32),
            vmem((4, 2048, 128), f32), vmem((4, 2048, 128), f32),
            vmem((4, 512, 128), f32), vmem((4, 512, 128), f32),
            vmem((8, 128), i32), vmem((32, 128), i32), vmem((32, 128), i32),
            vmem((128, 128), i32), vmem((128, 128), i32), vmem((128, 128), i32),
            smem((128, 128), i32), smem((128, 128), i32), smem((128, 128), i32),
            vmem((512, 128), f32), vmem((512, 128), f32), vmem((16, 128), f32), vmem((128, 128), f32),
            dma((2,)), dma((15,)), dma((15,)), dma((27,)), dma((27,)), dma((48,)), dma((48,)),
            dma((15,)), dma((15,)), dma((3,)), dma((64,)), dma((64,)), dma((16,)), dma((16,)),
        ],
        compiler_params=pltpu.CompilerParams(
            collective_id=0, has_side_effects=True, vmem_limit_bytes=56 * 2**20
        ),
    )(matrix, signs.reshape(32, 128), indices.reshape(2, 128), counts)
    return sketch, gram[None]


def solution(mesh):
    in_specs = (P(("rx", "ry"), None), P(("rx", "ry")), P(("rx", "ry")), P(("rx", "ry")))
    out_specs = (P(("rx", "ry"), None), P("ry", None, None))
    return jax.shard_map(local, mesh=mesh, in_specs=in_specs, out_specs=out_specs, check_vma=False)
```

```python
import functools

import jax
import jax.numpy as jnp
from jax import lax
from jax.experimental import pallas as pl
from jax.experimental.pallas import tpu as pltpu
from jax.sharding import PartitionSpec as P

MESH = pl.DeviceIdType.MESH
BLK = 128
HALF = 64
PARTS = (("y", "x", "z"), ("x", "z", "y"), ("y", "z", "x"), ("z", "x", "y"))


def coords():
    rx = lax.axis_index("rx")
    return {"y": rx // 8, "z": (rx // 2) % 4, "c": rx % 2, "x": lax.axis_index("ry")}


def device(at):
    return ((at["y"] * 4 + at["z"]) * 2 + at["c"], at["x"])


def moved(at, **to):
    return device({**at, **to})


def sign4(a, b):
    odd = (a % 2) * (b % 2) + (a // 2) * (b // 2)
    return (1 - 2 * (odd % 2)).astype(jnp.float32)


def hadamard(n):
    both = lax.broadcasted_iota(jnp.int32, (n, n), 0) & lax.broadcasted_iota(jnp.int32, (n, n), 1)
    both = both ^ (both >> 4)
    both = both ^ (both >> 2)
    both = both ^ (both >> 1)
    return (1 - 2 * (both & 1)).astype(jnp.float32)


def kernel(
    x_hbm, sg, idx, cnt, sk_out, gr_out,
    xm, xo, so, had, ry, ro, sy, syo, cy, dy, r, a, b, c, d1, d3, e, f, g, h,
    tile, ly, lz, pzy, pxy, pxz, szy, sxy, sxz, gp, rb, co, ob,
    loc_sem, core_s, core_r, y_s, y_r, st_s, st_r, ix_s, ix_r, sm_sem, rs_s, rs_r, ag_s, ag_r,
):
    me = coords()
    done = {1: d1, 3: d3}
    lane = lax.broadcasted_iota(jnp.int32, (1, 128), 1) < HALF
    other = moved(me, c=1 - me["c"])

    def rows(start, size):
        return pl.ds(pl.multiple_of(start, 8), size)

    def remote(src, dst, send, recv, to):
        return pltpu.make_async_remote_copy(
            src_ref=src, dst_ref=dst, send_sem=send, recv_sem=recv, device_id=to, device_id_type=MESH
        )

    load = pltpu.make_async_copy(x_hbm.at[:, pl.ds(128, 128)], xm, loc_sem.at[0])
    keep = pltpu.make_async_copy(
        x_hbm.at[rows(me["y"] * 1024, 1024), pl.ds(0, 128)], ry.at[me["y"]], loc_sem.at[1]
    )
    load.start()
    keep.start()

    barrier = pltpu.get_barrier_semaphore()

    def greet(o, _):
        to = moved(me, y=(me["y"] + o // 16) % 4, z=(me["z"] + (o // 4) % 4) % 4, x=(me["x"] + o % 4) % 4)
        pl.semaphore_signal(barrier, inc=1, device_id=to, device_id_type=MESH)
        return 0

    pl.semaphore_signal(barrier, inc=1, device_id=other, device_id_type=MESH)
    lax.fori_loop(1, 64, greet, 0)

    had[...] = hadamard(BLK)
    slots = idx[...]
    tile[...] = jnp.zeros_like(tile)
    tile[pl.ds(0, 1), :] = slots[0:1, :]
    tile[pl.ds(1, 1), :] = slots[1:2, :] ^ 2048
    tile[pl.ds(2, 1), :] = slots[1:2, :]
    pl.semaphore_wait(barrier, 64)

    def core(i):
        if i == 8:
            return remote(sg, so, core_s.at[i], core_r.at[i], other)
        place = pl.ds(i % 2 * 2048 + i // 2 * 512, 512)
        return remote(x_hbm.at[place, pl.ds(128, 128)], xo.at[place, :], core_s.at[i], core_r.at[i], other)

    def out_y(k, dist):
        at = (me["y"] + dist) % 4
        i = k * 3 + dist - 1
        if k == 4:
            src, dst = sg.at[rows(at * 8, 8), :], sy.at[rows(me["y"] * 8, 8), :]
        else:
            src = x_hbm.at[rows(at * 1024 + k * 256, 256), pl.ds(0, 128)]
            dst = ry.at[me["y"], pl.ds(k * 256, 256), :]
        return remote(src, dst, y_s.at[i], y_r.at[i], moved(me, y=at))

    def back_y(k, dist):
        at = (me["y"] + dist) % 4
        i = 15 + k * 3 + dist - 1
        return remote(
            cy.at[at, pl.ds(k * 256, 256), :], dy.at[rows(me["y"] * 1024 + k * 256, 256), :],
            y_s.at[i], y_r.at[i], moved(me, y=at),
        )

    def core_y(k):
        i = 9 + k
        if k == 4:
            return remote(sy, syo, core_s.at[i], core_r.at[i], other)
        place = pl.ds(k * 256, 256)
        return remote(ry.at[:, place, :], ro.at[:, place, :], core_s.at[i], core_r.at[i], other)

    def line(buf, axis, n, dist):
        at = (me[axis] + dist) % 4
        i = n * 3 + dist - 1
        return remote(tile, buf.at[rows(me[axis] * 8, 8), :], ix_s.at[i], ix_r.at[i], moved(me, **{axis: at}))

    def plane(src, buf, axis, n, dist):
        at = (me[axis] + dist) % 4
        i = 6 + n * 3 + dist - 1
        return remote(src, buf.at[rows(me[axis] * 32, 32), :], ix_s.at[i], ix_r.at[i], moved(me, **{axis: at}))

    lines = ((ly, "y", 0), (lz, "z", 1))
    planes = ((ly, pzy, "z", 0), (ly, pxy, "x", 1), (lz, pxz, "x", 2))
    for buf, axis, n in lines:
        for dist in (1, 2, 3):
            line(buf, axis, n, dist).start()
        buf[rows(me[axis] * 8, 8), :] = tile[...]

    core(8).start()
    for i in range(2):
        core(i).start()
    for dist in (1, 2, 3):
        out_y(4, dist).start()
        out_y(0, dist).start()
    for i in range(2, 8):
        core(i).start()
    for k in range(1, 4):
        for dist in (1, 2, 3):
            out_y(k, dist).start()

    def exchange(stage, part, dist):
        axis = PARTS[part][max(stage - 1, 0)]
        at = (me[axis] + dist) % 4
        size = 128 if stage == 3 else 512
        i = (stage * 4 + part) * 3 + dist - 1
        src = (a, c, e, g)[stage].at[part // 2 if stage < 2 else part, rows(at * size, size), :]
        mine = rows(me[axis] * size, size)
        if stage == 1:
            dst = done[part].at[mine, :]
        else:
            dst = (b, None, f, h)[stage].at[part // 2 if stage < 2 else part, mine, :]
        return remote(src, dst, st_s.at[i], st_r.at[i], moved(me, **{axis: at}))

    def send(stage, part):
        for dist in (1, 2, 3):
            exchange(stage, part, dist).start()

    def arrive(stage, part):
        for dist in (1, 2, 3):
            exchange(stage, part, dist).wait_recv()

    sign = (1 - 2 * me["c"]).astype(jnp.float32)

    def mixed(s0, s1, x0, x1):
        hm = had[...]
        left = jnp.concatenate(
            [hm * (s0.astype(jnp.float32) * sign), hm * s1.astype(jnp.float32)], axis=1
        ).astype(jnp.bfloat16)
        both = jnp.concatenate([x0, x1], axis=0)
        hi = both.astype(jnp.bfloat16)
        lo = (both - hi.astype(jnp.float32)).astype(jnp.bfloat16)
        out = jnp.dot(left, jnp.concatenate([hi, lo], axis=1), preferred_element_type=jnp.float32)
        return out[:, :128] + out[:, 128:]

    def panel1(j):
        def block(at):
            place = rows(at * BLK, BLK)
            return mixed(sg[pl.ds(at, 1), :], so[pl.ds(at, 1), :], xm[place, :], xo[place, :])

        def pair(i, _):
            lo, hi = block(i), block(i + 16)
            place = rows(i * BLK, BLK)
            a[0, place, :] = jnp.where(lane, lo, pltpu.roll(hi, HALF, 1))
            a[1, place, :] = jnp.where(lane, pltpu.roll(lo, HALF, 1), hi)
            return 0

        lax.fori_loop(4 * j, 4 * j + 4, pair, 0)

    def four(v):
        s, t, u, w = v[0] + v[1], v[0] - v[1], v[2] + v[3], v[2] - v[3]
        return s + u, t + w, s - u, t - w

    def panel0(k):
        def step(n, _):
            at = k * 2 + n
            place = rows(at * BLK, BLK)
            v = [
                mixed(sy[pl.ds(q * 8 + at, 1), :], syo[pl.ds(q * 8 + at, 1), :], ry[q, place, :], ro[q, place, :])
                for q in range(4)
            ]
            for q, out in enumerate(four(v)):
                cy[q, place, :] = out
            return 0

        lax.fori_loop(0, 2, step, 0)
        for dist in (1, 2, 3):
            back_y(k, dist).start()
        dy[rows(me["y"] * 1024 + k * 256, 256), :] = cy[me["y"], pl.ds(k * 256, 256), :]

    def across(k):
        for dist in (1, 2, 3):
            out_y(k, dist).wait_recv()
        core_y(k).start()

    def own(axis, size):
        return rows(me[axis] * size, size)

    def whole(part):
        n, axis = part // 2, PARTS[part][0]
        b[n, own(axis, 512), :] = a[n, own(axis, 512), :]
        arrive(0, part)

        def step(i, _):
            for q, out in enumerate(four([b[n, rows(q * 512 + i * 32, 32), :] for q in range(4)])):
                c[n, rows(q * 512 + i * 32, 32), :] = out
            return 0

        lax.fori_loop(0, 16, step, 0)
        send(1, part)
        done[part][own(axis, 512), :] = c[n, own(axis, 512), :]

    def gather(part, m, dst):
        table, src = {1: szy, 3: sxy}[part], done[part]

        def some(i, _):
            row, k0 = (m * 4 + i // 2) * 8, (i % 2) * 64
            for u in range(64):
                lo = src[pl.ds(table[row, k0 + u], 1), :]
                hi = src[pl.ds(table[row + 1, k0 + u], 1), :]
                dst[part, pl.ds(m * 512 + i * 64 + u, 1), :] = jnp.where(lane, lo, hi)
            return 0

        lax.fori_loop(0, 8, some, 0)

    def pruned(part):
        axis = PARTS[part][1]
        arrive(1, part)

        def turn(i, _):
            done[part][rows(2048 + i * 64, 64), :] = pltpu.roll(done[part][rows(i * 64, 64), :], HALF, 1)
            return 0

        lax.fori_loop(0, 32, turn, 0)
        for dist in (1, 2, 3):
            gather(part, (me[axis] + dist) % 4, e)
            exchange(2, part, dist).start()
        gather(part, me[axis], f)

    def cells(xs, zs):
        def cell(n, _):
            x = (me["x"] + (xs[0] + n if len(xs) > 1 else xs[0])) % 4
            z = (me["z"] + (zs[0] + n if len(zs) > 1 else zs[0])) % 4
            row = (x * 4 + z) * 8

            def some(i, _):
                for u in range(32):
                    r[pl.ds(i * 32 + u, 1), :] = dy[pl.ds(sxz[row, i * 32 + u], 1), :]
                    r[pl.ds(128 + i * 32 + u, 1), :] = dy[pl.ds(sxz[row + 2, i * 32 + u], 1), :]
                return 0

            lax.fori_loop(0, 4, some, 0)
            lo, hi = r[pl.ds(0, 128), :], r[pl.ds(128, 128), :]
            e[0, rows(x * 512 + z * 128, 128), :] = jnp.where(lane, lo, pltpu.roll(hi, HALF, 1))
            e[2, rows(z * 512 + x * 128, 128), :] = jnp.where(lane, pltpu.roll(lo, HALF, 1), hi)
            return 0

        lax.fori_loop(0, max(len(xs), len(zs)), cell, 0)

    def pruned_y():
        for k in range(4):
            for dist in (1, 2, 3):
                back_y(k, dist).wait_recv()
        for dist in (1, 2, 3):
            cells((dist,), range(dist, 5))
            exchange(2, 0, dist).start()
            cells(range(dist + 1, 5), (dist,))
            exchange(2, 2, dist).start()
        cells((4,), (4,))
        for part in (0, 2):
            f[part, own(PARTS[part][1], 512), :] = e[part, own(PARTS[part][1], 512), :]

    def add_up(part, src, size, axis):
        signs = [sign4(me[axis], jnp.int32(q)) for q in range(4)]

        def at(start, count):
            total = src[part, pl.ds(start, count), :]
            for q in range(1, 4):
                total = total + signs[q] * src[part, rows(q * size + start, count), :]
            return total

        return at

    def last(part):
        axis = PARTS[part][2]
        arrive(2, part)
        sums = add_up(part, f, 512, PARTS[part][1])

        def step(i, _):
            start = pl.multiple_of(i * 32, 32)
            g[part, pl.ds(start, 32), :] = sums(start, 32)
            return 0

        lax.fori_loop(0, 16, step, 0)
        send(3, part)
        h[part, own(axis, 128), :] = g[part, own(axis, 128), :]

    def final(part):
        arrive(3, part)
        return add_up(part, h, 128, PARTS[part][2])(0, 128)

    load.wait()
    core(8).wait_recv()
    for j in range(4):
        core(2 * j).wait_recv()
        core(2 * j + 1).wait_recv()
        panel1(j)
        for part in (1, 3):
            axis = PARTS[part][0]

            @pl.when(me[axis] != j)
            def _():
                exchange(0, part, (j - me[axis] + 4) % 4).start()

    keep.wait()
    for dist in (1, 2, 3):
        out_y(4, dist).wait_recv()
    sy[own("y", 8), :] = sg[own("y", 8), :]
    core_y(4).start()
    across(0)
    for buf, axis, n in lines:
        for dist in (1, 2, 3):
            line(buf, axis, n, dist).wait_recv()
    for src, buf, axis, n in planes:
        for dist in (1, 2, 3):
            plane(src, buf, axis, n, dist).start()
        buf[rows(me[axis] * 32, 32), :] = src[...]
    core_y(4).wait_recv()
    core_y(0).wait_recv()
    panel0(0)
    across(1)
    core_y(1).wait_recv()
    panel0(1)
    across(2)
    whole(1)
    core_y(2).wait_recv()
    panel0(2)
    whole(3)
    across(3)
    core_y(3).wait_recv()
    panel0(3)
    for i, (src, buf, axis, n) in enumerate(planes):
        for dist in (1, 2, 3):
            plane(src, buf, axis, n, dist).wait_recv()
        pltpu.make_async_copy(buf, (szy, sxy, sxz)[i], sm_sem.at[i]).start()
    for i, (src, buf, axis, n) in enumerate(planes):
        pltpu.make_async_copy(buf, (szy, sxy, sxz)[i], sm_sem.at[i]).wait()

    pruned(1)
    pruned(3)
    pruned_y()
    last(1)
    last(3)
    last(0)
    last(2)

    scale = 1.0 / (128 * BLK) ** 0.5
    slot = lax.broadcasted_iota(jnp.int32, (128, 1), 0)
    count = cnt[0]
    for panel in (1, 0):
        p1 = final(3 if panel else 2)
        p0 = final(1 if panel else 0)
        cols = pl.ds(panel * 128, 128)
        lo = jnp.where(lane, p0, pltpu.roll(p1, HALF, 1)) * scale
        hi = jnp.where(lane, pltpu.roll(p0, HALF, 1), p1) * scale
        sk_out[pl.ds(0, 128), cols] = jnp.where(slot < count, lo, 0.0)
        sk_out[pl.ds(128, 128), cols] = jnp.where(slot + 128 < count, hi, 0.0)

    sk = sk_out[...]
    hi = sk.astype(jnp.bfloat16)
    lo = (sk - hi.astype(jnp.float32)).astype(jnp.bfloat16)

    def dot_t(p, q):
        return lax.dot_general(p, q, (((0,), (0,)), ((), ())), preferred_element_type=jnp.float32)

    gram = dot_t(hi, hi) + dot_t(hi, lo) + dot_t(lo, hi)
    for i in range(4):
        gp[pl.ds(i * 128, 128), :] = gram[i // 2 * 128 : i // 2 * 128 + 128, i % 2 * 128 : i % 2 * 128 + 128]

    here = me["y"] * 4 + me["z"]

    def piece(o):
        to = {"y": (me["y"] + o // 16) % 4, "z": (me["z"] + (o // 4) % 4) % 4, "x": (me["x"] + o % 4) % 4}
        src = pl.multiple_of(to["x"] * 128 + (to["y"] * 4 + to["z"]) * 8, 8)
        dst = pl.multiple_of((here * 4 + me["x"]) * 8, 8)
        return remote(gp.at[pl.ds(src, 8), :], rb.at[pl.ds(dst, 8), :], rs_s.at[o], rs_r.at[o], moved(me, **to))

    lax.fori_loop(1, 64, lambda o, _: (piece(o).start(), 0)[1], 0)
    rb[pl.ds(pl.multiple_of((here * 4 + me["x"]) * 8, 8), 8), :] = gp[
        pl.ds(pl.multiple_of(me["x"] * 128 + here * 8, 8), 8), :
    ]
    lax.fori_loop(1, 64, lambda o, _: (piece(o).wait_recv(), 0)[1], 0)
    co[pl.ds(0, 8), :] = rb[...].reshape(64, 8, 128).sum(0)
    swap = remote(co.at[pl.ds(0, 8), :], co.at[pl.ds(8, 8), :], core_s.at[14], core_r.at[14], other)
    swap.start()
    swap.wait_recv()
    mine = pl.ds(pl.multiple_of(here * 8, 8), 8)
    ob[mine, :] = (co[pl.ds(0, 8), :] + co[pl.ds(8, 8), :]) * (1.0 / (128 * 256))

    def share(o):
        to = {"y": (me["y"] + o // 4) % 4, "z": (me["z"] + o % 4) % 4}
        return remote(ob.at[mine, :], ob.at[mine, :], ag_s.at[o], ag_r.at[o], moved(me, **to))

    lax.fori_loop(1, 16, lambda o, _: (share(o).start(), 0)[1], 0)
    lax.fori_loop(1, 16, lambda o, _: (share(o).wait_recv(), 0)[1], 0)
    gr_out[...] = ob[...]

    lax.fori_loop(1, 16, lambda o, _: (share(o).wait_send(), 0)[1], 0)
    swap.wait_send()
    lax.fori_loop(1, 64, lambda o, _: (piece(o).wait_send(), 0)[1], 0)
    for i in range(9):
        core(i).wait_send()
    for k in range(5):
        core_y(k).wait_send()
    for dist in (1, 2, 3):
        for buf, axis, n in lines:
            line(buf, axis, n, dist).wait_send()
        for src, buf, axis, n in planes:
            plane(src, buf, axis, n, dist).wait_send()
        for k in range(5):
            out_y(k, dist).wait_send()
        for k in range(4):
            back_y(k, dist).wait_send()
        for stage in range(4):
            for part in (1, 3) if stage < 2 else range(4):
                exchange(stage, part, dist).wait_send()


def local(matrix, signs, indices, counts):
    f32, i32 = jnp.float32, jnp.int32
    vmem, smem, dma = pltpu.VMEM, pltpu.SMEM, pltpu.SemaphoreType.DMA
    in_vmem = pl.BlockSpec(memory_space=vmem)
    sketch, gram = pl.pallas_call(
        kernel,
        name="sketch_gram",
        out_shape=(jax.ShapeDtypeStruct((256, 256), f32), jax.ShapeDtypeStruct((128, 128), f32)),
        in_specs=[pl.BlockSpec(memory_space=pl.ANY), in_vmem, in_vmem, pl.BlockSpec(memory_space=smem)],
        out_specs=(in_vmem, in_vmem),
        scratch_shapes=[
            vmem((4096, 128), f32), vmem((4096, 128), f32), vmem((32, 128), i32), vmem((128, 128), f32),
            vmem((4, 1024, 128), f32), vmem((4, 1024, 128), f32), vmem((32, 128), i32), vmem((32, 128), i32),
            vmem((4, 1024, 128), f32), vmem((4096, 128), f32), vmem((256, 128), f32),
            vmem((2, 2048, 128), f32), vmem((2, 2048, 128), f32), vmem((2, 2048, 128), f32),
            vmem((4096, 128), f32), vmem((4096, 128), f32),
            vmem((4, 2048, 128), f32), vmem((4, 2048, 128), f32),
            vmem((4, 512, 128), f32), vmem((4, 512, 128), f32),
            vmem((8, 128), i32), vmem((32, 128), i32), vmem((32, 128), i32),
            vmem((128, 128), i32), vmem((128, 128), i32), vmem((128, 128), i32),
            smem((128, 128), i32), smem((128, 128), i32), smem((128, 128), i32),
            vmem((512, 128), f32), vmem((512, 128), f32), vmem((16, 128), f32), vmem((128, 128), f32),
            dma((2,)), dma((15,)), dma((15,)), dma((27,)), dma((27,)), dma((48,)), dma((48,)),
            dma((15,)), dma((15,)), dma((3,)), dma((64,)), dma((64,)), dma((16,)), dma((16,)),
        ],
        compiler_params=pltpu.CompilerParams(
            collective_id=0, has_side_effects=True, vmem_limit_bytes=56 * 2**20
        ),
    )(matrix, signs.reshape(32, 128), indices.reshape(2, 128), counts)
    return sketch, gram[None]


def solution(mesh):
    in_specs = (P(("rx", "ry"), None), P(("rx", "ry")), P(("rx", "ry")), P(("rx", "ry")))
    out_specs = (P(("rx", "ry"), None), P("ry", None, None))
    return jax.shard_map(local, mesh=mesh, in_specs=in_specs, out_specs=out_specs, check_vma=False)
```

```python
import functools

import jax
import jax.numpy as jnp
from jax import lax
from jax.experimental import pallas as pl
from jax.experimental.pallas import tpu as pltpu
from jax.sharding import PartitionSpec as P

MESH = pl.DeviceIdType.MESH
BLK = 128
HALF = 64
PARTS = (("y", "x", "z"), ("x", "z", "y"), ("y", "z", "x"), ("z", "x", "y"))


def coords():
    rx = lax.axis_index("rx")
    return {"y": rx // 8, "z": (rx // 2) % 4, "c": rx % 2, "x": lax.axis_index("ry")}


def device(at):
    return ((at["y"] * 4 + at["z"]) * 2 + at["c"], at["x"])


def moved(at, **to):
    return device({**at, **to})


def sign4(a, b):
    odd = (a % 2) * (b % 2) + (a // 2) * (b // 2)
    return (1 - 2 * (odd % 2)).astype(jnp.float32)


def hadamard(n):
    both = lax.broadcasted_iota(jnp.int32, (n, n), 0) & lax.broadcasted_iota(jnp.int32, (n, n), 1)
    both = both ^ (both >> 4)
    both = both ^ (both >> 2)
    both = both ^ (both >> 1)
    return (1 - 2 * (both & 1)).astype(jnp.float32)


def kernel(
    x_hbm, sg, idx, cnt, sk_out, gr_out,
    xm, xo, so, had, ry, ro, sy, syo, cy, dy, r, a, b, c, d1, d3, e, f, g, h,
    tile, ly, lz, pzy, pxy, pxz, szy, sxy, sxz, gp, rb, co, ob,
    loc_sem, core_s, core_r, y_s, y_r, st_s, st_r, ix_s, ix_r, sm_sem, rs_s, rs_r, ag_s, ag_r,
):
    me = coords()
    done = {1: d1, 3: d3}
    lane = lax.broadcasted_iota(jnp.int32, (1, 128), 1) < HALF
    other = moved(me, c=1 - me["c"])

    def rows(start, size):
        return pl.ds(pl.multiple_of(start, 1024 if size % 1024 == 0 else 8), size)

    def remote(src, dst, send, recv, to):
        return pltpu.make_async_remote_copy(
            src_ref=src, dst_ref=dst, send_sem=send, recv_sem=recv, device_id=to, device_id_type=MESH
        )

    load = pltpu.make_async_copy(x_hbm.at[:, pl.ds(128, 128)], xm, loc_sem.at[0])
    keep = pltpu.make_async_copy(
        x_hbm.at[rows(me["y"] * 1024, 1024), pl.ds(0, 128)], ry.at[me["y"]], loc_sem.at[1]
    )
    load.start()
    keep.start()

    barrier = pltpu.get_barrier_semaphore()

    def greet(o, _):
        to = moved(me, y=(me["y"] + o // 16) % 4, z=(me["z"] + (o // 4) % 4) % 4, x=(me["x"] + o % 4) % 4)
        pl.semaphore_signal(barrier, inc=1, device_id=to, device_id_type=MESH)
        return 0

    pl.semaphore_signal(barrier, inc=1, device_id=other, device_id_type=MESH)
    lax.fori_loop(1, 64, greet, 0)

    had[...] = hadamard(BLK)
    tile[...] = jnp.zeros_like(tile)
    tile[pl.ds(0, 128)] = idx[pl.ds(0, 128)]
    tile[pl.ds(128, 128)] = idx[pl.ds(128, 128)] ^ 2048
    tile[pl.ds(256, 128)] = idx[pl.ds(128, 128)]
    pl.semaphore_wait(barrier, 64)

    def core(i):
        if i == 8:
            return remote(sg, so, core_s.at[i], core_r.at[i], other)
        place = pl.ds(i % 2 * 2048 + i // 2 * 512, 512)
        return remote(x_hbm.at[place, pl.ds(128, 128)], xo.at[place, :], core_s.at[i], core_r.at[i], other)

    def out_y(k, dist):
        at = (me["y"] + dist) % 4
        i = k * 3 + dist - 1
        if k == 4:
            src, dst = sg.at[rows(at * 8, 8), :], sy.at[rows(me["y"] * 8, 8), :]
        else:
            src = x_hbm.at[rows(at * 1024 + k * 256, 256), pl.ds(0, 128)]
            dst = ry.at[me["y"], pl.ds(k * 256, 256), :]
        return remote(src, dst, y_s.at[i], y_r.at[i], moved(me, y=at))

    def back_y(k, dist):
        at = (me["y"] + dist) % 4
        i = 15 + k * 3 + dist - 1
        return remote(
            cy.at[at, pl.ds(k * 256, 256), :], dy.at[rows(me["y"] * 1024 + k * 256, 256), :],
            y_s.at[i], y_r.at[i], moved(me, y=at),
        )

    def core_y(k):
        i = 9 + k
        if k == 4:
            return remote(sy, syo, core_s.at[i], core_r.at[i], other)
        place = pl.ds(k * 256, 256)
        return remote(ry.at[:, place, :], ro.at[:, place, :], core_s.at[i], core_r.at[i], other)

    def line(buf, axis, n, dist):
        at = (me[axis] + dist) % 4
        i = n * 3 + dist - 1
        return remote(tile, buf.at[rows(me[axis] * 1024, 1024)], ix_s.at[i], ix_r.at[i], moved(me, **{axis: at}))

    def plane(src, buf, axis, n, dist):
        at = (me[axis] + dist) % 4
        i = 6 + n * 3 + dist - 1
        return remote(src, buf.at[rows(me[axis] * 4096, 4096)], ix_s.at[i], ix_r.at[i], moved(me, **{axis: at}))

    lines = ((ly, "y", 0), (lz, "z", 1))
    planes = ((ly, pzy, "z", 0), (ly, pxy, "x", 1), (lz, pxz, "x", 2))
    for buf, axis, n in lines:
        for dist in (1, 2, 3):
            line(buf, axis, n, dist).start()
        buf[rows(me[axis] * 1024, 1024)] = tile[...]

    core(8).start()
    for i in range(2):
        core(i).start()
    for dist in (1, 2, 3):
        out_y(4, dist).start()
        out_y(0, dist).start()
    for i in range(2, 8):
        core(i).start()
    for k in range(1, 4):
        for dist in (1, 2, 3):
            out_y(k, dist).start()

    def exchange(stage, part, dist):
        axis = PARTS[part][max(stage - 1, 0)]
        at = (me[axis] + dist) % 4
        size = 128 if stage == 3 else 512
        i = (stage * 4 + part) * 3 + dist - 1
        src = (a, c, e, g)[stage].at[part // 2 if stage < 2 else part, rows(at * size, size), :]
        mine = rows(me[axis] * size, size)
        if stage == 1:
            dst = done[part].at[mine, :]
        else:
            dst = (b, None, f, h)[stage].at[part // 2 if stage < 2 else part, mine, :]
        return remote(src, dst, st_s.at[i], st_r.at[i], moved(me, **{axis: at}))

    def send(stage, part):
        for dist in (1, 2, 3):
            exchange(stage, part, dist).start()

    def arrive(stage, part):
        for dist in (1, 2, 3):
            exchange(stage, part, dist).wait_recv()

    sign = (1 - 2 * me["c"]).astype(jnp.float32)

    def mixed(s0, s1, x0, x1):
        hm = had[...]
        left = jnp.concatenate(
            [hm * (s0.astype(jnp.float32) * sign), hm * s1.astype(jnp.float32)], axis=1
        ).astype(jnp.bfloat16)
        both = jnp.concatenate([x0, x1], axis=0)
        hi = both.astype(jnp.bfloat16)
        lo = (both - hi.astype(jnp.float32)).astype(jnp.bfloat16)
        out = jnp.dot(left, jnp.concatenate([hi, lo], axis=1), preferred_element_type=jnp.float32)
        return out[:, :128] + out[:, 128:]

    def panel1(j):
        def block(at):
            place = rows(at * BLK, BLK)
            return mixed(sg[pl.ds(at, 1), :], so[pl.ds(at, 1), :], xm[place, :], xo[place, :])

        def pair(i, _):
            lo, hi = block(i), block(i + 16)
            place = rows(i * BLK, BLK)
            a[0, place, :] = jnp.where(lane, lo, pltpu.roll(hi, HALF, 1))
            a[1, place, :] = jnp.where(lane, pltpu.roll(lo, HALF, 1), hi)
            return 0

        lax.fori_loop(4 * j, 4 * j + 4, pair, 0)

    def four(v):
        s, t, u, w = v[0] + v[1], v[0] - v[1], v[2] + v[3], v[2] - v[3]
        return s + u, t + w, s - u, t - w

    def panel0(k):
        def step(n, _):
            at = k * 2 + n
            place = rows(at * BLK, BLK)
            v = [
                mixed(sy[pl.ds(q * 8 + at, 1), :], syo[pl.ds(q * 8 + at, 1), :], ry[q, place, :], ro[q, place, :])
                for q in range(4)
            ]
            for q, out in enumerate(four(v)):
                cy[q, place, :] = out
            return 0

        lax.fori_loop(0, 2, step, 0)
        for dist in (1, 2, 3):
            back_y(k, dist).start()
        dy[rows(me["y"] * 1024 + k * 256, 256), :] = cy[me["y"], pl.ds(k * 256, 256), :]

    def across(k):
        for dist in (1, 2, 3):
            out_y(k, dist).wait_recv()
        core_y(k).start()

    def own(axis, size):
        return rows(me[axis] * size, size)

    def whole(part):
        n, axis = part // 2, PARTS[part][0]
        b[n, own(axis, 512), :] = a[n, own(axis, 512), :]
        arrive(0, part)

        def step(i, _):
            for q, out in enumerate(four([b[n, rows(q * 512 + i * 32, 32), :] for q in range(4)])):
                c[n, rows(q * 512 + i * 32, 32), :] = out
            return 0

        lax.fori_loop(0, 16, step, 0)
        send(1, part)
        done[part][own(axis, 512), :] = c[n, own(axis, 512), :]

    def gather(part, m, dst):
        table, src = {1: szy, 3: sxy}[part], done[part]

        def some(i, _):
            base = (m * 4 + i // 2) * 1024 + (i % 2) * 64
            for u in range(64):
                lo = src[pl.ds(table[base + u], 1), :]
                hi = src[pl.ds(table[base + 128 + u], 1), :]
                dst[part, pl.ds(m * 512 + i * 64 + u, 1), :] = jnp.where(lane, lo, hi)
            return 0

        lax.fori_loop(0, 8, some, 0)

    def pruned(part):
        axis = PARTS[part][1]
        arrive(1, part)

        def turn(i, _):
            done[part][rows(2048 + i * 64, 64), :] = pltpu.roll(done[part][rows(i * 64, 64), :], HALF, 1)
            return 0

        lax.fori_loop(0, 32, turn, 0)
        for dist in (1, 2, 3):
            gather(part, (me[axis] + dist) % 4, e)
            exchange(2, part, dist).start()
        gather(part, me[axis], f)

    def cells(xs, zs):
        def cell(n, _):
            x = (me["x"] + (xs[0] + n if len(xs) > 1 else xs[0])) % 4
            z = (me["z"] + (zs[0] + n if len(zs) > 1 else zs[0])) % 4
            base = (x * 4 + z) * 1024
            table = sxz

            def some(i, _):
                for u in range(32):
                    r[pl.ds(i * 32 + u, 1), :] = dy[pl.ds(table[base + i * 32 + u], 1), :]
                    r[pl.ds(128 + i * 32 + u, 1), :] = dy[pl.ds(table[base + 256 + i * 32 + u], 1), :]
                return 0

            lax.fori_loop(0, 4, some, 0)
            lo, hi = r[pl.ds(0, 128), :], r[pl.ds(128, 128), :]
            e[0, rows(x * 512 + z * 128, 128), :] = jnp.where(lane, lo, pltpu.roll(hi, HALF, 1))
            e[2, rows(z * 512 + x * 128, 128), :] = jnp.where(lane, pltpu.roll(lo, HALF, 1), hi)
            return 0

        lax.fori_loop(0, max(len(xs), len(zs)), cell, 0)

    def pruned_y():
        for k in range(4):
            for dist in (1, 2, 3):
                back_y(k, dist).wait_recv()
        for dist in (1, 2, 3):
            cells((dist,), range(dist, 5))
            exchange(2, 0, dist).start()
            cells(range(dist + 1, 5), (dist,))
            exchange(2, 2, dist).start()
        cells((4,), (4,))
        for part in (0, 2):
            f[part, own(PARTS[part][1], 512), :] = e[part, own(PARTS[part][1], 512), :]

    def add_up(part, src, size, axis):
        signs = [sign4(me[axis], jnp.int32(q)) for q in range(4)]

        def at(start, count):
            total = src[part, pl.ds(start, count), :]
            for q in range(1, 4):
                total = total + signs[q] * src[part, rows(q * size + start, count), :]
            return total

        return at

    def last(part):
        axis = PARTS[part][2]
        arrive(2, part)
        sums = add_up(part, f, 512, PARTS[part][1])

        def step(i, _):
            start = pl.multiple_of(i * 32, 32)
            g[part, pl.ds(start, 32), :] = sums(start, 32)
            return 0

        lax.fori_loop(0, 16, step, 0)
        send(3, part)
        h[part, own(axis, 128), :] = g[part, own(axis, 128), :]

    def final(part):
        arrive(3, part)
        return add_up(part, h, 128, PARTS[part][2])(0, 128)

    load.wait()
    core(8).wait_recv()
    for j in range(4):
        core(2 * j).wait_recv()
        core(2 * j + 1).wait_recv()
        panel1(j)
        for part in (1, 3):
            axis = PARTS[part][0]

            @pl.when(me[axis] != j)
            def _():
                exchange(0, part, (j - me[axis] + 4) % 4).start()

    keep.wait()
    for dist in (1, 2, 3):
        out_y(4, dist).wait_recv()
    sy[own("y", 8), :] = sg[own("y", 8), :]
    core_y(4).start()
    across(0)
    for buf, axis, n in lines:
        for dist in (1, 2, 3):
            line(buf, axis, n, dist).wait_recv()
    for src, buf, axis, n in planes:
        for dist in (1, 2, 3):
            plane(src, buf, axis, n, dist).start()
        buf[rows(me[axis] * 4096, 4096)] = src[...]
    core_y(4).wait_recv()
    core_y(0).wait_recv()
    panel0(0)
    across(1)
    core_y(1).wait_recv()
    panel0(1)
    whole(1)
    whole(3)
    across(2)
    core_y(2).wait_recv()
    panel0(2)

    def to_smem(i):
        return pltpu.make_async_copy(planes[i][1], (szy, sxy, sxz)[i], sm_sem.at[i])

    for i, (src, buf, axis, n) in enumerate(planes):
        for dist in (1, 2, 3):
            plane(src, buf, axis, n, dist).wait_recv()
        to_smem(i).start()
    across(3)
    core_y(3).wait_recv()
    panel0(3)
    for i in range(3):
        to_smem(i).wait()
    pruned(1)
    pruned(3)
    pruned_y()
    scale = 1.0 / (128 * BLK) ** 0.5
    slot = lax.broadcasted_iota(jnp.int32, (128, 1), 0)
    count = cnt[0]

    def finish(panel, lower, upper):
        p0, p1 = final(lower), final(upper)
        cols = pl.ds(panel * 128, 128)
        lo = jnp.where(lane, p0, pltpu.roll(p1, HALF, 1)) * scale
        hi = jnp.where(lane, pltpu.roll(p0, HALF, 1), p1) * scale
        sk_out[pl.ds(0, 128), cols] = jnp.where(slot < count, lo, 0.0)
        sk_out[pl.ds(128, 128), cols] = jnp.where(slot + 128 < count, hi, 0.0)
        sk = sk_out[:, cols]
        hi = sk.astype(jnp.bfloat16)
        return hi, (sk - hi.astype(jnp.float32)).astype(jnp.bfloat16)

    here = me["y"] * 4 + me["z"]

    def gram(n, p, q):
        def dot(u, v):
            return lax.dot_general(u, v, (((0,), (0,)), ((), ())), preferred_element_type=jnp.float32)

        gp[pl.ds(n * 128, 128), :] = dot(p[0], q[0]) + dot(p[0], q[1]) + dot(p[1], q[0])

    def piece(dx, o):
        to = {"y": (me["y"] + o // 4) % 4, "z": (me["z"] + o % 4) % 4, "x": (me["x"] + dx) % 4}
        src = to["x"] * 128 + (to["y"] * 4 + to["z"]) * 8
        dst = (here * 4 + me["x"]) * 8
        n = dx * 16 + o
        return remote(gp.at[rows(src, 8), :], rb.at[rows(dst, 8), :], rs_s.at[n], rs_r.at[n], moved(me, **to))

    def scatter(n):
        dx = (n - me["x"] + 4) % 4

        def step(o, _):
            piece(dx, o).start()
            return 0

        lax.fori_loop(1, 16, step, 0)

        @pl.when(dx != 0)
        def _():
            piece(dx, 0).start()

    def each_piece(act):
        def step(n, _):
            act(piece(n // 16, n % 16))
            return 0

        lax.fori_loop(1, 64, step, 0)

    last(1)
    last(3)
    sk1 = finish(1, 1, 3)
    gram(3, sk1, sk1)
    scatter(3)
    last(0)
    last(2)
    sk0 = finish(0, 0, 2)
    gram(0, sk0, sk0)
    scatter(0)
    gram(1, sk0, sk1)
    scatter(1)
    gram(2, sk1, sk0)
    scatter(2)
    rb[rows((here * 4 + me["x"]) * 8, 8), :] = gp[rows(me["x"] * 128 + here * 8, 8), :]
    each_piece(lambda p: p.wait_recv())
    co[pl.ds(0, 8), :] = rb[...].reshape(64, 8, 128).sum(0)
    swap = remote(co.at[pl.ds(0, 8), :], co.at[pl.ds(8, 8), :], core_s.at[14], core_r.at[14], other)
    swap.start()
    swap.wait_recv()
    mine = pl.ds(pl.multiple_of(here * 8, 8), 8)
    ob[mine, :] = (co[pl.ds(0, 8), :] + co[pl.ds(8, 8), :]) * (1.0 / (128 * 256))

    def share(o):
        to = {"y": (me["y"] + o // 4) % 4, "z": (me["z"] + o % 4) % 4}
        return remote(ob.at[mine, :], ob.at[mine, :], ag_s.at[o], ag_r.at[o], moved(me, **to))

    lax.fori_loop(1, 16, lambda o, _: (share(o).start(), 0)[1], 0)
    lax.fori_loop(1, 16, lambda o, _: (share(o).wait_recv(), 0)[1], 0)
    gr_out[...] = ob[...]

    lax.fori_loop(1, 16, lambda o, _: (share(o).wait_send(), 0)[1], 0)
    swap.wait_send()
    each_piece(lambda p: p.wait_send())
    for i in range(9):
        core(i).wait_send()
    for k in range(5):
        core_y(k).wait_send()
    for dist in (1, 2, 3):
        for buf, axis, n in lines:
            line(buf, axis, n, dist).wait_send()
        for src, buf, axis, n in planes:
            plane(src, buf, axis, n, dist).wait_send()
        for k in range(5):
            out_y(k, dist).wait_send()
        for k in range(4):
            back_y(k, dist).wait_send()
        for stage in range(4):
            for part in (1, 3) if stage < 2 else range(4):
                exchange(stage, part, dist).wait_send()


def hand_on(a, b, to_a, to_b, sem):
    both = pltpu.make_async_copy(a, to_a, sem.at[0]), pltpu.make_async_copy(b, to_b, sem.at[1])
    for copy in both:
        copy.start()
    for copy in both:
        copy.wait()


def local(matrix, signs, indices, counts):
    f32, i32 = jnp.float32, jnp.int32
    vmem, smem, dma = pltpu.VMEM, pltpu.SMEM, pltpu.SemaphoreType.DMA
    in_vmem = pl.BlockSpec(memory_space=vmem)
    sketch, gram = pl.pallas_call(
        kernel,
        name="sketch_gram",
        out_shape=(jax.ShapeDtypeStruct((256, 256), f32), jax.ShapeDtypeStruct((128, 128), f32)),
        in_specs=[pl.BlockSpec(memory_space=pl.ANY), in_vmem, in_vmem, pl.BlockSpec(memory_space=smem)],
        out_specs=(in_vmem, in_vmem),
        scratch_shapes=[
            vmem((4096, 128), f32), vmem((4096, 128), f32), vmem((32, 128), i32), vmem((128, 128), f32),
            vmem((4, 1024, 128), f32), vmem((4, 1024, 128), f32), vmem((32, 128), i32), vmem((32, 128), i32),
            vmem((4, 1024, 128), f32), vmem((4096, 128), f32), vmem((256, 128), f32),
            vmem((2, 2048, 128), f32), vmem((2, 2048, 128), f32), vmem((2, 2048, 128), f32),
            vmem((4096, 128), f32), vmem((4096, 128), f32),
            vmem((4, 2048, 128), f32), vmem((4, 2048, 128), f32),
            vmem((4, 512, 128), f32), vmem((4, 512, 128), f32),
            vmem((1024,), i32), vmem((4096,), i32), vmem((4096,), i32),
            vmem((16384,), i32), vmem((16384,), i32), vmem((16384,), i32),
            smem((16384,), i32), smem((16384,), i32), smem((16384,), i32),
            vmem((512, 128), f32), vmem((512, 128), f32), vmem((16, 128), f32), vmem((128, 128), f32),
            dma((2,)), dma((15,)), dma((15,)), dma((27,)), dma((27,)), dma((48,)), dma((48,)),
            dma((15,)), dma((15,)), dma((3,)), dma((64,)), dma((64,)), dma((16,)), dma((16,)),
        ],
        compiler_params=pltpu.CompilerParams(
            collective_id=0, has_side_effects=True, vmem_limit_bytes=56 * 2**20
        ),
    )(matrix, signs.reshape(32, 128), indices, counts)
    anywhere = pl.BlockSpec(memory_space=pl.ANY)
    sketch, gram = pl.pallas_call(
        hand_on,
        name="hand_on",
        out_shape=(jax.ShapeDtypeStruct((256, 256), f32), jax.ShapeDtypeStruct((128, 128), f32)),
        in_specs=[anywhere] * 2,
        out_specs=(anywhere,) * 2,
        scratch_shapes=[dma((2,))],
    )(sketch, gram)
    return sketch, gram[None]


def solution(mesh):
    in_specs = (P(("rx", "ry"), None), P(("rx", "ry")), P(("rx", "ry")), P(("rx", "ry")))
    out_specs = (P(("rx", "ry"), None), P("ry", None, None))
    return jax.shard_map(local, mesh=mesh, in_specs=in_specs, out_specs=out_specs, check_vma=False)
```

```python
import functools

import jax
import jax.numpy as jnp
from jax import lax
from jax.experimental import pallas as pl
from jax.experimental.pallas import tpu as pltpu
from jax.sharding import PartitionSpec as P

MESH = pl.DeviceIdType.MESH
BLK = 128
HALF = 64
PARTS = (("y", "x", "z"), ("x", "z", "y"), ("y", "z", "x"), ("z", "x", "y"))


def coords():
    rx = lax.axis_index("rx")
    return {"y": rx // 8, "z": (rx // 2) % 4, "c": rx % 2, "x": lax.axis_index("ry")}


def device(at):
    return ((at["y"] * 4 + at["z"]) * 2 + at["c"], at["x"])


def moved(at, **to):
    return device({**at, **to})


def sign4(a, b):
    odd = (a % 2) * (b % 2) + (a // 2) * (b // 2)
    return (1 - 2 * (odd % 2)).astype(jnp.float32)


def hadamard(n):
    both = lax.broadcasted_iota(jnp.int32, (n, n), 0) & lax.broadcasted_iota(jnp.int32, (n, n), 1)
    both = both ^ (both >> 4)
    both = both ^ (both >> 2)
    both = both ^ (both >> 1)
    return (1 - 2 * (both & 1)).astype(jnp.float32)


def kernel(
    x_hbm, sg, idx, cnt, sk_out, gr_out,
    xm, xo, so, had, ry, ro, sy, syo, cy, dy, r, a, b, c, d1, d3, e, f, g, h,
    tile, ly, lz, pzy, pxy, pxz, szy, sxy, sxz, gp, rb, co, ob,
    loc_sem, core_s, core_r, y_s, y_r, st_s, st_r, ix_s, ix_r, sm_sem, rs_s, rs_r, ag_s, ag_r,
):
    me = coords()
    done = {1: d1, 3: d3}
    lane = lax.broadcasted_iota(jnp.int32, (1, 128), 1) < HALF
    other = moved(me, c=1 - me["c"])

    def rows(start, size):
        return pl.ds(pl.multiple_of(start, 1024 if size % 1024 == 0 else 8), size)

    def remote(src, dst, send, recv, to):
        return pltpu.make_async_remote_copy(
            src_ref=src, dst_ref=dst, send_sem=send, recv_sem=recv, device_id=to, device_id_type=MESH
        )

    load = pltpu.make_async_copy(x_hbm.at[:, pl.ds(128, 128)], xm, loc_sem.at[0])
    keep = pltpu.make_async_copy(
        x_hbm.at[rows(me["y"] * 1024, 1024), pl.ds(0, 128)], ry.at[me["y"]], loc_sem.at[1]
    )
    load.start()
    keep.start()

    barrier = pltpu.get_barrier_semaphore()

    for axis in "yxz":
        for dist in (1, 2, 3):
            to = moved(me, **{axis: (me[axis] + dist) % 4})
            pl.semaphore_signal(barrier, inc=1, device_id=to, device_id_type=MESH)
    pl.semaphore_signal(barrier, inc=1, device_id=other, device_id_type=MESH)

    had[...] = hadamard(BLK)
    tile[...] = jnp.zeros_like(tile)
    tile[pl.ds(0, 128)] = idx[pl.ds(0, 128)]
    tile[pl.ds(128, 128)] = idx[pl.ds(128, 128)] ^ 2048
    tile[pl.ds(256, 128)] = idx[pl.ds(128, 128)]
    pl.semaphore_wait(barrier, 10)

    def core(i):
        if i == 8:
            return remote(sg, so, core_s.at[i], core_r.at[i], other)
        place = pl.ds(i % 2 * 2048 + i // 2 * 512, 512)
        return remote(x_hbm.at[place, pl.ds(128, 128)], xo.at[place, :], core_s.at[i], core_r.at[i], other)

    def out_y(k, dist):
        at = (me["y"] + dist) % 4
        i = k * 3 + dist - 1
        if k == 4:
            src, dst = sg.at[rows(at * 8, 8), :], sy.at[rows(me["y"] * 8, 8), :]
        else:
            src = x_hbm.at[rows(at * 1024 + k * 256, 256), pl.ds(0, 128)]
            dst = ry.at[me["y"], pl.ds(k * 256, 256), :]
        return remote(src, dst, y_s.at[i], y_r.at[i], moved(me, y=at))

    def back_y(k, dist):
        at = (me["y"] + dist) % 4
        i = 15 + k * 3 + dist - 1
        return remote(
            cy.at[at, pl.ds(k * 256, 256), :], dy.at[rows(me["y"] * 1024 + k * 256, 256), :],
            y_s.at[i], y_r.at[i], moved(me, y=at),
        )

    def core_y(k):
        i = 9 + k
        if k == 4:
            return remote(sy, syo, core_s.at[i], core_r.at[i], other)
        place = pl.ds(k * 256, 256)
        return remote(ry.at[:, place, :], ro.at[:, place, :], core_s.at[i], core_r.at[i], other)

    def line(buf, axis, n, dist):
        at = (me[axis] + dist) % 4
        i = n * 3 + dist - 1
        return remote(tile, buf.at[rows(me[axis] * 1024, 1024)], ix_s.at[i], ix_r.at[i], moved(me, **{axis: at}))

    def plane(src, buf, axis, n, dist):
        at = (me[axis] + dist) % 4
        i = 6 + n * 3 + dist - 1
        return remote(src, buf.at[rows(me[axis] * 4096, 4096)], ix_s.at[i], ix_r.at[i], moved(me, **{axis: at}))

    lines = ((ly, "y", 0), (lz, "z", 1))
    planes = ((ly, pzy, "z", 0), (ly, pxy, "x", 1), (lz, pxz, "x", 2))
    def core(i):
        if i == 8:
            return remote(sg, so, core_s.at[i], core_r.at[i], other)
        place = pl.ds(i % 2 * 2048 + i // 2 * 512, 512)
        return remote(x_hbm.at[place, pl.ds(128, 128)], xo.at[place, :], core_s.at[i], core_r.at[i], other)

    def out_y(k, dist):
        at = (me["y"] + dist) % 4
        i = k * 3 + dist - 1
        if k == 4:
            src, dst = sg.at[rows(at * 8, 8), :], sy.at[rows(me["y"] * 8, 8), :]
        else:
            src = x_hbm.at[rows(at * 1024 + k * 256, 256), pl.ds(0, 128)]
            dst = ry.at[me["y"], pl.ds(k * 256, 256), :]
        return remote(src, dst, y_s.at[i], y_r.at[i], moved(me, y=at))

    def back_y(k, dist):
        at = (me["y"] + dist) % 4
        i = 15 + k * 3 + dist - 1
        return remote(
            cy.at[at, pl.ds(k * 256, 256), :], dy.at[rows(me["y"] * 1024 + k * 256, 256), :],
            y_s.at[i], y_r.at[i], moved(me, y=at),
        )

    def core_y(k):
        i = 9 + k
        if k == 4:
            return remote(sy, syo, core_s.at[i], core_r.at[i], other)
        place = pl.ds(k * 256, 256)
        return remote(ry.at[:, place, :], ro.at[:, place, :], core_s.at[i], core_r.at[i], other)

    def line(buf, axis, n, dist):
        at = (me[axis] + dist) % 4
        i = n * 3 + dist - 1
        return remote(tile, buf.at[rows(me[axis] * 1024, 1024)], ix_s.at[i], ix_r.at[i], moved(me, **{axis: at}))

    def plane(src, buf, axis, n, dist):
        at = (me[axis] + dist) % 4
        i = 6 + n * 3 + dist - 1
        return remote(src, buf.at[rows(me[axis] * 4096, 4096)], ix_s.at[i], ix_r.at[i], moved(me, **{axis: at}))

    lines = ((ly, "y", 0), (lz, "z", 1))
    planes = ((ly, pzy, "z", 0), (ly, pxy, "x", 1), (lz, pxz, "x", 2))
    for buf, axis, n in lines:
        for dist in (1, 2, 3):
            line(buf, axis, n, dist).start()
        buf[rows(me[axis] * 1024, 1024)] = tile[...]

    for dist in (1, 2, 3):
        out_y(4, dist).start()
        out_y(0, dist).start()
    core(8).start()
    for i in range(2):
        core(i).start()

    for i in range(2, 8):
        core(i).start()
    for k in range(1, 4):
        for dist in (1, 2, 3):
            out_y(k, dist).start()

    def exchange(stage, part, dist):
        axis = PARTS[part][max(stage - 1, 0)]
        at = (me[axis] + dist) % 4
        size = 128 if stage == 3 else 512
        i = (stage * 4 + part) * 3 + dist - 1
        src = (a, c, e, g)[stage].at[part // 2 if stage < 2 else part, rows(at * size, size), :]
        mine = rows(me[axis] * size, size)
        if stage == 1:
            dst = done[part].at[mine, :]
        else:
            dst = (b, None, f, h)[stage].at[part // 2 if stage < 2 else part, mine, :]
        return remote(src, dst, st_s.at[i], st_r.at[i], moved(me, **{axis: at}))

    def send(stage, part):
        for dist in (1, 2, 3):
            exchange(stage, part, dist).start()

    def arrive(stage, part):
        for dist in (1, 2, 3):
            exchange(stage, part, dist).wait_recv()

    sign = (1 - 2 * me["c"]).astype(jnp.float32)

    def mixed(s0, s1, x0, x1):
        hm = had[...]
        left = jnp.concatenate(
            [hm * (s0.astype(jnp.float32) * sign), hm * s1.astype(jnp.float32)], axis=1
        ).astype(jnp.bfloat16)
        both = jnp.concatenate([x0, x1], axis=0)
        hi = both.astype(jnp.bfloat16)
        lo = (both - hi.astype(jnp.float32)).astype(jnp.bfloat16)
        out = jnp.dot(left, jnp.concatenate([hi, lo], axis=1), preferred_element_type=jnp.float32)
        return out[:, :128] + out[:, 128:]

    def panel1(j):
        def block(at):
            place = rows(at * BLK, BLK)
            return mixed(sg[pl.ds(at, 1), :], so[pl.ds(at, 1), :], xm[place, :], xo[place, :])

        def pair(i, _):
            lo, hi = block(i), block(i + 16)
            place = rows(i * BLK, BLK)
            a[0, place, :] = jnp.where(lane, lo, pltpu.roll(hi, HALF, 1))
            a[1, place, :] = jnp.where(lane, pltpu.roll(lo, HALF, 1), hi)
            return 0

        lax.fori_loop(4 * j, 4 * j + 4, pair, 0)

    def four(v):
        s, t, u, w = v[0] + v[1], v[0] - v[1], v[2] + v[3], v[2] - v[3]
        return s + u, t + w, s - u, t - w

    def panel0(k):
        def step(n, _):
            at = k * 2 + n
            place = rows(at * BLK, BLK)
            v = [
                mixed(sy[pl.ds(q * 8 + at, 1), :], syo[pl.ds(q * 8 + at, 1), :], ry[q, place, :], ro[q, place, :])
                for q in range(4)
            ]
            for q, out in enumerate(four(v)):
                cy[q, place, :] = out
            return 0

        lax.fori_loop(0, 2, step, 0)
        for dist in (1, 2, 3):
            back_y(k, dist).start()
        dy[rows(me["y"] * 1024 + k * 256, 256), :] = cy[me["y"], pl.ds(k * 256, 256), :]

    def across(k):
        for dist in (1, 2, 3):
            out_y(k, dist).wait_recv()
        core_y(k).start()

    def own(axis, size):
        return rows(me[axis] * size, size)

    def whole(part):
        n, axis = part // 2, PARTS[part][0]
        b[n, own(axis, 512), :] = a[n, own(axis, 512), :]
        arrive(0, part)

        def step(i, _):
            for q, out in enumerate(four([b[n, rows(q * 512 + i * 32, 32), :] for q in range(4)])):
                c[n, rows(q * 512 + i * 32, 32), :] = out
            return 0

        lax.fori_loop(0, 16, step, 0)
        send(1, part)
        done[part][own(axis, 512), :] = c[n, own(axis, 512), :]

    def gather(part, m, dst):
        table, src = {1: szy, 3: sxy}[part], done[part]

        def some(i, _):
            base = (m * 4 + i // 2) * 1024 + (i % 2) * 64
            for u in range(64):
                lo = src[pl.ds(table[base + u], 1), :]
                hi = src[pl.ds(table[base + 128 + u], 1), :]
                dst[part, pl.ds(m * 512 + i * 64 + u, 1), :] = jnp.where(lane, lo, hi)
            return 0

        lax.fori_loop(0, 8, some, 0)

    def turned(part):
        arrive(1, part)

        def turn(i, _):
            done[part][rows(2048 + i * 64, 64), :] = pltpu.roll(done[part][rows(i * 64, 64), :], HALF, 1)
            return 0

        lax.fori_loop(0, 32, turn, 0)

    def pruned(part, dist):
        axis = PARTS[part][1]
        gather(part, (me[axis] + dist) % 4, e if dist else f)
        if dist:
            exchange(2, part, dist).start()

    def cells(xs, zs):
        def cell(n, _):
            x = (me["x"] + (xs[0] + n if len(xs) > 1 else xs[0])) % 4
            z = (me["z"] + (zs[0] + n if len(zs) > 1 else zs[0])) % 4
            base = (x * 4 + z) * 1024
            table = sxz

            def some(i, _):
                for u in range(32):
                    r[pl.ds(i * 32 + u, 1), :] = dy[pl.ds(table[base + i * 32 + u], 1), :]
                    r[pl.ds(128 + i * 32 + u, 1), :] = dy[pl.ds(table[base + 256 + i * 32 + u], 1), :]
                return 0

            lax.fori_loop(0, 4, some, 0)
            lo, hi = r[pl.ds(0, 128), :], r[pl.ds(128, 128), :]
            e[0, rows(x * 512 + z * 128, 128), :] = jnp.where(lane, lo, pltpu.roll(hi, HALF, 1))
            e[2, rows(z * 512 + x * 128, 128), :] = jnp.where(lane, pltpu.roll(lo, HALF, 1), hi)
            return 0

        lax.fori_loop(0, max(len(xs), len(zs)), cell, 0)

    def pruned_y():
        for k in range(4):
            for dist in (1, 2, 3):
                back_y(k, dist).wait_recv()
        for dist in (1, 2, 3):
            cells((dist,), range(dist, 5))
            exchange(2, 0, dist).start()
            cells(range(dist + 1, 5), (dist,))
            exchange(2, 2, dist).start()
        cells((4,), (4,))
        for part in (0, 2):
            f[part, own(PARTS[part][1], 512), :] = e[part, own(PARTS[part][1], 512), :]

    def add_up(part, src, size, axis):
        signs = [sign4(me[axis], jnp.int32(q)) for q in range(4)]

        def at(start, count):
            total = src[part, pl.ds(start, count), :]
            for q in range(1, 4):
                total = total + signs[q] * src[part, rows(q * size + start, count), :]
            return total

        return at

    def last(part):
        axis = PARTS[part][2]
        arrive(2, part)
        sums = add_up(part, f, 512, PARTS[part][1])

        def step(i, _):
            start = pl.multiple_of(i * 32, 32)
            g[part, pl.ds(start, 32), :] = sums(start, 32)
            return 0

        lax.fori_loop(0, 16, step, 0)
        send(3, part)
        h[part, own(axis, 128), :] = g[part, own(axis, 128), :]

    def final(part):
        arrive(3, part)
        return add_up(part, h, 128, PARTS[part][2])(0, 128)

    load.wait()
    core(8).wait_recv()
    for j in range(4):
        core(2 * j).wait_recv()
        core(2 * j + 1).wait_recv()
        panel1(j)
        for part in (1, 3):
            axis = PARTS[part][0]

            @pl.when(me[axis] != j)
            def _():
                exchange(0, part, (j - me[axis] + 4) % 4).start()

    keep.wait()
    for dist in (1, 2, 3):
        out_y(4, dist).wait_recv()
    sy[own("y", 8), :] = sg[own("y", 8), :]
    core_y(4).start()
    across(0)
    for buf, axis, n in lines:
        for dist in (1, 2, 3):
            line(buf, axis, n, dist).wait_recv()
    for src, buf, axis, n in planes:
        for dist in (1, 2, 3):
            plane(src, buf, axis, n, dist).start()
        buf[rows(me[axis] * 4096, 4096)] = src[...]
    core_y(4).wait_recv()
    core_y(0).wait_recv()
    panel0(0)
    across(1)
    core_y(1).wait_recv()
    panel0(1)
    whole(1)
    whole(3)
    across(2)
    core_y(2).wait_recv()
    panel0(2)

    def to_smem(i):
        return pltpu.make_async_copy(planes[i][1], (szy, sxy, sxz)[i], sm_sem.at[i])

    for i, (src, buf, axis, n) in enumerate(planes):
        for dist in (1, 2, 3):
            plane(src, buf, axis, n, dist).wait_recv()
        to_smem(i).start()
    across(3)
    core_y(3).wait_recv()
    panel0(3)
    for i in range(3):
        to_smem(i).wait()
    turned(1)
    pruned(1, 1)
    turned(3)
    pruned(3, 1)
    pruned(1, 2)
    pruned(3, 2)
    pruned(1, 3)
    pruned(3, 3)
    pruned(1, 0)
    pruned(3, 0)
    pruned_y()
    scale = 1.0 / (128 * BLK) ** 0.5
    slot = lax.broadcasted_iota(jnp.int32, (128, 1), 0)
    count = cnt[0]

    def finish(panel, lower, upper):
        p0, p1 = final(lower), final(upper)
        cols = pl.ds(panel * 128, 128)
        lo = jnp.where(lane, p0, pltpu.roll(p1, HALF, 1)) * scale
        hi = jnp.where(lane, pltpu.roll(p0, HALF, 1), p1) * scale
        sk_out[pl.ds(0, 128), cols] = jnp.where(slot < count, lo, 0.0)
        sk_out[pl.ds(128, 128), cols] = jnp.where(slot + 128 < count, hi, 0.0)
        sk = sk_out[:, cols]
        hi = sk.astype(jnp.bfloat16)
        return hi, (sk - hi.astype(jnp.float32)).astype(jnp.bfloat16)

    here = me["y"] * 4 + me["z"]

    def gram(n, p, q):
        def dot(u, v):
            return lax.dot_general(u, v, (((0,), (0,)), ((), ())), preferred_element_type=jnp.float32)

        gp[pl.ds(n * 128, 128), :] = dot(p[0], q[0]) + dot(p[0], q[1]) + dot(p[1], q[0])

    def piece(dx, o):
        to = {"y": (me["y"] + o // 4) % 4, "z": (me["z"] + o % 4) % 4, "x": (me["x"] + dx) % 4}
        src = to["x"] * 128 + (to["y"] * 4 + to["z"]) * 8
        dst = (here * 4 + me["x"]) * 8
        n = dx * 16 + o
        return remote(gp.at[rows(src, 8), :], rb.at[rows(dst, 8), :], rs_s.at[n], rs_r.at[n], moved(me, **to))

    def scatter(n):
        dx = (n - me["x"] + 4) % 4

        def step(o, _):
            piece(dx, o).start()
            return 0

        lax.fori_loop(1, 16, step, 0)

        @pl.when(dx != 0)
        def _():
            piece(dx, 0).start()

    def each_piece(act):
        def step(n, _):
            act(piece(n // 16, n % 16))
            return 0

        lax.fori_loop(1, 64, step, 0)

    last(1)
    last(3)
    sk1 = finish(1, 1, 3)
    gram(3, sk1, sk1)
    scatter(3)
    last(0)
    last(2)
    sk0 = finish(0, 0, 2)
    gram(0, sk0, sk0)
    scatter(0)
    gram(1, sk0, sk1)
    scatter(1)
    gram(2, sk1, sk0)
    scatter(2)
    rb[rows((here * 4 + me["x"]) * 8, 8), :] = gp[rows(me["x"] * 128 + here * 8, 8), :]
    for i in range(9):
        core(i).wait_send()
    for k in range(5):
        core_y(k).wait_send()
    for dist in (1, 2, 3):
        for buf, axis, n in lines:
            line(buf, axis, n, dist).wait_send()
        for src, buf, axis, n in planes:
            plane(src, buf, axis, n, dist).wait_send()
        for k in range(5):
            out_y(k, dist).wait_send()
        for k in range(4):
            back_y(k, dist).wait_send()
        for stage in range(4):
            for part in (1, 3) if stage < 2 else range(4):
                exchange(stage, part, dist).wait_send()
    each_piece(lambda p: p.wait_recv())
    co[pl.ds(0, 8), :] = rb[...].reshape(64, 8, 128).sum(0)
    swap = remote(co.at[pl.ds(0, 8), :], co.at[pl.ds(8, 8), :], core_s.at[14], core_r.at[14], other)
    swap.start()
    swap.wait_recv()
    mine = pl.ds(pl.multiple_of(here * 8, 8), 8)
    ob[mine, :] = (co[pl.ds(0, 8), :] + co[pl.ds(8, 8), :]) * (1.0 / (128 * 256))

    def share(o):
        to = {"y": (me["y"] + o // 4) % 4, "z": (me["z"] + o % 4) % 4}
        return remote(ob.at[mine, :], ob.at[mine, :], ag_s.at[o], ag_r.at[o], moved(me, **to))

    lax.fori_loop(1, 16, lambda o, _: (share(o).start(), 0)[1], 0)
    swap.wait_send()
    each_piece(lambda p: p.wait_send())
    lax.fori_loop(1, 16, lambda o, _: (share(o).wait_send(), 0)[1], 0)
    lax.fori_loop(1, 16, lambda o, _: (share(o).wait_recv(), 0)[1], 0)
    gr_out[...] = ob[...]


def hand_on(a, b, to_a, to_b):
    to_a[...] = a[...]
    to_b[...] = b[...]


def local(matrix, signs, indices, counts):
    f32, i32 = jnp.float32, jnp.int32
    vmem, smem, dma = pltpu.VMEM, pltpu.SMEM, pltpu.SemaphoreType.DMA
    in_vmem = pl.BlockSpec(memory_space=vmem)
    sketch, gram = pl.pallas_call(
        kernel,
        name="sketch_gram",
        out_shape=(jax.ShapeDtypeStruct((256, 256), f32), jax.ShapeDtypeStruct((128, 128), f32)),
        in_specs=[pl.BlockSpec(memory_space=pl.ANY), in_vmem, in_vmem, pl.BlockSpec(memory_space=smem)],
        out_specs=(in_vmem, in_vmem),
        scratch_shapes=[
            vmem((4096, 128), f32), vmem((4096, 128), f32), vmem((32, 128), i32), vmem((128, 128), f32),
            vmem((4, 1024, 128), f32), vmem((4, 1024, 128), f32), vmem((32, 128), i32), vmem((32, 128), i32),
            vmem((4, 1024, 128), f32), vmem((4096, 128), f32), vmem((256, 128), f32),
            vmem((2, 2048, 128), f32), vmem((2, 2048, 128), f32), vmem((2, 2048, 128), f32),
            vmem((4096, 128), f32), vmem((4096, 128), f32),
            vmem((4, 2048, 128), f32), vmem((4, 2048, 128), f32),
            vmem((4, 512, 128), f32), vmem((4, 512, 128), f32),
            vmem((1024,), i32), vmem((4096,), i32), vmem((4096,), i32),
            vmem((16384,), i32), vmem((16384,), i32), vmem((16384,), i32),
            smem((16384,), i32), smem((16384,), i32), smem((16384,), i32),
            vmem((512, 128), f32), vmem((512, 128), f32), vmem((16, 128), f32), vmem((128, 128), f32),
            dma((2,)), dma((15,)), dma((15,)), dma((27,)), dma((27,)), dma((48,)), dma((48,)),
            dma((15,)), dma((15,)), dma((3,)), dma((64,)), dma((64,)), dma((16,)), dma((16,)),
        ],
        compiler_params=pltpu.CompilerParams(
            collective_id=0, has_side_effects=True, vmem_limit_bytes=56 * 2**20
        ),
    )(matrix, signs.reshape(32, 128), indices, counts)
    sketch, gram = pl.pallas_call(
        hand_on,
        name="hand_on",
        out_shape=(jax.ShapeDtypeStruct((256, 256), f32), jax.ShapeDtypeStruct((128, 128), f32)),
        in_specs=[in_vmem] * 2,
        out_specs=(in_vmem,) * 2,
    )(sketch, gram)
    return sketch, gram[None]


def solution(mesh):
    in_specs = (P(("rx", "ry"), None), P(("rx", "ry")), P(("rx", "ry")), P(("rx", "ry")))
    out_specs = (P(("rx", "ry"), None), P("ry", None, None))
    return jax.shard_map(local, mesh=mesh, in_specs=in_specs, out_specs=out_specs, check_vma=False)
```

```python
import functools

import jax
import jax.numpy as jnp
from jax import lax
from jax.experimental import pallas as pl
from jax.experimental.pallas import tpu as pltpu
from jax.sharding import PartitionSpec as P

MESH = pl.DeviceIdType.MESH
BLK = 128
HALF = 64
FAR = (2, 1, 3)
PARTS = (("y", "x", "z"), ("x", "z", "y"), ("y", "z", "x"), ("z", "x", "y"))


def coords():
    rx = lax.axis_index("rx")
    return {"y": rx // 8, "z": (rx // 2) % 4, "c": rx % 2, "x": lax.axis_index("ry")}


def device(at):
    return ((at["y"] * 4 + at["z"]) * 2 + at["c"], at["x"])


def moved(at, **to):
    return device({**at, **to})


def sign4(a, b):
    odd = (a % 2) * (b % 2) + (a // 2) * (b // 2)
    return (1 - 2 * (odd % 2)).astype(jnp.float32)


def hadamard(n):
    both = lax.broadcasted_iota(jnp.int32, (n, n), 0) & lax.broadcasted_iota(jnp.int32, (n, n), 1)
    both = both ^ (both >> 4)
    both = both ^ (both >> 2)
    both = both ^ (both >> 1)
    return (1 - 2 * (both & 1)).astype(jnp.float32)


def kernel(
    x_hbm, sg, idx, cnt, sk_out, gr_out,
    xm, xo, so, had, ry, ro, sy, syo, cy, dy, r, a, b, c, d1, d3, e, f, g, h,
    tile, ly, lz, pzy, pxy, pxz, szy, sxy, sxz, gp, rb, co, ob,
    loc_sem, core_s, core_r, y_s, y_r, st_s, st_r, ix_s, ix_r, sm_sem, rs_s, rs_r, ag_s, ag_r,
):
    me = coords()
    done = {1: d1, 3: d3}
    lane = lax.broadcasted_iota(jnp.int32, (1, 128), 1) < HALF
    other = moved(me, c=1 - me["c"])

    def rows(start, size):
        return pl.ds(pl.multiple_of(start, 1024 if size % 1024 == 0 else 8), size)

    def remote(src, dst, send, recv, to):
        return pltpu.make_async_remote_copy(
            src_ref=src, dst_ref=dst, send_sem=send, recv_sem=recv, device_id=to, device_id_type=MESH
        )

    load = pltpu.make_async_copy(x_hbm.at[:, pl.ds(128, 128)], xm, loc_sem.at[0])
    keep = pltpu.make_async_copy(
        x_hbm.at[rows(me["y"] * 1024, 1024), pl.ds(0, 128)], ry.at[me["y"]], loc_sem.at[1]
    )
    load.start()
    keep.start()

    barrier = pltpu.get_barrier_semaphore()

    for axis in "yxz":
        for dist in (1, 2, 3):
            to = moved(me, **{axis: (me[axis] + dist) % 4})
            pl.semaphore_signal(barrier, inc=1, device_id=to, device_id_type=MESH)
    pl.semaphore_signal(barrier, inc=1, device_id=other, device_id_type=MESH)

    had[...] = hadamard(BLK)
    tile[...] = jnp.zeros_like(tile)
    tile[pl.ds(0, 128)] = idx[pl.ds(0, 128)]
    tile[pl.ds(128, 128)] = idx[pl.ds(128, 128)] ^ 2048
    tile[pl.ds(256, 128)] = idx[pl.ds(128, 128)]
    pl.semaphore_wait(barrier, 10)

    def core(i):
        if i == 8:
            return remote(sg, so, core_s.at[i], core_r.at[i], other)
        place = pl.ds(i % 2 * 2048 + i // 2 * 512, 512)
        return remote(x_hbm.at[place, pl.ds(128, 128)], xo.at[place, :], core_s.at[i], core_r.at[i], other)

    def out_y(k, dist):
        at = (me["y"] + dist) % 4
        i = k * 3 + dist - 1
        if k == 4:
            src, dst = sg.at[rows(at * 8, 8), :], sy.at[rows(me["y"] * 8, 8), :]
        else:
            src = x_hbm.at[rows(at * 1024 + k * 256, 256), pl.ds(0, 128)]
            dst = ry.at[me["y"], pl.ds(k * 256, 256), :]
        return remote(src, dst, y_s.at[i], y_r.at[i], moved(me, y=at))

    def back_y(k, dist):
        at = (me["y"] + dist) % 4
        i = 15 + k * 3 + dist - 1
        return remote(
            cy.at[at, pl.ds(k * 256, 256), :], dy.at[rows(me["y"] * 1024 + k * 256, 256), :],
            y_s.at[i], y_r.at[i], moved(me, y=at),
        )

    def core_y(k):
        i = 9 + k
        if k == 4:
            return remote(sy, syo, core_s.at[i], core_r.at[i], other)
        place = pl.ds(k * 256, 256)
        return remote(ry.at[:, place, :], ro.at[:, place, :], core_s.at[i], core_r.at[i], other)

    def line(buf, axis, n, dist):
        at = (me[axis] + dist) % 4
        i = n * 3 + dist - 1
        return remote(tile, buf.at[rows(me[axis] * 1024, 1024)], ix_s.at[i], ix_r.at[i], moved(me, **{axis: at}))

    def plane(src, buf, axis, n, dist):
        at = (me[axis] + dist) % 4
        i = 6 + n * 3 + dist - 1
        return remote(src, buf.at[rows(me[axis] * 4096, 4096)], ix_s.at[i], ix_r.at[i], moved(me, **{axis: at}))

    lines = ((ly, "y", 0), (lz, "z", 1))
    planes = ((ly, pzy, "z", 0), (ly, pxy, "x", 1), (lz, pxz, "x", 2))
    def core(i):
        if i == 8:
            return remote(sg, so, core_s.at[i], core_r.at[i], other)
        place = pl.ds(i % 2 * 2048 + i // 2 * 512, 512)
        return remote(x_hbm.at[place, pl.ds(128, 128)], xo.at[place, :], core_s.at[i], core_r.at[i], other)

    def out_y(k, dist):
        at = (me["y"] + dist) % 4
        i = k * 3 + dist - 1
        if k == 4:
            src, dst = sg.at[rows(at * 8, 8), :], sy.at[rows(me["y"] * 8, 8), :]
        else:
            src = x_hbm.at[rows(at * 1024 + k * 256, 256), pl.ds(0, 128)]
            dst = ry.at[me["y"], pl.ds(k * 256, 256), :]
        return remote(src, dst, y_s.at[i], y_r.at[i], moved(me, y=at))

    def back_y(k, dist):
        at = (me["y"] + dist) % 4
        i = 15 + k * 3 + dist - 1
        return remote(
            cy.at[at, pl.ds(k * 256, 256), :], dy.at[rows(me["y"] * 1024 + k * 256, 256), :],
            y_s.at[i], y_r.at[i], moved(me, y=at),
        )

    def core_y(k):
        i = 9 + k
        if k == 4:
            return remote(sy, syo, core_s.at[i], core_r.at[i], other)
        place = pl.ds(k * 256, 256)
        return remote(ry.at[:, place, :], ro.at[:, place, :], core_s.at[i], core_r.at[i], other)

    def line(buf, axis, n, dist):
        at = (me[axis] + dist) % 4
        i = n * 3 + dist - 1
        return remote(tile, buf.at[rows(me[axis] * 1024, 1024)], ix_s.at[i], ix_r.at[i], moved(me, **{axis: at}))

    def plane(src, buf, axis, n, dist):
        at = (me[axis] + dist) % 4
        i = 6 + n * 3 + dist - 1
        return remote(src, buf.at[rows(me[axis] * 4096, 4096)], ix_s.at[i], ix_r.at[i], moved(me, **{axis: at}))

    lines = ((ly, "y", 0), (lz, "z", 1))
    planes = ((ly, pzy, "z", 0), (ly, pxy, "x", 1), (lz, pxz, "x", 2))
    for buf, axis, n in lines:
        for dist in (1, 2, 3):
            line(buf, axis, n, dist).start()
        buf[rows(me[axis] * 1024, 1024)] = tile[...]

    for dist in FAR:
        out_y(4, dist).start()
        out_y(0, dist).start()
    core(8).start()
    for i in range(2):
        core(i).start()

    for i in range(2, 8):
        core(i).start()
    for k in range(1, 4):
        for dist in FAR:
            out_y(k, dist).start()

    def exchange(stage, part, dist):
        axis = PARTS[part][max(stage - 1, 0)]
        at = (me[axis] + dist) % 4
        size = 128 if stage == 3 else 512
        i = (stage * 4 + part) * 3 + dist - 1
        src = (a, c, e, g)[stage].at[part // 2 if stage < 2 else part, rows(at * size, size), :]
        mine = rows(me[axis] * size, size)
        if stage == 1:
            dst = done[part].at[mine, :]
        else:
            dst = (b, None, f, h)[stage].at[part // 2 if stage < 2 else part, mine, :]
        return remote(src, dst, st_s.at[i], st_r.at[i], moved(me, **{axis: at}))

    def send(stage, part):
        for dist in FAR:
            exchange(stage, part, dist).start()

    def arrive(stage, part):
        for dist in (1, 2, 3):
            exchange(stage, part, dist).wait_recv()

    sign = (1 - 2 * me["c"]).astype(jnp.float32)

    def mixed(s0, s1, x0, x1):
        hm = had[...]
        left = jnp.concatenate(
            [hm * (s0.astype(jnp.float32) * sign), hm * s1.astype(jnp.float32)], axis=1
        ).astype(jnp.bfloat16)
        both = jnp.concatenate([x0, x1], axis=0)
        hi = both.astype(jnp.bfloat16)
        lo = (both - hi.astype(jnp.float32)).astype(jnp.bfloat16)
        out = jnp.dot(left, jnp.concatenate([hi, lo], axis=1), preferred_element_type=jnp.float32)
        return out[:, :128] + out[:, 128:]

    def panel1(j):
        def block(at):
            place = rows(at * BLK, BLK)
            return mixed(sg[pl.ds(at, 1), :], so[pl.ds(at, 1), :], xm[place, :], xo[place, :])

        def pair(i, _):
            lo, hi = block(i), block(i + 16)
            place = rows(i * BLK, BLK)
            a[0, place, :] = jnp.where(lane, lo, pltpu.roll(hi, HALF, 1))
            a[1, place, :] = jnp.where(lane, pltpu.roll(lo, HALF, 1), hi)
            return 0

        lax.fori_loop(0, 4, lambda i, _: pair(4 * j + i, _), 0)

    def four(v):
        s, t, u, w = v[0] + v[1], v[0] - v[1], v[2] + v[3], v[2] - v[3]
        return s + u, t + w, s - u, t - w

    def panel0(k):
        def step(n, _):
            at = k * 2 + n
            place = rows(at * BLK, BLK)
            v = [
                mixed(sy[pl.ds(q * 8 + at, 1), :], syo[pl.ds(q * 8 + at, 1), :], ry[q, place, :], ro[q, place, :])
                for q in range(4)
            ]
            for q, out in enumerate(four(v)):
                cy[q, place, :] = out
            return 0

        lax.fori_loop(0, 2, step, 0)
        for dist in FAR:
            back_y(k, dist).start()
        dy[rows(me["y"] * 1024 + k * 256, 256), :] = cy[me["y"], pl.ds(k * 256, 256), :]

    def across(k):
        for dist in (1, 2, 3):
            out_y(k, dist).wait_recv()
        core_y(k).start()

    def own(axis, size):
        return rows(me[axis] * size, size)

    def whole(part):
        n, axis = part // 2, PARTS[part][0]
        b[n, own(axis, 512), :] = a[n, own(axis, 512), :]
        arrive(0, part)

        def step(i, _):
            for q, out in enumerate(four([b[n, rows(q * 512 + i * 32, 32), :] for q in range(4)])):
                c[n, rows(q * 512 + i * 32, 32), :] = out
            return 0

        lax.fori_loop(0, 16, step, 0)
        send(1, part)
        done[part][own(axis, 512), :] = c[n, own(axis, 512), :]

    def gather(part, m, dst):
        table, src = {1: szy, 3: sxy}[part], done[part]

        def some(i, _):
            base = (m * 4 + i // 2) * 1024 + (i % 2) * 64
            for u in range(64):
                lo = src[pl.ds(table[base + u], 1), :]
                hi = src[pl.ds(table[base + 128 + u], 1), :]
                dst[part, pl.ds(m * 512 + i * 64 + u, 1), :] = jnp.where(lane, lo, hi)
            return 0

        lax.fori_loop(0, 8, some, 0)

    def turned(part):
        arrive(1, part)

        def turn(i, _):
            done[part][rows(2048 + i * 64, 64), :] = pltpu.roll(done[part][rows(i * 64, 64), :], HALF, 1)
            return 0

        lax.fori_loop(0, 32, turn, 0)

    def pruned(part, dist):
        axis = PARTS[part][1]
        gather(part, (me[axis] + dist) % 4, e if dist else f)
        if dist:
            exchange(2, part, dist).start()

    def far(n):
        return jnp.where(n == 0, 2, jnp.where(n == 1, 1, jnp.where(n == 2, 3, 0)))

    def cells(xs, zs):
        def cell(n, _):
            x = (me["x"] + far(xs[0] + n if len(xs) > 1 else xs[0])) % 4
            z = (me["z"] + far(zs[0] + n if len(zs) > 1 else zs[0])) % 4
            base = (x * 4 + z) * 1024
            table = sxz

            def some(i, _):
                for u in range(32):
                    r[pl.ds(i * 32 + u, 1), :] = dy[pl.ds(table[base + i * 32 + u], 1), :]
                    r[pl.ds(128 + i * 32 + u, 1), :] = dy[pl.ds(table[base + 256 + i * 32 + u], 1), :]
                return 0

            lax.fori_loop(0, 4, some, 0)
            lo, hi = r[pl.ds(0, 128), :], r[pl.ds(128, 128), :]
            e[0, rows(x * 512 + z * 128, 128), :] = jnp.where(lane, lo, pltpu.roll(hi, HALF, 1))
            e[2, rows(z * 512 + x * 128, 128), :] = jnp.where(lane, pltpu.roll(lo, HALF, 1), hi)
            return 0

        lax.fori_loop(0, max(len(xs), len(zs)), cell, 0)

    def pruned_y():
        for k in range(4):
            for dist in (1, 2, 3):
                back_y(k, dist).wait_recv()
        for n, dist in enumerate(FAR):
            cells((n,), range(n, 4))
            exchange(2, 0, dist).start()
            cells(range(n + 1, 4), (n,))
            exchange(2, 2, dist).start()
        cells((3,), (3,))
        for part in (0, 2):
            f[part, own(PARTS[part][1], 512), :] = e[part, own(PARTS[part][1], 512), :]

    def add_up(part, src, size, axis):
        signs = [sign4(me[axis], jnp.int32(q)) for q in range(4)]

        def at(start, count):
            total = src[part, pl.ds(start, count), :]
            for q in range(1, 4):
                total = total + signs[q] * src[part, rows(q * size + start, count), :]
            return total

        return at

    def last(part):
        axis = PARTS[part][2]
        arrive(2, part)
        sums = add_up(part, f, 512, PARTS[part][1])

        def step(i, _):
            start = pl.multiple_of(i * 32, 32)
            g[part, pl.ds(start, 32), :] = sums(start, 32)
            return 0

        lax.fori_loop(0, 16, step, 0)
        send(3, part)
        h[part, own(axis, 128), :] = g[part, own(axis, 128), :]

    def final(part):
        arrive(3, part)
        return add_up(part, h, 128, PARTS[part][2])(0, 128)

    load.wait()
    core(8).wait_recv()
    for i in range(8):
        core(i).wait_recv()
    for dist in FAR:
        panel1((me["x"] + dist) % 4)
        exchange(0, 1, dist).start()
    panel1(me["x"])
    send(0, 3)
    keep.wait()
    for dist in (1, 2, 3):
        out_y(4, dist).wait_recv()
    sy[own("y", 8), :] = sg[own("y", 8), :]
    core_y(4).start()
    across(0)
    for buf, axis, n in lines:
        for dist in (1, 2, 3):
            line(buf, axis, n, dist).wait_recv()
    for src, buf, axis, n in planes:
        for dist in (1, 2, 3):
            plane(src, buf, axis, n, dist).start()
        buf[rows(me[axis] * 4096, 4096)] = src[...]
    core_y(4).wait_recv()
    core_y(0).wait_recv()
    panel0(0)
    across(1)
    core_y(1).wait_recv()
    panel0(1)
    whole(1)
    whole(3)
    across(2)
    core_y(2).wait_recv()
    panel0(2)

    def to_smem(i):
        return pltpu.make_async_copy(planes[i][1], (szy, sxy, sxz)[i], sm_sem.at[i])

    for i, (src, buf, axis, n) in enumerate(planes):
        for dist in (1, 2, 3):
            plane(src, buf, axis, n, dist).wait_recv()
        to_smem(i).start()
    across(3)
    core_y(3).wait_recv()
    panel0(3)
    for i in range(3):
        to_smem(i).wait()
    turned(1)
    pruned(1, 2)
    turned(3)
    pruned(3, 2)
    pruned(1, 1)
    pruned(3, 1)
    pruned(1, 3)
    pruned(3, 3)
    pruned(1, 0)
    pruned(3, 0)
    pruned_y()
    scale = 1.0 / (128 * BLK) ** 0.5
    slot = lax.broadcasted_iota(jnp.int32, (128, 1), 0)
    count = cnt[0]

    def finish(panel, lower, upper):
        p0, p1 = final(lower), final(upper)
        cols = pl.ds(panel * 128, 128)
        lo = jnp.where(lane, p0, pltpu.roll(p1, HALF, 1)) * scale
        hi = jnp.where(lane, pltpu.roll(p0, HALF, 1), p1) * scale
        sk_out[pl.ds(0, 128), cols] = jnp.where(slot < count, lo, 0.0)
        sk_out[pl.ds(128, 128), cols] = jnp.where(slot + 128 < count, hi, 0.0)
        sk = sk_out[:, cols]
        hi = sk.astype(jnp.bfloat16)
        return hi, (sk - hi.astype(jnp.float32)).astype(jnp.bfloat16)

    here = me["y"] * 4 + me["z"]

    def gram(n, p, q):
        def dot(u, v):
            return lax.dot_general(u, v, (((0,), (0,)), ((), ())), preferred_element_type=jnp.float32)

        gp[pl.ds(n * 128, 128), :] = dot(p[0], q[0]) + dot(p[0], q[1]) + dot(p[1], q[0])

    def piece(dx, o):
        to = {"y": (me["y"] + o // 4) % 4, "z": (me["z"] + o % 4) % 4, "x": (me["x"] + dx) % 4}
        src = to["x"] * 128 + (to["y"] * 4 + to["z"]) * 8
        dst = (here * 4 + me["x"]) * 8
        n = dx * 16 + o
        return remote(gp.at[rows(src, 8), :], rb.at[rows(dst, 8), :], rs_s.at[n], rs_r.at[n], moved(me, **to))

    def scatter(n):
        dx = (n - me["x"] + 4) % 4

        def step(o, _):
            piece(dx, o).start()
            return 0

        lax.fori_loop(1, 16, step, 0)

        @pl.when(dx != 0)
        def _():
            piece(dx, 0).start()

    def each_piece(act):
        def step(n, _):
            act(piece(n // 16, n % 16))
            return 0

        lax.fori_loop(1, 64, step, 0)

    last(1)
    last(3)
    last(0)
    last(2)
    sk1 = finish(1, 1, 3)
    gram(3, sk1, sk1)
    scatter(3)
    sk0 = finish(0, 0, 2)
    gram(0, sk0, sk0)
    scatter(0)
    gram(1, sk0, sk1)
    scatter(1)
    gram(2, sk1, sk0)
    scatter(2)
    rb[rows((here * 4 + me["x"]) * 8, 8), :] = gp[rows(me["x"] * 128 + here * 8, 8), :]
    for i in range(9):
        core(i).wait_send()
    for k in range(5):
        core_y(k).wait_send()
    for dist in (1, 2, 3):
        for buf, axis, n in lines:
            line(buf, axis, n, dist).wait_send()
        for src, buf, axis, n in planes:
            plane(src, buf, axis, n, dist).wait_send()
        for k in range(5):
            out_y(k, dist).wait_send()
        for k in range(4):
            back_y(k, dist).wait_send()
        for stage in range(4):
            for part in (1, 3) if stage < 2 else range(4):
                exchange(stage, part, dist).wait_send()
    each_piece(lambda p: p.wait_recv())
    co[pl.ds(0, 8), :] = rb[...].reshape(64, 8, 128).sum(0)
    swap = remote(co.at[pl.ds(0, 8), :], co.at[pl.ds(8, 8), :], core_s.at[14], core_r.at[14], other)
    swap.start()
    swap.wait_recv()
    mine = pl.ds(pl.multiple_of(here * 8, 8), 8)
    ob[mine, :] = (co[pl.ds(0, 8), :] + co[pl.ds(8, 8), :]) * (1.0 / (128 * 256))

    def share(o):
        to = {"y": (me["y"] + o // 4) % 4, "z": (me["z"] + o % 4) % 4}
        return remote(ob.at[mine, :], ob.at[mine, :], ag_s.at[o], ag_r.at[o], moved(me, **to))

    lax.fori_loop(1, 16, lambda o, _: (share(o).start(), 0)[1], 0)
    swap.wait_send()
    each_piece(lambda p: p.wait_send())
    lax.fori_loop(1, 16, lambda o, _: (share(o).wait_send(), 0)[1], 0)
    lax.fori_loop(1, 16, lambda o, _: (share(o).wait_recv(), 0)[1], 0)
    gr_out[...] = ob[...]


def hand_on(a, b, to_a, to_b):
    to_a[...] = a[...]
    to_b[...] = b[...]


def local(matrix, signs, indices, counts):
    f32, i32 = jnp.float32, jnp.int32
    vmem, smem, dma = pltpu.VMEM, pltpu.SMEM, pltpu.SemaphoreType.DMA
    in_vmem = pl.BlockSpec(memory_space=vmem)
    sketch, gram = pl.pallas_call(
        kernel,
        name="sketch_gram",
        out_shape=(jax.ShapeDtypeStruct((256, 256), f32), jax.ShapeDtypeStruct((128, 128), f32)),
        in_specs=[pl.BlockSpec(memory_space=pl.ANY), in_vmem, in_vmem, pl.BlockSpec(memory_space=smem)],
        out_specs=(in_vmem, in_vmem),
        scratch_shapes=[
            vmem((4096, 128), f32), vmem((4096, 128), f32), vmem((32, 128), i32), vmem((128, 128), f32),
            vmem((4, 1024, 128), f32), vmem((4, 1024, 128), f32), vmem((32, 128), i32), vmem((32, 128), i32),
            vmem((4, 1024, 128), f32), vmem((4096, 128), f32), vmem((256, 128), f32),
            vmem((2, 2048, 128), f32), vmem((2, 2048, 128), f32), vmem((2, 2048, 128), f32),
            vmem((4096, 128), f32), vmem((4096, 128), f32),
            vmem((4, 2048, 128), f32), vmem((4, 2048, 128), f32),
            vmem((4, 512, 128), f32), vmem((4, 512, 128), f32),
            vmem((1024,), i32), vmem((4096,), i32), vmem((4096,), i32),
            vmem((16384,), i32), vmem((16384,), i32), vmem((16384,), i32),
            smem((16384,), i32), smem((16384,), i32), smem((16384,), i32),
            vmem((512, 128), f32), vmem((512, 128), f32), vmem((16, 128), f32), vmem((128, 128), f32),
            dma((2,)), dma((15,)), dma((15,)), dma((27,)), dma((27,)), dma((48,)), dma((48,)),
            dma((15,)), dma((15,)), dma((3,)), dma((64,)), dma((64,)), dma((16,)), dma((16,)),
        ],
        compiler_params=pltpu.CompilerParams(
            collective_id=0, has_side_effects=True, vmem_limit_bytes=56 * 2**20
        ),
    )(matrix, signs.reshape(32, 128), indices, counts)
    sketch, gram = pl.pallas_call(
        hand_on,
        name="hand_on",
        out_shape=(jax.ShapeDtypeStruct((256, 256), f32), jax.ShapeDtypeStruct((128, 128), f32)),
        in_specs=[in_vmem] * 2,
        out_specs=(in_vmem,) * 2,
    )(sketch, gram)
    return sketch, gram[None]


def solution(mesh):
    in_specs = (P(("rx", "ry"), None), P(("rx", "ry")), P(("rx", "ry")), P(("rx", "ry")))
    out_specs = (P(("rx", "ry"), None), P("ry", None, None))
    return jax.shard_map(local, mesh=mesh, in_specs=in_specs, out_specs=out_specs, check_vma=False)
```

```python
import functools

import jax
import jax.numpy as jnp
from jax import lax
from jax.experimental import pallas as pl
from jax.experimental.pallas import tpu as pltpu
from jax.sharding import PartitionSpec as P

MESH = pl.DeviceIdType.MESH
BLK = 128
HALF = 64
FAR = (2, 1, 3)
PARTS = (("y", "x", "z"), ("x", "z", "y"), ("y", "z", "x"), ("z", "x", "y"))


def coords():
    rx = lax.axis_index("rx")
    return {"y": rx // 8, "z": (rx // 2) % 4, "c": rx % 2, "x": lax.axis_index("ry")}


def device(at):
    return ((at["y"] * 4 + at["z"]) * 2 + at["c"], at["x"])


def moved(at, **to):
    return device({**at, **to})


def sign4(a, b):
    odd = (a % 2) * (b % 2) + (a // 2) * (b // 2)
    return (1 - 2 * (odd % 2)).astype(jnp.float32)


def hadamard(n):
    both = lax.broadcasted_iota(jnp.int32, (n, n), 0) & lax.broadcasted_iota(jnp.int32, (n, n), 1)
    both = both ^ (both >> 4)
    both = both ^ (both >> 2)
    both = both ^ (both >> 1)
    return (1 - 2 * (both & 1)).astype(jnp.float32)


def kernel(
    x_hbm, sg, idx, cnt, sk_out, gr_out,
    xm, bo, had, ry, ro, sy, syo, cy, dy, r, a, b, c, d1, d3, e, f, g, h,
    tile, ly, lz, pzy, pxy, pxz, szy, sxy, sxz, gp, rb, co, ob,
    loc_sem, core_s, core_r, y_s, y_r, st_s, st_r, ix_s, ix_r, sm_sem, rs_s, rs_r, ag_s, ag_r,
):
    me = coords()
    done = {1: d1, 3: d3}
    lane = lax.broadcasted_iota(jnp.int32, (1, 128), 1) < HALF
    other = moved(me, c=1 - me["c"])

    def rows(start, size):
        return pl.ds(pl.multiple_of(start, 1024 if size % 1024 == 0 else 8), size)

    def remote(src, dst, send, recv, to):
        return pltpu.make_async_remote_copy(
            src_ref=src, dst_ref=dst, send_sem=send, recv_sem=recv, device_id=to, device_id_type=MESH
        )

    load = pltpu.make_async_copy(x_hbm.at[:, pl.ds(128, 128)], xm, loc_sem.at[0])
    keep = pltpu.make_async_copy(
        x_hbm.at[rows(me["y"] * 1024, 1024), pl.ds(0, 128)], ry.at[me["y"]], loc_sem.at[1]
    )
    load.start()
    keep.start()

    barrier = pltpu.get_barrier_semaphore()

    for axis in "yxz":
        for dist in (1, 2, 3):
            to = moved(me, **{axis: (me[axis] + dist) % 4})
            pl.semaphore_signal(barrier, inc=1, device_id=to, device_id_type=MESH)
    pl.semaphore_signal(barrier, inc=1, device_id=other, device_id_type=MESH)

    had[...] = hadamard(BLK)
    tile[...] = jnp.zeros_like(tile)
    tile[pl.ds(0, 128)] = idx[pl.ds(0, 128)]
    tile[pl.ds(128, 128)] = idx[pl.ds(128, 128)] ^ 2048
    tile[pl.ds(256, 128)] = idx[pl.ds(128, 128)]

    def split(v):
        hi = v.astype(jnp.bfloat16)
        return hi, (v - hi.astype(jnp.float32)).astype(jnp.bfloat16)

    def times(left, v):
        out = jnp.dot(left, jnp.concatenate(split(v), axis=1), preferred_element_type=jnp.float32)
        return out[:, :128] + out[:, 128:]

    def panel1(i, _):
        def block(at):
            left = had[...] * sg[pl.ds(at, 1), :].astype(jnp.float32)
            return times(left.astype(jnp.bfloat16), xm[rows(at * BLK, BLK), :])

        lo, hi = block(i), block(i + 16)
        place = rows(i * BLK, BLK)
        a[0, place, :] = jnp.where(lane, lo, pltpu.roll(hi, HALF, 1))
        a[1, place, :] = jnp.where(lane, pltpu.roll(lo, HALF, 1), hi)
        return 0

    load.wait()
    lax.fori_loop(0, 16, panel1, 0)
    pl.semaphore_wait(barrier, 10)

    def out_y(k, dist):
        at = (me["y"] + dist) % 4
        i = k * 3 + dist - 1
        if k == 4:
            src, dst = sg.at[rows(at * 8, 8), :], sy.at[rows(me["y"] * 8, 8), :]
        else:
            src = x_hbm.at[rows(at * 1024 + k * 256, 256), pl.ds(0, 128)]
            dst = ry.at[me["y"], pl.ds(k * 256, 256), :]
        return remote(src, dst, y_s.at[i], y_r.at[i], moved(me, y=at))

    def back_y(k, dist):
        at = (me["y"] + dist) % 4
        i = 15 + k * 3 + dist - 1
        return remote(
            cy.at[at, pl.ds(k * 256, 256), :], dy.at[rows(me["y"] * 1024 + k * 256, 256), :],
            y_s.at[i], y_r.at[i], moved(me, y=at),
        )

    def core_y(k):
        i = 9 + k
        if k == 4:
            return remote(sy, syo, core_s.at[i], core_r.at[i], other)
        place = pl.ds(k * 256, 256)
        return remote(ry.at[:, place, :], ro.at[:, place, :], core_s.at[i], core_r.at[i], other)

    def line(buf, axis, n, dist):
        at = (me[axis] + dist) % 4
        i = n * 3 + dist - 1
        return remote(tile, buf.at[rows(me[axis] * 1024, 1024)], ix_s.at[i], ix_r.at[i], moved(me, **{axis: at}))

    def plane(src, buf, axis, n, dist):
        at = (me[axis] + dist) % 4
        i = 6 + n * 3 + dist - 1
        return remote(src, buf.at[rows(me[axis] * 4096, 4096)], ix_s.at[i], ix_r.at[i], moved(me, **{axis: at}))

    lines = ((ly, "y", 0), (lz, "z", 1))
    planes = ((ly, pzy, "z", 0), (ly, pxy, "x", 1), (lz, pxz, "x", 2))

    def exchange(stage, part, dist):
        axis = PARTS[part][max(stage - 1, 0)]
        at = (me[axis] + dist) % 4
        size = 128 if stage == 3 else 512
        i = (stage * 4 + part) * 3 + dist - 1
        src = (a, c, e, g)[stage].at[part // 2 if stage < 2 else part, rows(at * size, size), :]
        mine = rows(me[axis] * size, size)
        if stage == 1:
            dst = done[part].at[mine, :]
        else:
            dst = (b, None, f, h)[stage].at[part // 2 if stage < 2 else part, mine, :]
        return remote(src, dst, st_s.at[i], st_r.at[i], moved(me, **{axis: at}))

    def send(stage, part):
        for dist in FAR:
            exchange(stage, part, dist).start()

    def arrive(stage, part):
        for dist in (1, 2, 3):
            exchange(stage, part, dist).wait_recv()

    def own(axis, size):
        return rows(me[axis] * size, size)

    def core_b(part, dist):
        n, i = part // 2, part // 2 * 4 + dist
        place = rows((me[PARTS[part][0]] - dist + 4) % 4 * 512, 512)
        return remote(b.at[n, place, :], bo.at[n, place, :], core_s.at[i], core_r.at[i], other)

    for dist in FAR:
        out_y(4, dist).start()
        out_y(0, dist).start()
    for part in (1, 3):
        send(0, part)
        b[part // 2, own(PARTS[part][0], 512), :] = a[part // 2, own(PARTS[part][0], 512), :]
        core_b(part, 0).start()
    for buf, axis, n in lines:
        for dist in (1, 2, 3):
            line(buf, axis, n, dist).start()
        buf[rows(me[axis] * 1024, 1024)] = tile[...]
    for k in range(1, 4):
        for dist in FAR:
            out_y(k, dist).start()

    sign = (1 - 2 * me["c"]).astype(jnp.float32)

    def mixed(s0, s1, x0, x1):
        hm = had[...]
        left = jnp.concatenate(
            [hm * (s0.astype(jnp.float32) * sign), hm * s1.astype(jnp.float32)], axis=1
        ).astype(jnp.bfloat16)
        return times(left, jnp.concatenate([x0, x1], axis=0))

    def four(v):
        s, t, u, w = v[0] + v[1], v[0] - v[1], v[2] + v[3], v[2] - v[3]
        return s + u, t + w, s - u, t - w

    def panel0(k):
        def step(n, _):
            at = k * 2 + n
            place = rows(at * BLK, BLK)
            v = [
                mixed(sy[pl.ds(q * 8 + at, 1), :], syo[pl.ds(q * 8 + at, 1), :], ry[q, place, :], ro[q, place, :])
                for q in range(4)
            ]
            for q, out in enumerate(four(v)):
                cy[q, place, :] = out
            return 0

        lax.fori_loop(0, 2, step, 0)
        for dist in FAR:
            back_y(k, dist).start()
        dy[rows(me["y"] * 1024 + k * 256, 256), :] = cy[me["y"], pl.ds(k * 256, 256), :]

    def across(k):
        for dist in (1, 2, 3):
            out_y(k, dist).wait_recv()
        core_y(k).start()

    def across_b(part):
        for dist in FAR:
            exchange(0, part, dist).wait_recv()
            core_b(part, dist).start()

    def whole(part):
        n, axis = part // 2, PARTS[part][0]
        for dist in range(4):
            core_b(part, dist).wait_recv()

        def step(i, _):
            places = [rows(q * 512 + i * 32, 32) for q in range(4)]
            for place, out in zip(places, four([b[n, p, :] * sign + bo[n, p, :] for p in places])):
                c[n, place, :] = out
            return 0

        lax.fori_loop(0, 16, step, 0)
        send(1, part)
        done[part][own(axis, 512), :] = c[n, own(axis, 512), :]

    def gather(part, m, dst):
        table, src = {1: szy, 3: sxy}[part], done[part]

        def some(i, _):
            base = (m * 4 + i // 2) * 1024 + (i % 2) * 64
            for u in range(64):
                lo = src[pl.ds(table[base + u], 1), :]
                hi = src[pl.ds(table[base + 128 + u], 1), :]
                dst[part, pl.ds(m * 512 + i * 64 + u, 1), :] = jnp.where(lane, lo, hi)
            return 0

        lax.fori_loop(0, 8, some, 0)

    def turned(part):
        arrive(1, part)

        def turn(i, _):
            done[part][rows(2048 + i * 64, 64), :] = pltpu.roll(done[part][rows(i * 64, 64), :], HALF, 1)
            return 0

        lax.fori_loop(0, 32, turn, 0)

    def pruned(part, dist):
        axis = PARTS[part][1]
        gather(part, (me[axis] + dist) % 4, e if dist else f)
        if dist:
            exchange(2, part, dist).start()

    def far(n):
        return jnp.where(n == 0, 2, jnp.where(n == 1, 1, jnp.where(n == 2, 3, 0)))

    def cells(xs, zs):
        def cell(n, _):
            x = (me["x"] + far(xs[0] + n if len(xs) > 1 else xs[0])) % 4
            z = (me["z"] + far(zs[0] + n if len(zs) > 1 else zs[0])) % 4
            base = (x * 4 + z) * 1024
            table = sxz

            def some(i, _):
                for u in range(32):
                    r[pl.ds(i * 32 + u, 1), :] = dy[pl.ds(table[base + i * 32 + u], 1), :]
                    r[pl.ds(128 + i * 32 + u, 1), :] = dy[pl.ds(table[base + 256 + i * 32 + u], 1), :]
                return 0

            lax.fori_loop(0, 4, some, 0)
            lo, hi = r[pl.ds(0, 128), :], r[pl.ds(128, 128), :]
            e[0, rows(x * 512 + z * 128, 128), :] = jnp.where(lane, lo, pltpu.roll(hi, HALF, 1))
            e[2, rows(z * 512 + x * 128, 128), :] = jnp.where(lane, pltpu.roll(lo, HALF, 1), hi)
            return 0

        lax.fori_loop(0, max(len(xs), len(zs)), cell, 0)

    def pruned_y():
        for k in range(4):
            for dist in (1, 2, 3):
                back_y(k, dist).wait_recv()
        for n, dist in enumerate(FAR):
            cells((n,), range(n, 4))
            exchange(2, 0, dist).start()
            cells(range(n + 1, 4), (n,))
            exchange(2, 2, dist).start()
        cells((3,), (3,))
        for part in (0, 2):
            f[part, own(PARTS[part][1], 512), :] = e[part, own(PARTS[part][1], 512), :]

    def add_up(part, src, size, axis):
        signs = [sign4(me[axis], jnp.int32(q)) for q in range(4)]

        def at(start, count):
            total = src[part, pl.ds(start, count), :]
            for q in range(1, 4):
                total = total + signs[q] * src[part, rows(q * size + start, count), :]
            return total

        return at

    def last(part):
        axis = PARTS[part][2]
        arrive(2, part)
        sums = add_up(part, f, 512, PARTS[part][1])

        def step(i, _):
            start = pl.multiple_of(i * 32, 32)
            g[part, pl.ds(start, 32), :] = sums(start, 32)
            return 0

        lax.fori_loop(0, 16, step, 0)
        send(3, part)
        h[part, own(axis, 128), :] = g[part, own(axis, 128), :]

    def final(part):
        arrive(3, part)
        return add_up(part, h, 128, PARTS[part][2])(0, 128)

    keep.wait()
    for dist in (1, 2, 3):
        out_y(4, dist).wait_recv()
    sy[own("y", 8), :] = sg[own("y", 8), :]
    core_y(4).start()
    across(0)
    for buf, axis, n in lines:
        for dist in (1, 2, 3):
            line(buf, axis, n, dist).wait_recv()
    for src, buf, axis, n in planes:
        for dist in (1, 2, 3):
            plane(src, buf, axis, n, dist).start()
        buf[rows(me[axis] * 4096, 4096)] = src[...]
    core_y(4).wait_recv()
    core_y(0).wait_recv()
    panel0(0)
    across(1)
    across_b(1)
    across_b(3)
    core_y(1).wait_recv()
    panel0(1)
    whole(1)
    whole(3)
    across(2)
    core_y(2).wait_recv()
    panel0(2)

    def to_smem(i):
        return pltpu.make_async_copy(planes[i][1], (szy, sxy, sxz)[i], sm_sem.at[i])

    for i, (src, buf, axis, n) in enumerate(planes):
        for dist in (1, 2, 3):
            plane(src, buf, axis, n, dist).wait_recv()
        to_smem(i).start()
    across(3)
    core_y(3).wait_recv()
    panel0(3)
    for i in range(3):
        to_smem(i).wait()
    turned(1)
    pruned(1, 2)
    turned(3)
    pruned(3, 2)
    pruned(1, 1)
    pruned(3, 1)
    pruned(1, 3)
    pruned(3, 3)
    pruned(1, 0)
    pruned(3, 0)
    pruned_y()
    scale = 1.0 / (128 * BLK) ** 0.5
    slot = lax.broadcasted_iota(jnp.int32, (128, 1), 0)
    count = cnt[0]

    def finish(panel, lower, upper):
        p0, p1 = final(lower), final(upper)
        cols = pl.ds(panel * 128, 128)
        lo = jnp.where(lane, p0, pltpu.roll(p1, HALF, 1)) * scale
        hi = jnp.where(lane, pltpu.roll(p0, HALF, 1), p1) * scale
        sk_out[pl.ds(0, 128), cols] = jnp.where(slot < count, lo, 0.0)
        sk_out[pl.ds(128, 128), cols] = jnp.where(slot + 128 < count, hi, 0.0)
        return jnp.concatenate(split(sk_out[:, cols]), axis=1)

    here = me["y"] * 4 + me["z"]

    def gram(p, q):
        out = lax.dot_general(p, q, (((0,), (0,)), ((), ())), preferred_element_type=jnp.float32)
        out = out[:128] + out[128:]
        return [out[:, i : i + 128] + out[:, i + 128 : i + 256] for i in range(0, out.shape[1], 256)]

    def piece(dx, o):
        to = {"y": (me["y"] + o // 4) % 4, "z": (me["z"] + o % 4) % 4, "x": (me["x"] + dx) % 4}
        src = to["x"] * 128 + (to["y"] * 4 + to["z"]) * 8
        dst = (here * 4 + me["x"]) * 8
        n = dx * 16 + o
        return remote(gp.at[rows(src, 8), :], rb.at[rows(dst, 8), :], rs_s.at[n], rs_r.at[n], moved(me, **to))

    def scatter(n):
        dx = (n - me["x"] + 4) % 4

        def step(o, _):
            piece(dx, o).start()
            return 0

        lax.fori_loop(1, 16, step, 0)

        @pl.when(dx != 0)
        def _():
            piece(dx, 0).start()

    def each_piece(act):
        def step(n, _):
            act(piece(n // 16, n % 16))
            return 0

        lax.fori_loop(1, 64, step, 0)

    last(1)
    last(3)
    last(0)
    last(2)
    sk1 = finish(1, 1, 3)
    gp[pl.ds(384, 128), :] = gram(sk1, sk1)[0]
    scatter(3)
    sk0 = finish(0, 0, 2)
    first, second = gram(sk0, jnp.concatenate([sk0, sk1], axis=1))
    gp[pl.ds(0, 128), :] = first
    scatter(0)
    gp[pl.ds(128, 128), :] = second
    scatter(1)
    gp[pl.ds(256, 128), :] = second.T
    scatter(2)
    rb[rows((here * 4 + me["x"]) * 8, 8), :] = gp[rows(me["x"] * 128 + here * 8, 8), :]
    for part in (1, 3):
        for dist in range(4):
            core_b(part, dist).wait_send()
    for k in range(5):
        core_y(k).wait_send()
    for dist in (1, 2, 3):
        for buf, axis, n in lines:
            line(buf, axis, n, dist).wait_send()
        for src, buf, axis, n in planes:
            plane(src, buf, axis, n, dist).wait_send()
        for k in range(5):
            out_y(k, dist).wait_send()
        for k in range(4):
            back_y(k, dist).wait_send()
        for stage in range(4):
            for part in (1, 3) if stage < 2 else range(4):
                exchange(stage, part, dist).wait_send()
    each_piece(lambda p: p.wait_recv())
    co[pl.ds(0, 8), :] = rb[...].reshape(64, 8, 128).sum(0)
    swap = remote(co.at[pl.ds(0, 8), :], co.at[pl.ds(8, 8), :], core_s.at[14], core_r.at[14], other)
    swap.start()
    swap.wait_recv()
    mine = pl.ds(pl.multiple_of(here * 8, 8), 8)
    ob[mine, :] = (co[pl.ds(0, 8), :] + co[pl.ds(8, 8), :]) * (1.0 / (128 * 256))

    def share(o):
        to = {"y": (me["y"] + o // 4) % 4, "z": (me["z"] + o % 4) % 4}
        return remote(ob.at[mine, :], ob.at[mine, :], ag_s.at[o], ag_r.at[o], moved(me, **to))

    lax.fori_loop(1, 16, lambda o, _: (share(o).start(), 0)[1], 0)
    swap.wait_send()
    each_piece(lambda p: p.wait_send())
    lax.fori_loop(1, 16, lambda o, _: (share(o).wait_send(), 0)[1], 0)
    lax.fori_loop(1, 16, lambda o, _: (share(o).wait_recv(), 0)[1], 0)
    gr_out[...] = ob[...]


def hand_on(a, b, to_a, to_b):
    to_a[...] = a[...]
    to_b[...] = b[...]


def local(matrix, signs, indices, counts):
    f32, i32 = jnp.float32, jnp.int32
    vmem, smem, dma = pltpu.VMEM, pltpu.SMEM, pltpu.SemaphoreType.DMA
    in_vmem = pl.BlockSpec(memory_space=vmem)
    sketch, gram = pl.pallas_call(
        kernel,
        name="sketch_gram",
        out_shape=(jax.ShapeDtypeStruct((256, 256), f32), jax.ShapeDtypeStruct((128, 128), f32)),
        in_specs=[pl.BlockSpec(memory_space=pl.ANY), in_vmem, in_vmem, pl.BlockSpec(memory_space=smem)],
        out_specs=(in_vmem, in_vmem),
        scratch_shapes=[
            vmem((4096, 128), f32), vmem((2, 2048, 128), f32), vmem((128, 128), f32),
            vmem((4, 1024, 128), f32), vmem((4, 1024, 128), f32), vmem((32, 128), i32), vmem((32, 128), i32),
            vmem((4, 1024, 128), f32), vmem((4096, 128), f32), vmem((256, 128), f32),
            vmem((2, 2048, 128), f32), vmem((2, 2048, 128), f32), vmem((2, 2048, 128), f32),
            vmem((4096, 128), f32), vmem((4096, 128), f32),
            vmem((4, 2048, 128), f32), vmem((4, 2048, 128), f32),
            vmem((4, 512, 128), f32), vmem((4, 512, 128), f32),
            vmem((1024,), i32), vmem((4096,), i32), vmem((4096,), i32),
            vmem((16384,), i32), vmem((16384,), i32), vmem((16384,), i32),
            smem((16384,), i32), smem((16384,), i32), smem((16384,), i32),
            vmem((512, 128), f32), vmem((512, 128), f32), vmem((16, 128), f32), vmem((128, 128), f32),
            dma((2,)), dma((15,)), dma((15,)), dma((27,)), dma((27,)), dma((48,)), dma((48,)),
            dma((15,)), dma((15,)), dma((3,)), dma((64,)), dma((64,)), dma((16,)), dma((16,)),
        ],
        compiler_params=pltpu.CompilerParams(
            collective_id=0, has_side_effects=True, vmem_limit_bytes=56 * 2**20
        ),
    )(matrix, signs.reshape(32, 128), indices, counts)
    sketch, gram = pl.pallas_call(
        hand_on,
        name="hand_on",
        out_shape=(jax.ShapeDtypeStruct((256, 256), f32), jax.ShapeDtypeStruct((128, 128), f32)),
        in_specs=[in_vmem] * 2,
        out_specs=(in_vmem,) * 2,
    )(sketch, gram)
    return sketch, gram[None]


def solution(mesh):
    in_specs = (P(("rx", "ry"), None), P(("rx", "ry")), P(("rx", "ry")), P(("rx", "ry")))
    out_specs = (P(("rx", "ry"), None), P("ry", None, None))
    return jax.shard_map(local, mesh=mesh, in_specs=in_specs, out_specs=out_specs, check_vma=False)
```

```python
import functools

import jax
import jax.numpy as jnp
from jax import lax
from jax.experimental import pallas as pl
from jax.experimental.pallas import tpu as pltpu
from jax.sharding import PartitionSpec as P

MESH = pl.DeviceIdType.MESH
BLK = 128
HALF = 64
FAR = (2, 1, 3)
PARTS = (("y", "x", "z"), ("x", "z", "y"), ("y", "z", "x"), ("z", "x", "y"))


def coords():
    rx = lax.axis_index("rx")
    return {"y": rx // 8, "z": (rx // 2) % 4, "c": rx % 2, "x": lax.axis_index("ry")}


def device(at):
    return ((at["y"] * 4 + at["z"]) * 2 + at["c"], at["x"])


def moved(at, **to):
    return device({**at, **to})


def sign4(a, b):
    odd = (a % 2) * (b % 2) + (a // 2) * (b // 2)
    return (1 - 2 * (odd % 2)).astype(jnp.float32)


def hadamard(n):
    both = lax.broadcasted_iota(jnp.int32, (n, n), 0) & lax.broadcasted_iota(jnp.int32, (n, n), 1)
    both = both ^ (both >> 4)
    both = both ^ (both >> 2)
    both = both ^ (both >> 1)
    return (1 - 2 * (both & 1)).astype(jnp.float32)


def kernel(
    x_hbm, sg, idx, cnt, sk_out, gr_out,
    xm, bo, had, ry, ro, sy, syo, cy, dy, r, a, b, c, d1, d3, e, f, g, h,
    tile, ly, lz, pzy, pxy, pxz, szy, sxy, sxz, gp, rb, co, ob,
    loc_sem, core_s, core_r, y_s, y_r, st_s, st_r, ix_s, ix_r, sm_sem, rs_s, rs_r, ag_s, ag_r,
):
    me = coords()
    done = {1: d1, 3: d3}
    lane = lax.broadcasted_iota(jnp.int32, (1, 128), 1) < HALF
    other = moved(me, c=1 - me["c"])

    def rows(start, size):
        return pl.ds(pl.multiple_of(start, 1024 if size % 1024 == 0 else 8), size)

    def remote(src, dst, send, recv, to):
        return pltpu.make_async_remote_copy(
            src_ref=src, dst_ref=dst, send_sem=send, recv_sem=recv, device_id=to, device_id_type=MESH
        )

    load = pltpu.make_async_copy(x_hbm.at[:, pl.ds(128, 128)], xm, loc_sem.at[0])
    keep = pltpu.make_async_copy(
        x_hbm.at[rows(me["y"] * 1024, 1024), pl.ds(0, 128)], ry.at[me["y"]], loc_sem.at[1]
    )
    load.start()
    keep.start()

    barrier = pltpu.get_barrier_semaphore()

    for axis in "yxz":
        for dist in (1, 2, 3):
            to = moved(me, **{axis: (me[axis] + dist) % 4})
            pl.semaphore_signal(barrier, inc=1, device_id=to, device_id_type=MESH)
    pl.semaphore_signal(barrier, inc=1, device_id=other, device_id_type=MESH)

    had[...] = hadamard(BLK)
    tile[...] = jnp.zeros_like(tile)
    tile[pl.ds(0, 128)] = idx[pl.ds(0, 128)]
    tile[pl.ds(128, 128)] = idx[pl.ds(128, 128)] ^ 2048
    tile[pl.ds(256, 128)] = idx[pl.ds(128, 128)]

    def split(v):
        hi = v.astype(jnp.bfloat16)
        return hi, (v - hi.astype(jnp.float32)).astype(jnp.bfloat16)

    def times(left, v):
        out = jnp.dot(left, jnp.concatenate(split(v), axis=1), preferred_element_type=jnp.float32)
        return out[:, :128] + out[:, 128:]

    def panel1(i, _):
        def block(at):
            left = had[...] * sg[pl.ds(at, 1), :].astype(jnp.float32)
            return times(left.astype(jnp.bfloat16), xm[rows(at * BLK, BLK), :])

        lo, hi = block(i), block(i + 16)
        place = rows(i * BLK, BLK)
        a[0, place, :] = jnp.where(lane, lo, pltpu.roll(hi, HALF, 1))
        a[1, place, :] = jnp.where(lane, pltpu.roll(lo, HALF, 1), hi)
        return 0

    pl.semaphore_wait(barrier, 10)

    def out_y(k, dist):
        at = (me["y"] + dist) % 4
        i = k * 3 + dist - 1
        if k == 4:
            src, dst = sg.at[rows(at * 8, 8), :], sy.at[rows(me["y"] * 8, 8), :]
        else:
            src = x_hbm.at[rows(at * 1024 + k * 256, 256), pl.ds(0, 128)]
            dst = ry.at[me["y"], pl.ds(k * 256, 256), :]
        return remote(src, dst, y_s.at[i], y_r.at[i], moved(me, y=at))

    def back_y(k, dist):
        at = (me["y"] + dist) % 4
        i = 15 + k * 3 + dist - 1
        return remote(
            cy.at[at, pl.ds(k * 256, 256), :], dy.at[rows(me["y"] * 1024 + k * 256, 256), :],
            y_s.at[i], y_r.at[i], moved(me, y=at),
        )

    def core_y(k):
        i = 9 + k
        if k == 4:
            return remote(sy, syo, core_s.at[i], core_r.at[i], other)
        place = pl.ds(k * 256, 256)
        return remote(ry.at[:, place, :], ro.at[:, place, :], core_s.at[i], core_r.at[i], other)

    def line(buf, axis, n, dist):
        at = (me[axis] + dist) % 4
        i = n * 3 + dist - 1
        return remote(tile, buf.at[rows(me[axis] * 1024, 1024)], ix_s.at[i], ix_r.at[i], moved(me, **{axis: at}))

    def plane(src, buf, axis, n, dist):
        at = (me[axis] + dist) % 4
        i = 6 + n * 3 + dist - 1
        return remote(src, buf.at[rows(me[axis] * 4096, 4096)], ix_s.at[i], ix_r.at[i], moved(me, **{axis: at}))

    lines = ((ly, "y", 0), (lz, "z", 1))
    planes = ((ly, pzy, "z", 0), (ly, pxy, "x", 1), (lz, pxz, "x", 2))

    def exchange(stage, part, dist):
        axis = PARTS[part][max(stage - 1, 0)]
        at = (me[axis] + dist) % 4
        size = 128 if stage == 3 else 512
        i = (stage * 4 + part) * 3 + dist - 1
        src = (a, c, e, g)[stage].at[part // 2 if stage < 2 else part, rows(at * size, size), :]
        mine = rows(me[axis] * size, size)
        if stage == 1:
            dst = done[part].at[mine, :]
        else:
            dst = (b, None, f, h)[stage].at[part // 2 if stage < 2 else part, mine, :]
        return remote(src, dst, st_s.at[i], st_r.at[i], moved(me, **{axis: at}))

    def send(stage, part):
        for dist in FAR:
            exchange(stage, part, dist).start()

    def arrive(stage, part):
        for dist in (1, 2, 3):
            exchange(stage, part, dist).wait_recv()

    def own(axis, size):
        return rows(me[axis] * size, size)

    def core_b(part, dist):
        n, i = part // 2, part // 2 * 4 + dist
        place = rows((me[PARTS[part][0]] - dist + 4) % 4 * 512, 512)
        return remote(b.at[n, place, :], bo.at[n, place, :], core_s.at[i], core_r.at[i], other)

    for dist in FAR:
        out_y(4, dist).start()
    for buf, axis, n in lines:
        for dist in (1, 2, 3):
            line(buf, axis, n, dist).start()
    for dist in FAR:
        out_y(0, dist).start()
    load.wait()
    lax.fori_loop(0, 16, panel1, 0)
    for part in (1, 3):
        send(0, part)
        b[part // 2, own(PARTS[part][0], 512), :] = a[part // 2, own(PARTS[part][0], 512), :]
        core_b(part, 0).start()
    for k in range(1, 4):
        for dist in FAR:
            out_y(k, dist).start()
    for buf, axis, n in lines:
        buf[rows(me[axis] * 1024, 1024)] = tile[...]

    sign = (1 - 2 * me["c"]).astype(jnp.float32)

    def mixed(s0, s1, x0, x1):
        hm = had[...]
        left = jnp.concatenate(
            [hm * (s0.astype(jnp.float32) * sign), hm * s1.astype(jnp.float32)], axis=1
        ).astype(jnp.bfloat16)
        return times(left, jnp.concatenate([x0, x1], axis=0))

    def four(v):
        s, t, u, w = v[0] + v[1], v[0] - v[1], v[2] + v[3], v[2] - v[3]
        return s + u, t + w, s - u, t - w

    def panel0(k):
        def step(n, _):
            at = k * 2 + n
            place = rows(at * BLK, BLK)
            v = [
                mixed(sy[pl.ds(q * 8 + at, 1), :], syo[pl.ds(q * 8 + at, 1), :], ry[q, place, :], ro[q, place, :])
                for q in range(4)
            ]
            for q, out in enumerate(four(v)):
                cy[q, place, :] = out
            return 0

        lax.fori_loop(0, 2, step, 0)
        for dist in FAR:
            back_y(k, dist).start()
        dy[rows(me["y"] * 1024 + k * 256, 256), :] = cy[me["y"], pl.ds(k * 256, 256), :]

    def across(k):
        for dist in (1, 2, 3):
            out_y(k, dist).wait_recv()
        core_y(k).start()

    def across_b(part):
        for dist in FAR:
            exchange(0, part, dist).wait_recv()
            core_b(part, dist).start()

    def whole(part):
        n, axis = part // 2, PARTS[part][0]
        for dist in range(4):
            core_b(part, dist).wait_recv()

        def step(i, _):
            places = [rows(q * 512 + i * 32, 32) for q in range(4)]
            for place, out in zip(places, four([b[n, p, :] * sign + bo[n, p, :] for p in places])):
                c[n, place, :] = out
            return 0

        lax.fori_loop(0, 16, step, 0)
        send(1, part)
        done[part][own(axis, 512), :] = c[n, own(axis, 512), :]

    def gather(part, m, dst):
        table, src = {1: szy, 3: sxy}[part], done[part]

        def some(i, _):
            base = (m * 4 + i // 2) * 1024 + (i % 2) * 64
            for u in range(64):
                lo = src[pl.ds(table[base + u], 1), :]
                hi = src[pl.ds(table[base + 128 + u], 1), :]
                dst[part, pl.ds(m * 512 + i * 64 + u, 1), :] = jnp.where(lane, lo, hi)
            return 0

        lax.fori_loop(0, 8, some, 0)

    def turned(part):
        arrive(1, part)

        def turn(i, _):
            done[part][rows(2048 + i * 64, 64), :] = pltpu.roll(done[part][rows(i * 64, 64), :], HALF, 1)
            return 0

        lax.fori_loop(0, 32, turn, 0)

    def pruned(part, dist):
        axis = PARTS[part][1]
        gather(part, (me[axis] + dist) % 4, e if dist else f)
        if dist:
            exchange(2, part, dist).start()

    def far(n):
        return jnp.where(n == 0, 2, jnp.where(n == 1, 1, jnp.where(n == 2, 3, 0)))

    def cells(xs, zs):
        def cell(n, _):
            x = (me["x"] + far(xs[0] + n if len(xs) > 1 else xs[0])) % 4
            z = (me["z"] + far(zs[0] + n if len(zs) > 1 else zs[0])) % 4
            base = (x * 4 + z) * 1024
            table = sxz

            def some(i, _):
                for u in range(32):
                    r[pl.ds(i * 32 + u, 1), :] = dy[pl.ds(table[base + i * 32 + u], 1), :]
                    r[pl.ds(128 + i * 32 + u, 1), :] = dy[pl.ds(table[base + 256 + i * 32 + u], 1), :]
                return 0

            lax.fori_loop(0, 4, some, 0)
            lo, hi = r[pl.ds(0, 128), :], r[pl.ds(128, 128), :]
            e[0, rows(x * 512 + z * 128, 128), :] = jnp.where(lane, lo, pltpu.roll(hi, HALF, 1))
            e[2, rows(z * 512 + x * 128, 128), :] = jnp.where(lane, pltpu.roll(lo, HALF, 1), hi)
            return 0

        lax.fori_loop(0, max(len(xs), len(zs)), cell, 0)

    def pruned_y():
        for k in range(4):
            for dist in (1, 2, 3):
                back_y(k, dist).wait_recv()
        for n, dist in enumerate(FAR):
            cells((n,), range(n, 4))
            exchange(2, 0, dist).start()
            cells(range(n + 1, 4), (n,))
            exchange(2, 2, dist).start()
        cells((3,), (3,))
        for part in (0, 2):
            f[part, own(PARTS[part][1], 512), :] = e[part, own(PARTS[part][1], 512), :]

    def add_up(part, src, size, axis):
        signs = [sign4(me[axis], jnp.int32(q)) for q in range(4)]

        def at(start, count):
            total = src[part, pl.ds(start, count), :]
            for q in range(1, 4):
                total = total + signs[q] * src[part, rows(q * size + start, count), :]
            return total

        return at

    def last(part):
        axis = PARTS[part][2]
        arrive(2, part)
        sums = add_up(part, f, 512, PARTS[part][1])

        def step(i, _):
            start = pl.multiple_of(i * 32, 32)
            g[part, pl.ds(start, 32), :] = sums(start, 32)
            return 0

        lax.fori_loop(0, 16, step, 0)
        send(3, part)
        h[part, own(axis, 128), :] = g[part, own(axis, 128), :]

    def final(part):
        arrive(3, part)
        return add_up(part, h, 128, PARTS[part][2])(0, 128)

    keep.wait()
    for dist in (1, 2, 3):
        out_y(4, dist).wait_recv()
    sy[own("y", 8), :] = sg[own("y", 8), :]
    core_y(4).start()
    across(0)
    for buf, axis, n in lines:
        for dist in (1, 2, 3):
            line(buf, axis, n, dist).wait_recv()
    for src, buf, axis, n in planes:
        for dist in (1, 2, 3):
            plane(src, buf, axis, n, dist).start()
        buf[rows(me[axis] * 4096, 4096)] = src[...]
    core_y(4).wait_recv()
    core_y(0).wait_recv()
    panel0(0)
    across(1)
    across_b(1)
    across_b(3)
    core_y(1).wait_recv()
    panel0(1)
    whole(1)
    whole(3)
    across(2)
    core_y(2).wait_recv()
    panel0(2)

    def to_smem(i):
        return pltpu.make_async_copy(planes[i][1], (szy, sxy, sxz)[i], sm_sem.at[i])

    for i, (src, buf, axis, n) in enumerate(planes):
        for dist in (1, 2, 3):
            plane(src, buf, axis, n, dist).wait_recv()
        to_smem(i).start()
    across(3)
    core_y(3).wait_recv()
    panel0(3)
    for i in range(3):
        to_smem(i).wait()
    turned(1)
    pruned(1, 2)
    turned(3)
    pruned(3, 2)
    pruned(1, 1)
    pruned(3, 1)
    pruned(1, 3)
    pruned(3, 3)
    pruned(1, 0)
    pruned(3, 0)
    pruned_y()
    scale = 1.0 / (128 * BLK) ** 0.5
    slot = lax.broadcasted_iota(jnp.int32, (128, 1), 0)
    count = cnt[0]

    def finish(panel, lower, upper):
        p0, p1 = final(lower), final(upper)
        cols = pl.ds(panel * 128, 128)
        lo = jnp.where(lane, p0, pltpu.roll(p1, HALF, 1)) * scale
        hi = jnp.where(lane, pltpu.roll(p0, HALF, 1), p1) * scale
        sk_out[pl.ds(0, 128), cols] = jnp.where(slot < count, lo, 0.0)
        sk_out[pl.ds(128, 128), cols] = jnp.where(slot + 128 < count, hi, 0.0)
        return jnp.concatenate(split(sk_out[:, cols]), axis=1)

    here = me["y"] * 4 + me["z"]

    def gram(p, q):
        out = lax.dot_general(p, q, (((0,), (0,)), ((), ())), preferred_element_type=jnp.float32)
        out = out[:128] + out[128:]
        return [out[:, i : i + 128] + out[:, i + 128 : i + 256] for i in range(0, out.shape[1], 256)]

    def piece(dx, o):
        to = {"y": (me["y"] + o // 4) % 4, "z": (me["z"] + o % 4) % 4, "x": (me["x"] + dx) % 4}
        src = to["x"] * 128 + (to["y"] * 4 + to["z"]) * 8
        dst = (here * 4 + me["x"]) * 8
        n = dx * 16 + o
        return remote(gp.at[rows(src, 8), :], rb.at[rows(dst, 8), :], rs_s.at[n], rs_r.at[n], moved(me, **to))

    def scatter(n):
        dx = (n - me["x"] + 4) % 4

        def step(o, _):
            piece(dx, o).start()
            return 0

        lax.fori_loop(1, 16, step, 0)

        @pl.when(dx != 0)
        def _():
            piece(dx, 0).start()

    def each_piece(act):
        def step(n, _):
            act(piece(n // 16, n % 16))
            return 0

        lax.fori_loop(1, 64, step, 0)

    last(1)
    last(3)
    last(0)
    last(2)
    sk1 = finish(1, 1, 3)
    gp[pl.ds(384, 128), :] = gram(sk1, sk1)[0]
    scatter(3)
    sk0 = finish(0, 0, 2)
    first, second = gram(sk0, jnp.concatenate([sk0, sk1], axis=1))
    gp[pl.ds(0, 128), :] = first
    scatter(0)
    gp[pl.ds(128, 128), :] = second
    scatter(1)
    gp[pl.ds(256, 128), :] = second.T
    scatter(2)
    rb[rows((here * 4 + me["x"]) * 8, 8), :] = gp[rows(me["x"] * 128 + here * 8, 8), :]
    for part in (1, 3):
        for dist in range(4):
            core_b(part, dist).wait_send()
    for k in range(5):
        core_y(k).wait_send()
    for dist in (1, 2, 3):
        for buf, axis, n in lines:
            line(buf, axis, n, dist).wait_send()
        for src, buf, axis, n in planes:
            plane(src, buf, axis, n, dist).wait_send()
        for k in range(5):
            out_y(k, dist).wait_send()
        for k in range(4):
            back_y(k, dist).wait_send()
        for stage in range(4):
            for part in (1, 3) if stage < 2 else range(4):
                exchange(stage, part, dist).wait_send()
    each_piece(lambda p: p.wait_recv())
    co[pl.ds(0, 8), :] = rb[...].reshape(64, 8, 128).sum(0)
    swap = remote(co.at[pl.ds(0, 8), :], co.at[pl.ds(8, 8), :], core_s.at[14], core_r.at[14], other)
    swap.start()
    swap.wait_recv()
    mine = pl.ds(pl.multiple_of(here * 8, 8), 8)
    ob[mine, :] = (co[pl.ds(0, 8), :] + co[pl.ds(8, 8), :]) * (1.0 / (128 * 256))

    def share(o):
        to = {"y": (me["y"] + o // 4) % 4, "z": (me["z"] + o % 4) % 4}
        return remote(ob.at[mine, :], ob.at[mine, :], ag_s.at[o], ag_r.at[o], moved(me, **to))

    lax.fori_loop(1, 16, lambda o, _: (share(o).start(), 0)[1], 0)
    swap.wait_send()
    each_piece(lambda p: p.wait_send())
    lax.fori_loop(1, 16, lambda o, _: (share(o).wait_send(), 0)[1], 0)
    lax.fori_loop(1, 16, lambda o, _: (share(o).wait_recv(), 0)[1], 0)
    gr_out[...] = ob[...]


def hand_on(a, b, to_a, to_b):
    to_a[...] = a[...]
    to_b[...] = b[...]


def local(matrix, signs, indices, counts):
    f32, i32 = jnp.float32, jnp.int32
    vmem, smem, dma = pltpu.VMEM, pltpu.SMEM, pltpu.SemaphoreType.DMA
    in_vmem = pl.BlockSpec(memory_space=vmem)
    sketch, gram = pl.pallas_call(
        kernel,
        name="sketch_gram",
        out_shape=(jax.ShapeDtypeStruct((256, 256), f32), jax.ShapeDtypeStruct((128, 128), f32)),
        in_specs=[pl.BlockSpec(memory_space=pl.ANY), in_vmem, in_vmem, pl.BlockSpec(memory_space=smem)],
        out_specs=(in_vmem, in_vmem),
        scratch_shapes=[
            vmem((4096, 128), f32), vmem((2, 2048, 128), f32), vmem((128, 128), f32),
            vmem((4, 1024, 128), f32), vmem((4, 1024, 128), f32), vmem((32, 128), i32), vmem((32, 128), i32),
            vmem((4, 1024, 128), f32), vmem((4096, 128), f32), vmem((256, 128), f32),
            vmem((2, 2048, 128), f32), vmem((2, 2048, 128), f32), vmem((2, 2048, 128), f32),
            vmem((4096, 128), f32), vmem((4096, 128), f32),
            vmem((4, 2048, 128), f32), vmem((4, 2048, 128), f32),
            vmem((4, 512, 128), f32), vmem((4, 512, 128), f32),
            vmem((1024,), i32), vmem((4096,), i32), vmem((4096,), i32),
            vmem((16384,), i32), vmem((16384,), i32), vmem((16384,), i32),
            smem((16384,), i32), smem((16384,), i32), smem((16384,), i32),
            vmem((512, 128), f32), vmem((512, 128), f32), vmem((16, 128), f32), vmem((128, 128), f32),
            dma((2,)), dma((15,)), dma((15,)), dma((27,)), dma((27,)), dma((48,)), dma((48,)),
            dma((15,)), dma((15,)), dma((3,)), dma((64,)), dma((64,)), dma((16,)), dma((16,)),
        ],
        compiler_params=pltpu.CompilerParams(
            collective_id=0, has_side_effects=True, vmem_limit_bytes=56 * 2**20
        ),
    )(matrix, signs.reshape(32, 128), indices, counts)
    sketch, gram = pl.pallas_call(
        hand_on,
        name="hand_on",
        out_shape=(jax.ShapeDtypeStruct((256, 256), f32), jax.ShapeDtypeStruct((128, 128), f32)),
        in_specs=[in_vmem] * 2,
        out_specs=(in_vmem,) * 2,
    )(sketch, gram)
    return sketch, gram[None]


def solution(mesh):
    in_specs = (P(("rx", "ry"), None), P(("rx", "ry")), P(("rx", "ry")), P(("rx", "ry")))
    out_specs = (P(("rx", "ry"), None), P("ry", None, None))
    return jax.shard_map(local, mesh=mesh, in_specs=in_specs, out_specs=out_specs, check_vma=False)
```

```python
import functools

import jax
import jax.numpy as jnp
from jax import lax
from jax.experimental import pallas as pl
from jax.experimental.pallas import tpu as pltpu
from jax.sharding import PartitionSpec as P

MESH = pl.DeviceIdType.MESH
BLK = 128
HALF = 64
FAR = (2, 1, 3)
PARTS = (("y", "x", "z"), ("x", "z", "y"), ("y", "z", "x"), ("z", "x", "y"))


def coords():
    rx = lax.axis_index("rx")
    return {"y": rx // 8, "z": (rx // 2) % 4, "c": rx % 2, "x": lax.axis_index("ry")}


def device(at):
    return ((at["y"] * 4 + at["z"]) * 2 + at["c"], at["x"])


def moved(at, **to):
    return device({**at, **to})


def sign4(a, b):
    odd = (a % 2) * (b % 2) + (a // 2) * (b // 2)
    return (1 - 2 * (odd % 2)).astype(jnp.float32)


def hadamard(n):
    both = lax.broadcasted_iota(jnp.int32, (n, n), 0) & lax.broadcasted_iota(jnp.int32, (n, n), 1)
    both = both ^ (both >> 4)
    both = both ^ (both >> 2)
    both = both ^ (both >> 1)
    return (1 - 2 * (both & 1)).astype(jnp.float32)


def kernel(
    x_hbm, sg, idx, cnt, sk_out, gr_out,
    xm, bo, had, ry, ro, sy, syo, cy, dy, r, a, b, c, d1, d3, e, f, g, h,
    tile, ly, lz, pzy, pxy, pxz, szy, sxy, sxz, gp, rb, ob,
    loc_sem, core_s, core_r, y_s, y_r, st_s, st_r, ix_s, ix_r, sm_sem, rs_s, rs_r, ag_s, ag_r,
):
    me = coords()
    done = {1: d1, 3: d3}
    lane = lax.broadcasted_iota(jnp.int32, (1, 128), 1) < HALF
    other = moved(me, c=1 - me["c"])

    def rows(start, size):
        return pl.ds(pl.multiple_of(start, 1024 if size % 1024 == 0 else 8), size)

    def remote(src, dst, send, recv, to):
        return pltpu.make_async_remote_copy(
            src_ref=src, dst_ref=dst, send_sem=send, recv_sem=recv, device_id=to, device_id_type=MESH
        )

    load = pltpu.make_async_copy(x_hbm.at[:, pl.ds(128, 128)], xm, loc_sem.at[0])
    keep = pltpu.make_async_copy(
        x_hbm.at[rows(me["y"] * 1024, 1024), pl.ds(0, 128)], ry.at[me["y"]], loc_sem.at[1]
    )
    load.start()
    keep.start()

    barrier = pltpu.get_barrier_semaphore()

    for axis in "yxz":
        for dist in (1, 2, 3):
            to = moved(me, **{axis: (me[axis] + dist) % 4})
            pl.semaphore_signal(barrier, inc=1, device_id=to, device_id_type=MESH)
    pl.semaphore_signal(barrier, inc=1, device_id=other, device_id_type=MESH)

    had[...] = hadamard(BLK)
    tile[...] = jnp.zeros_like(tile)
    tile[pl.ds(0, 128)] = idx[pl.ds(0, 128)]
    tile[pl.ds(128, 128)] = idx[pl.ds(128, 128)] ^ 2048
    tile[pl.ds(256, 128)] = idx[pl.ds(128, 128)]

    def split(v):
        hi = v.astype(jnp.bfloat16)
        return hi, (v - hi.astype(jnp.float32)).astype(jnp.bfloat16)

    def times(left, v):
        out = jnp.dot(left, jnp.concatenate(split(v), axis=1), preferred_element_type=jnp.float32)
        return out[:, :128] + out[:, 128:]

    def panel1(i, _):
        def block(at):
            left = had[...] * sg[pl.ds(at, 1), :].astype(jnp.float32)
            return times(left.astype(jnp.bfloat16), xm[rows(at * BLK, BLK), :])

        lo, hi = block(i), block(i + 16)
        place = rows(i * BLK, BLK)
        a[0, place, :] = jnp.where(lane, lo, pltpu.roll(hi, HALF, 1))
        a[1, place, :] = jnp.where(lane, pltpu.roll(lo, HALF, 1), hi)
        return 0

    pl.semaphore_wait(barrier, 10)

    def out_y(k, dist):
        at = (me["y"] + dist) % 4
        i = k * 3 + dist - 1
        if k == 4:
            src, dst = sg.at[rows(at * 8, 8), :], sy.at[rows(me["y"] * 8, 8), :]
        else:
            src = x_hbm.at[rows(at * 1024 + k * 256, 256), pl.ds(0, 128)]
            dst = ry.at[me["y"], pl.ds(k * 256, 256), :]
        return remote(src, dst, y_s.at[i], y_r.at[i], moved(me, y=at))

    def back_y(k, dist):
        at = (me["y"] + dist) % 4
        i = 15 + k * 3 + dist - 1
        return remote(
            cy.at[at, pl.ds(k * 256, 256), :], dy.at[rows(me["y"] * 1024 + k * 256, 256), :],
            y_s.at[i], y_r.at[i], moved(me, y=at),
        )

    def core_y(k):
        i = 9 + k
        if k == 4:
            return remote(sy, syo, core_s.at[i], core_r.at[i], other)
        place = pl.ds(k * 256, 256)
        return remote(ry.at[:, place, :], ro.at[:, place, :], core_s.at[i], core_r.at[i], other)

    def line(buf, axis, n, dist):
        at = (me[axis] + dist) % 4
        i = n * 3 + dist - 1
        return remote(tile, buf.at[rows(me[axis] * 1024, 1024)], ix_s.at[i], ix_r.at[i], moved(me, **{axis: at}))

    def plane(src, buf, axis, n, dist):
        at = (me[axis] + dist) % 4
        i = 6 + n * 3 + dist - 1
        return remote(src, buf.at[rows(me[axis] * 4096, 4096)], ix_s.at[i], ix_r.at[i], moved(me, **{axis: at}))

    lines = ((ly, "y", 0), (lz, "z", 1))
    planes = ((ly, pzy, "z", 0), (ly, pxy, "x", 1), (lz, pxz, "x", 2))

    def exchange(stage, part, dist):
        axis = PARTS[part][max(stage - 1, 0)]
        at = (me[axis] + dist) % 4
        size = 128 if stage == 3 else 512
        i = (stage * 4 + part) * 3 + dist - 1
        src = (a, c, e, g)[stage].at[part // 2 if stage < 2 else part, rows(at * size, size), :]
        mine = rows(me[axis] * size, size)
        if stage == 1:
            dst = done[part].at[mine, :]
        else:
            dst = (b, None, f, h)[stage].at[part // 2 if stage < 2 else part, mine, :]
        return remote(src, dst, st_s.at[i], st_r.at[i], moved(me, **{axis: at}))

    def send(stage, part):
        for dist in FAR:
            exchange(stage, part, dist).start()

    def arrive(stage, part):
        for dist in (1, 2, 3):
            exchange(stage, part, dist).wait_recv()

    def own(axis, size):
        return rows(me[axis] * size, size)

    def core_b(part, dist):
        n, i = part // 2, part // 2 * 4 + dist
        place = rows((me[PARTS[part][0]] - dist + 4) % 4 * 512, 512)
        return remote(b.at[n, place, :], bo.at[n, place, :], core_s.at[i], core_r.at[i], other)

    for dist in FAR:
        out_y(4, dist).start()
    for buf, axis, n in lines:
        for dist in (1, 2, 3):
            line(buf, axis, n, dist).start()
    for dist in FAR:
        out_y(0, dist).start()
    load.wait()
    lax.fori_loop(0, 16, panel1, 0)
    for part in (1, 3):
        send(0, part)
        b[part // 2, own(PARTS[part][0], 512), :] = a[part // 2, own(PARTS[part][0], 512), :]
        core_b(part, 0).start()
    for k in range(1, 4):
        for dist in FAR:
            out_y(k, dist).start()
    for buf, axis, n in lines:
        buf[rows(me[axis] * 1024, 1024)] = tile[...]

    sign = (1 - 2 * me["c"]).astype(jnp.float32)

    def mixed(s0, s1, x0, x1):
        hm = had[...]
        left = jnp.concatenate(
            [hm * (s0.astype(jnp.float32) * sign), hm * s1.astype(jnp.float32)], axis=1
        ).astype(jnp.bfloat16)
        return times(left, jnp.concatenate([x0, x1], axis=0))

    def four(v):
        s, t, u, w = v[0] + v[1], v[0] - v[1], v[2] + v[3], v[2] - v[3]
        return s + u, t + w, s - u, t - w

    def panel0(k):
        def step(n, _):
            at = k * 2 + n
            place = rows(at * BLK, BLK)
            v = [
                mixed(sy[pl.ds(q * 8 + at, 1), :], syo[pl.ds(q * 8 + at, 1), :], ry[q, place, :], ro[q, place, :])
                for q in range(4)
            ]
            for q, out in enumerate(four(v)):
                cy[q, place, :] = out
            return 0

        lax.fori_loop(0, 2, step, 0)
        for dist in FAR:
            back_y(k, dist).start()
        dy[rows(me["y"] * 1024 + k * 256, 256), :] = cy[me["y"], pl.ds(k * 256, 256), :]

    def across(k):
        for dist in (1, 2, 3):
            out_y(k, dist).wait_recv()
        core_y(k).start()

    def across_b(part):
        for dist in FAR:
            exchange(0, part, dist).wait_recv()
            core_b(part, dist).start()

    def whole(part):
        n, axis = part // 2, PARTS[part][0]
        for dist in range(4):
            core_b(part, dist).wait_recv()

        def step(i, _):
            places = [rows(q * 512 + i * 32, 32) for q in range(4)]
            for place, out in zip(places, four([b[n, p, :] * sign + bo[n, p, :] for p in places])):
                c[n, place, :] = out
            return 0

        lax.fori_loop(0, 16, step, 0)
        send(1, part)
        done[part][own(axis, 512), :] = c[n, own(axis, 512), :]

    def gather(part, m, dst):
        table, src = {1: szy, 3: sxy}[part], done[part]

        def some(i, _):
            base = (m * 4 + i // 2) * 1024 + (i % 2) * 64
            for u in range(64):
                lo = src[pl.ds(table[base + u], 1), :]
                hi = src[pl.ds(table[base + 128 + u], 1), :]
                dst[part, pl.ds(m * 512 + i * 64 + u, 1), :] = jnp.where(lane, lo, hi)
            return 0

        lax.fori_loop(0, 8, some, 0)

    def turned(part):
        arrive(1, part)

        def turn(i, _):
            done[part][rows(2048 + i * 64, 64), :] = pltpu.roll(done[part][rows(i * 64, 64), :], HALF, 1)
            return 0

        lax.fori_loop(0, 32, turn, 0)

    def pruned(part, dist):
        axis = PARTS[part][1]
        gather(part, (me[axis] + dist) % 4, e if dist else f)
        if dist:
            exchange(2, part, dist).start()

    def far(n):
        return jnp.where(n == 0, 2, jnp.where(n == 1, 1, jnp.where(n == 2, 3, 0)))

    def cells(xs, zs):
        def cell(n, _):
            x = (me["x"] + far(xs[0] + n if len(xs) > 1 else xs[0])) % 4
            z = (me["z"] + far(zs[0] + n if len(zs) > 1 else zs[0])) % 4
            base = (x * 4 + z) * 1024
            table = sxz

            def some(i, _):
                for u in range(32):
                    r[pl.ds(i * 32 + u, 1), :] = dy[pl.ds(table[base + i * 32 + u], 1), :]
                    r[pl.ds(128 + i * 32 + u, 1), :] = dy[pl.ds(table[base + 256 + i * 32 + u], 1), :]
                return 0

            lax.fori_loop(0, 4, some, 0)
            lo, hi = r[pl.ds(0, 128), :], r[pl.ds(128, 128), :]
            e[0, rows(x * 512 + z * 128, 128), :] = jnp.where(lane, lo, pltpu.roll(hi, HALF, 1))
            e[2, rows(z * 512 + x * 128, 128), :] = jnp.where(lane, pltpu.roll(lo, HALF, 1), hi)
            return 0

        lax.fori_loop(0, max(len(xs), len(zs)), cell, 0)

    def pruned_y():
        for k in range(4):
            for dist in (1, 2, 3):
                back_y(k, dist).wait_recv()
        for n, dist in enumerate(FAR):
            cells((n,), range(n, 4))
            exchange(2, 0, dist).start()
            cells(range(n + 1, 4), (n,))
            exchange(2, 2, dist).start()
        cells((3,), (3,))
        for part in (0, 2):
            f[part, own(PARTS[part][1], 512), :] = e[part, own(PARTS[part][1], 512), :]

    def add_up(part, src, size, axis):
        signs = [sign4(me[axis], jnp.int32(q)) for q in range(4)]

        def at(start, count):
            total = src[part, pl.ds(start, count), :]
            for q in range(1, 4):
                total = total + signs[q] * src[part, rows(q * size + start, count), :]
            return total

        return at

    def last(part):
        axis = PARTS[part][2]
        arrive(2, part)
        sums = add_up(part, f, 512, PARTS[part][1])

        def step(i, _):
            start = pl.multiple_of(i * 32, 32)
            g[part, pl.ds(start, 32), :] = sums(start, 32)
            return 0

        lax.fori_loop(0, 16, step, 0)
        send(3, part)
        h[part, own(axis, 128), :] = g[part, own(axis, 128), :]

    def final(part):
        arrive(3, part)
        return add_up(part, h, 128, PARTS[part][2])(0, 128)

    keep.wait()
    for dist in (1, 2, 3):
        out_y(4, dist).wait_recv()
    sy[own("y", 8), :] = sg[own("y", 8), :]
    core_y(4).start()
    across(0)
    for buf, axis, n in lines:
        for dist in (1, 2, 3):
            line(buf, axis, n, dist).wait_recv()
    for src, buf, axis, n in planes:
        for dist in (1, 2, 3):
            plane(src, buf, axis, n, dist).start()
        buf[rows(me[axis] * 4096, 4096)] = src[...]
    core_y(4).wait_recv()
    core_y(0).wait_recv()
    panel0(0)
    across(1)
    across_b(1)
    across_b(3)
    core_y(1).wait_recv()
    panel0(1)
    whole(1)
    whole(3)
    across(2)
    core_y(2).wait_recv()
    panel0(2)

    def to_smem(i):
        return pltpu.make_async_copy(planes[i][1], (szy, sxy, sxz)[i], sm_sem.at[i])

    for i, (src, buf, axis, n) in enumerate(planes):
        for dist in (1, 2, 3):
            plane(src, buf, axis, n, dist).wait_recv()
        to_smem(i).start()
    across(3)
    core_y(3).wait_recv()
    panel0(3)
    for i in range(3):
        to_smem(i).wait()
    turned(1)
    pruned(1, 2)
    turned(3)
    pruned(3, 2)
    pruned(1, 1)
    pruned(3, 1)
    pruned(1, 3)
    pruned(3, 3)
    pruned(1, 0)
    pruned(3, 0)
    pruned_y()
    scale = 1.0 / (128 * BLK) ** 0.5
    slot = lax.broadcasted_iota(jnp.int32, (128, 1), 0)
    count = cnt[0]

    def finish(panel, lower, upper):
        p0, p1 = final(lower), final(upper)
        cols = pl.ds(panel * 128, 128)
        lo = jnp.where(lane, p0, pltpu.roll(p1, HALF, 1)) * scale
        hi = jnp.where(lane, pltpu.roll(p0, HALF, 1), p1) * scale
        sk_out[pl.ds(0, 128), cols] = jnp.where(slot < count, lo, 0.0)
        sk_out[pl.ds(128, 128), cols] = jnp.where(slot + 128 < count, hi, 0.0)
        return jnp.concatenate(split(sk_out[:, cols]), axis=1)

    here = me["y"] * 4 + me["z"]

    def gram(p, q):
        out = lax.dot_general(p, q, (((0,), (0,)), ((), ())), preferred_element_type=jnp.float32)
        out = out[:128] + out[128:]
        return [out[:, i : i + 128] + out[:, i + 128 : i + 256] for i in range(0, out.shape[1], 256)]

    def piece(dx, o):
        to = {"y": (me["y"] + o // 4) % 4, "z": (me["z"] + o % 4) % 4, "x": (me["x"] + dx) % 4}
        src = to["x"] * 128 + (to["y"] * 4 + to["z"]) * 8
        dst = (here * 4 + me["x"]) * 8
        n = dx * 16 + o
        return remote(gp.at[rows(src, 8), :], rb.at[rows(dst, 8), :], rs_s.at[n], rs_r.at[n], moved(me, **to))

    def scatter(n):
        dx = (n - me["x"] + 4) % 4
        for o in range(1, 16):
            piece(dx, o).start()

        @pl.when(dx != 0)
        def _():
            piece(dx, 0).start()

    def each_piece(act):
        for n in range(1, 64):
            act(piece(n // 16, n % 16))

    last(1)
    last(3)
    for part in (1, 3):
        for dist in range(4):
            core_b(part, dist).wait_send()
    for k in range(5):
        core_y(k).wait_send()
    for dist in (1, 2, 3):
        for buf, axis, n in lines:
            line(buf, axis, n, dist).wait_send()
        for src, buf, axis, n in planes:
            plane(src, buf, axis, n, dist).wait_send()
        for k in range(5):
            out_y(k, dist).wait_send()
        for k in range(4):
            back_y(k, dist).wait_send()
        for stage in range(4):
            for part in (1, 3):
                exchange(stage, part, dist).wait_send()
    last(0)
    last(2)
    sk1 = finish(1, 1, 3)
    gp[pl.ds(384, 128), :] = gram(sk1, sk1)[0]
    scatter(3)
    sk0 = finish(0, 0, 2)
    first, second = gram(sk0, jnp.concatenate([sk0, sk1], axis=1))
    gp[pl.ds(0, 128), :] = first
    scatter(0)
    gp[pl.ds(128, 128), :] = second
    scatter(1)
    gp[pl.ds(256, 128), :] = second.T
    scatter(2)
    rb[rows((here * 4 + me["x"]) * 8, 8), :] = gp[rows(me["x"] * 128 + here * 8, 8), :]
    for dist in (1, 2, 3):
        for stage in (2, 3):
            for part in (0, 2):
                exchange(stage, part, dist).wait_send()
    each_piece(lambda p: p.wait_recv())
    mine = rows(here * 8, 8)
    ob[me["c"], mine, :] = rb[...].reshape(64, 8, 128).sum(0) * (1.0 / (128 * 256))

    def share(o):
        to = {"c": (me["c"] + o // 16) % 2, "y": (me["y"] + o // 4 % 4) % 4, "z": (me["z"] + o % 4) % 4}
        piece_of = ob.at[me["c"], mine, :]
        return remote(piece_of, piece_of, ag_s.at[o], ag_r.at[o], moved(me, **to))

    for o in range(1, 32):
        share(o).start()
    each_piece(lambda p: p.wait_send())
    for o in range(1, 32):
        share(o).wait_send()
        share(o).wait_recv()
    gr_out[...] = ob[0] + ob[1]


def hand_on(a, b, to_a, to_b):
    to_a[...] = a[...]
    to_b[...] = b[...]


def local(matrix, signs, indices, counts):
    f32, i32 = jnp.float32, jnp.int32
    vmem, smem, dma = pltpu.VMEM, pltpu.SMEM, pltpu.SemaphoreType.DMA
    in_vmem = pl.BlockSpec(memory_space=vmem)
    sketch, gram = pl.pallas_call(
        kernel,
        name="sketch_gram",
        out_shape=(jax.ShapeDtypeStruct((256, 256), f32), jax.ShapeDtypeStruct((128, 128), f32)),
        in_specs=[pl.BlockSpec(memory_space=pl.ANY), in_vmem, in_vmem, pl.BlockSpec(memory_space=smem)],
        out_specs=(in_vmem, in_vmem),
        scratch_shapes=[
            vmem((4096, 128), f32), vmem((2, 2048, 128), f32), vmem((128, 128), f32),
            vmem((4, 1024, 128), f32), vmem((4, 1024, 128), f32), vmem((32, 128), i32), vmem((32, 128), i32),
            vmem((4, 1024, 128), f32), vmem((4096, 128), f32), vmem((256, 128), f32),
            vmem((2, 2048, 128), f32), vmem((2, 2048, 128), f32), vmem((2, 2048, 128), f32),
            vmem((4096, 128), f32), vmem((4096, 128), f32),
            vmem((4, 2048, 128), f32), vmem((4, 2048, 128), f32),
            vmem((4, 512, 128), f32), vmem((4, 512, 128), f32),
            vmem((1024,), i32), vmem((4096,), i32), vmem((4096,), i32),
            vmem((16384,), i32), vmem((16384,), i32), vmem((16384,), i32),
            smem((16384,), i32), smem((16384,), i32), smem((16384,), i32),
            vmem((512, 128), f32), vmem((512, 128), f32), vmem((2, 128, 128), f32),
            dma((2,)), dma((15,)), dma((15,)), dma((27,)), dma((27,)), dma((48,)), dma((48,)),
            dma((15,)), dma((15,)), dma((3,)), dma((64,)), dma((64,)), dma((32,)), dma((32,)),
        ],
        compiler_params=pltpu.CompilerParams(
            collective_id=0, has_side_effects=True, vmem_limit_bytes=56 * 2**20
        ),
    )(matrix, signs.reshape(32, 128), indices, counts)
    sketch, gram = pl.pallas_call(
        hand_on,
        name="hand_on",
        out_shape=(jax.ShapeDtypeStruct((256, 256), f32), jax.ShapeDtypeStruct((128, 128), f32)),
        in_specs=[in_vmem] * 2,
        out_specs=(in_vmem,) * 2,
    )(sketch, gram)
    return sketch, gram[None]


def solution(mesh):
    in_specs = (P(("rx", "ry"), None), P(("rx", "ry")), P(("rx", "ry")), P(("rx", "ry")))
    out_specs = (P(("rx", "ry"), None), P("ry", None, None))
    return jax.shard_map(local, mesh=mesh, in_specs=in_specs, out_specs=out_specs, check_vma=False)
```

```python
import functools

import jax
import jax.numpy as jnp
from jax import lax
from jax.experimental import pallas as pl
from jax.experimental.pallas import tpu as pltpu
from jax.sharding import PartitionSpec as P

MESH = pl.DeviceIdType.MESH
BLK = 128
HALF = 64
FAR = (2, 1, 3)
PARTS = (("y", "x", "z"), ("x", "z", "y"), ("y", "z", "x"), ("z", "x", "y"))


def coords():
    rx = lax.axis_index("rx")
    return {"y": rx // 8, "z": (rx // 2) % 4, "c": rx % 2, "x": lax.axis_index("ry")}


def device(at):
    return ((at["y"] * 4 + at["z"]) * 2 + at["c"], at["x"])


def moved(at, **to):
    return device({**at, **to})


def sign4(a, b):
    odd = (a % 2) * (b % 2) + (a // 2) * (b // 2)
    return (1 - 2 * (odd % 2)).astype(jnp.float32)


def hadamard(n):
    both = lax.broadcasted_iota(jnp.int32, (n, n), 0) & lax.broadcasted_iota(jnp.int32, (n, n), 1)
    both = both ^ (both >> 4)
    both = both ^ (both >> 2)
    both = both ^ (both >> 1)
    return (1 - 2 * (both & 1)).astype(jnp.float32)


def kernel(
    x_hbm, sg, idx, cnt, sk_out, gr_out,
    xm, bo, had, ry, ro, sy, syo, cy, dy, r, a, b, c, d1, d3, e, f, g, h,
    tile, ly, lz, pzy, pxy, pxz, szy, sxy, sxz, gp, rb, ob,
    loc_sem, core_s, core_r, y_s, y_r, st_s, st_r, ix_s, ix_r, sm_sem, rs_s, rs_r, ag_s, ag_r,
):
    me = coords()
    done = {1: d1, 3: d3}
    lane = lax.broadcasted_iota(jnp.int32, (1, 128), 1) < HALF
    other = moved(me, c=1 - me["c"])

    def rows(start, size):
        return pl.ds(pl.multiple_of(start, 1024 if size % 1024 == 0 else 8), size)

    def remote(src, dst, send, recv, to):
        return pltpu.make_async_remote_copy(
            src_ref=src, dst_ref=dst, send_sem=send, recv_sem=recv, device_id=to, device_id_type=MESH
        )

    load = pltpu.make_async_copy(x_hbm.at[:, pl.ds(128, 128)], xm, loc_sem.at[0])
    keep = pltpu.make_async_copy(
        x_hbm.at[rows(me["y"] * 1024, 1024), pl.ds(0, 128)], ry.at[me["y"]], loc_sem.at[1]
    )
    load.start()
    keep.start()

    barrier = pltpu.get_barrier_semaphore()

    for axis in "yxz":
        for dist in (1, 2, 3):
            to = moved(me, **{axis: (me[axis] + dist) % 4})
            pl.semaphore_signal(barrier, inc=1, device_id=to, device_id_type=MESH)
    pl.semaphore_signal(barrier, inc=1, device_id=other, device_id_type=MESH)

    had[...] = hadamard(BLK)
    tile[...] = jnp.zeros_like(tile)
    tile[pl.ds(0, 128)] = idx[pl.ds(0, 128)]
    tile[pl.ds(128, 128)] = idx[pl.ds(128, 128)] ^ 2048
    tile[pl.ds(256, 128)] = idx[pl.ds(128, 128)]

    def split(v):
        hi = v.astype(jnp.bfloat16)
        return hi, (v - hi.astype(jnp.float32)).astype(jnp.bfloat16)

    def times(left, v):
        out = jnp.dot(left, jnp.concatenate(split(v), axis=1), preferred_element_type=jnp.float32)
        return out[:, :128] + out[:, 128:]

    def panel1(i, _):
        def block(at):
            left = had[...] * sg[pl.ds(at, 1), :].astype(jnp.float32)
            return times(left.astype(jnp.bfloat16), xm[rows(at * BLK, BLK), :])

        lo, hi = block(i), block(i + 16)
        place = rows(i * BLK, BLK)
        a[0, place, :] = jnp.where(lane, lo, pltpu.roll(hi, HALF, 1))
        a[1, place, :] = jnp.where(lane, pltpu.roll(lo, HALF, 1), hi)
        return 0

    pl.semaphore_wait(barrier, 10)

    def out_y(k, dist):
        at = (me["y"] + dist) % 4
        if k == 4:
            src, dst = sg.at[rows(at * 8, 8), :], sy.at[rows(me["y"] * 8, 8), :]
        else:
            src = x_hbm.at[rows(at * 1024 + k * 256, 256), pl.ds(0, 128)]
            dst = ry.at[me["y"], pl.ds(k * 256, 256), :]
        return remote(src, dst, y_s.at[k], y_r.at[k], moved(me, y=at))

    def all_out_y(k):
        if k == 4:
            return remote(sg.at[pl.ds(0, 24), :], sy.at[pl.ds(0, 24), :], y_s.at[k], y_r.at[k], other)
        return remote(
            x_hbm.at[pl.ds(0, 768), pl.ds(0, 128)], ry.at[0, pl.ds(0, 768), :], y_s.at[k], y_r.at[k], other
        )

    def back_y(k, dist):
        at = (me["y"] + dist) % 4
        return remote(
            cy.at[at, pl.ds(k * 256, 256), :], dy.at[rows(me["y"] * 1024 + k * 256, 256), :],
            y_s.at[5], y_r.at[5], moved(me, y=at),
        )

    def all_back_y():
        return remote(cy.at[pl.ds(0, 3)], ro.at[pl.ds(0, 3)], y_s.at[5], y_r.at[5], other)

    def core_y(k):
        i = 2 + k
        if k == 4:
            return remote(sy, syo, core_s.at[i], core_r.at[i], other)
        place = pl.ds(k * 256, 256)
        return remote(ry.at[:, place, :], ro.at[:, place, :], core_s.at[i], core_r.at[i], other)

    def line(buf, axis, n, dist):
        to = moved(me, **{axis: (me[axis] + dist) % 4})
        return remote(tile, buf.at[rows(me[axis] * 1024, 1024)], ix_s.at[n], ix_r.at[n], to)

    def all_line(buf, n):
        return remote(lines[1 - n][0].at[pl.ds(0, 3072)], buf.at[pl.ds(0, 3072)], ix_s.at[n], ix_r.at[n], other)

    def plane(src, buf, axis, n, dist):
        to = moved(me, **{axis: (me[axis] + dist) % 4})
        return remote(src, buf.at[rows(me[axis] * 4096, 4096)], ix_s.at[2 + n], ix_r.at[2 + n], to)

    def all_plane(buf, n):
        some = pl.ds(0, 12288)
        return remote(planes[(n + 1) % 3][1].at[some], buf.at[some], ix_s.at[2 + n], ix_r.at[2 + n], other)

    lines = ((ly, "y", 0), (lz, "z", 1))
    planes = ((ly, pzy, "z", 0), (ly, pxy, "x", 1), (lz, pxz, "x", 2))

    def exchange(stage, part, dist):
        axis = PARTS[part][max(stage - 1, 0)]
        at = (me[axis] + dist) % 4
        size = 128 if stage == 3 else 512
        i = stage * 4 + part
        src = (a, c, e, g)[stage].at[part // 2 if stage < 2 else part, rows(at * size, size), :]
        mine = rows(me[axis] * size, size)
        if stage == 1:
            dst = done[part].at[mine, :]
        else:
            dst = (b, None, f, h)[stage].at[part // 2 if stage < 2 else part, mine, :]
        return remote(src, dst, st_s.at[i], st_r.at[i], moved(me, **{axis: at}))

    def all_three(stage, part):
        n, i = part // 2 if stage < 2 else part, stage * 4 + part
        three = pl.ds(0, 384 if stage == 3 else 1536)
        dst = done[part].at[three, :] if stage == 1 else (b, None, f, h)[stage].at[n, three, :]
        return remote((a, c, e, g)[stage].at[n, three, :], dst, st_s.at[i], st_r.at[i], other)

    def send(stage, part):
        for dist in FAR:
            exchange(stage, part, dist).start()

    def arrive(stage, part):
        all_three(stage, part).wait_recv()

    def own(axis, size):
        return rows(me[axis] * size, size)

    def core_b(part):
        n = part // 2
        return remote(b.at[n], bo.at[n], core_s.at[n], core_r.at[n], other)

    for dist in FAR:
        out_y(4, dist).start()
    for buf, axis, n in lines:
        for dist in (1, 2, 3):
            line(buf, axis, n, dist).start()
    for dist in FAR:
        out_y(0, dist).start()
    load.wait()
    lax.fori_loop(0, 16, panel1, 0)
    for part in (1, 3):
        send(0, part)
        b[part // 2, own(PARTS[part][0], 512), :] = a[part // 2, own(PARTS[part][0], 512), :]
    for k in range(1, 4):
        for dist in FAR:
            out_y(k, dist).start()
    for buf, axis, n in lines:
        buf[rows(me[axis] * 1024, 1024)] = tile[...]

    sign = (1 - 2 * me["c"]).astype(jnp.float32)

    def mixed(s0, s1, x0, x1):
        hm = had[...]
        left = jnp.concatenate(
            [hm * (s0.astype(jnp.float32) * sign), hm * s1.astype(jnp.float32)], axis=1
        ).astype(jnp.bfloat16)
        return times(left, jnp.concatenate([x0, x1], axis=0))

    def four(v):
        s, t, u, w = v[0] + v[1], v[0] - v[1], v[2] + v[3], v[2] - v[3]
        return s + u, t + w, s - u, t - w

    def panel0(k):
        def step(n, _):
            at = k * 2 + n
            place = rows(at * BLK, BLK)
            v = [
                mixed(sy[pl.ds(q * 8 + at, 1), :], syo[pl.ds(q * 8 + at, 1), :], ry[q, place, :], ro[q, place, :])
                for q in range(4)
            ]
            for q, out in enumerate(four(v)):
                cy[q, place, :] = out
            return 0

        lax.fori_loop(0, 2, step, 0)
        for dist in FAR:
            back_y(k, dist).start()
        dy[rows(me["y"] * 1024 + k * 256, 256), :] = cy[me["y"], pl.ds(k * 256, 256), :]

    def across(k):
        all_out_y(k).wait_recv()
        core_y(k).start()

    def across_b(part):
        arrive(0, part)
        core_b(part).start()

    def whole(part):
        n, axis = part // 2, PARTS[part][0]
        core_b(part).wait_recv()

        def step(i, _):
            places = [rows(q * 512 + i * 32, 32) for q in range(4)]
            for place, out in zip(places, four([b[n, p, :] * sign + bo[n, p, :] for p in places])):
                c[n, place, :] = out
            return 0

        lax.fori_loop(0, 16, step, 0)
        send(1, part)
        done[part][own(axis, 512), :] = c[n, own(axis, 512), :]

    def gather(part, m, dst):
        table, src = {1: szy, 3: sxy}[part], done[part]

        def some(i, _):
            base = (m * 4 + i // 2) * 1024 + (i % 2) * 64
            for u in range(64):
                lo = src[pl.ds(table[base + u], 1), :]
                hi = src[pl.ds(table[base + 128 + u], 1), :]
                dst[part, pl.ds(m * 512 + i * 64 + u, 1), :] = jnp.where(lane, lo, hi)
            return 0

        lax.fori_loop(0, 8, some, 0)

    def turned(part):
        arrive(1, part)

        def turn(i, _):
            done[part][rows(2048 + i * 64, 64), :] = pltpu.roll(done[part][rows(i * 64, 64), :], HALF, 1)
            return 0

        lax.fori_loop(0, 32, turn, 0)

    def pruned(part, dist):
        axis = PARTS[part][1]
        gather(part, (me[axis] + dist) % 4, e if dist else f)
        if dist:
            exchange(2, part, dist).start()

    def far(n):
        return jnp.where(n == 0, 2, jnp.where(n == 1, 1, jnp.where(n == 2, 3, 0)))

    def cells(xs, zs):
        def cell(n, _):
            x = (me["x"] + far(xs[0] + n if len(xs) > 1 else xs[0])) % 4
            z = (me["z"] + far(zs[0] + n if len(zs) > 1 else zs[0])) % 4
            base = (x * 4 + z) * 1024
            table = sxz

            def some(i, _):
                for u in range(32):
                    r[pl.ds(i * 32 + u, 1), :] = dy[pl.ds(table[base + i * 32 + u], 1), :]
                    r[pl.ds(128 + i * 32 + u, 1), :] = dy[pl.ds(table[base + 256 + i * 32 + u], 1), :]
                return 0

            lax.fori_loop(0, 4, some, 0)
            lo, hi = r[pl.ds(0, 128), :], r[pl.ds(128, 128), :]
            e[0, rows(x * 512 + z * 128, 128), :] = jnp.where(lane, lo, pltpu.roll(hi, HALF, 1))
            e[2, rows(z * 512 + x * 128, 128), :] = jnp.where(lane, pltpu.roll(lo, HALF, 1), hi)
            return 0

        lax.fori_loop(0, max(len(xs), len(zs)), cell, 0)

    def pruned_y():
        all_back_y().wait_recv()
        for n, dist in enumerate(FAR):
            cells((n,), range(n, 4))
            exchange(2, 0, dist).start()
            cells(range(n + 1, 4), (n,))
            exchange(2, 2, dist).start()
        cells((3,), (3,))
        for part in (0, 2):
            f[part, own(PARTS[part][1], 512), :] = e[part, own(PARTS[part][1], 512), :]

    def add_up(part, src, size, axis):
        signs = [sign4(me[axis], jnp.int32(q)) for q in range(4)]

        def at(start, count):
            total = src[part, pl.ds(start, count), :]
            for q in range(1, 4):
                total = total + signs[q] * src[part, rows(q * size + start, count), :]
            return total

        return at

    def last(part):
        axis = PARTS[part][2]
        arrive(2, part)
        sums = add_up(part, f, 512, PARTS[part][1])

        def step(i, _):
            start = pl.multiple_of(i * 32, 32)
            g[part, pl.ds(start, 32), :] = sums(start, 32)
            return 0

        lax.fori_loop(0, 16, step, 0)
        send(3, part)
        h[part, own(axis, 128), :] = g[part, own(axis, 128), :]

    def final(part):
        arrive(3, part)
        return add_up(part, h, 128, PARTS[part][2])(0, 128)

    keep.wait()
    all_out_y(4).wait_recv()
    sy[own("y", 8), :] = sg[own("y", 8), :]
    core_y(4).start()
    across(0)
    for buf, axis, n in lines:
        all_line(buf, n).wait_recv()
    for src, buf, axis, n in planes:
        for dist in (1, 2, 3):
            plane(src, buf, axis, n, dist).start()
        buf[rows(me[axis] * 4096, 4096)] = src[...]
    core_y(4).wait_recv()
    core_y(0).wait_recv()
    panel0(0)
    across(1)
    across_b(1)
    across_b(3)
    core_y(1).wait_recv()
    panel0(1)
    whole(1)
    whole(3)
    across(2)
    core_y(2).wait_recv()
    panel0(2)

    def to_smem(i):
        return pltpu.make_async_copy(planes[i][1], (szy, sxy, sxz)[i], sm_sem.at[i])

    for i, (src, buf, axis, n) in enumerate(planes):
        all_plane(buf, n).wait_recv()
        to_smem(i).start()
    across(3)
    core_y(3).wait_recv()
    panel0(3)
    for i in range(3):
        to_smem(i).wait()
    turned(1)
    pruned(1, 2)
    turned(3)
    pruned(3, 2)
    pruned(1, 1)
    pruned(3, 1)
    pruned(1, 3)
    pruned(3, 3)
    pruned(1, 0)
    pruned(3, 0)
    pruned_y()
    scale = 1.0 / (128 * BLK) ** 0.5
    slot = lax.broadcasted_iota(jnp.int32, (128, 1), 0)
    count = cnt[0]

    def finish(panel, lower, upper):
        p0, p1 = final(lower), final(upper)
        cols = pl.ds(panel * 128, 128)
        lo = jnp.where(lane, p0, pltpu.roll(p1, HALF, 1)) * scale
        hi = jnp.where(lane, pltpu.roll(p0, HALF, 1), p1) * scale
        sk_out[pl.ds(0, 128), cols] = jnp.where(slot < count, lo, 0.0)
        sk_out[pl.ds(128, 128), cols] = jnp.where(slot + 128 < count, hi, 0.0)
        return jnp.concatenate(split(sk_out[:, cols]), axis=1)

    here = me["y"] * 4 + me["z"]

    def gram(p, q):
        out = lax.dot_general(p, q, (((0,), (0,)), ((), ())), preferred_element_type=jnp.float32)
        out = out[:128] + out[128:]
        return [out[:, i : i + 128] + out[:, i + 128 : i + 256] for i in range(0, out.shape[1], 256)]

    def piece(dx, o):
        to = {"y": (me["y"] + o // 4) % 4, "z": (me["z"] + o % 4) % 4, "x": (me["x"] + dx) % 4}
        src = to["x"] * 128 + (to["y"] * 4 + to["z"]) * 8
        dst = (here * 4 + me["x"]) * 8
        return remote(gp.at[rows(src, 8), :], rb.at[rows(dst, 8), :], rs_s.at[0], rs_r.at[0], moved(me, **to))

    def scatter(n):
        dx = (n - me["x"] + 4) % 4
        for o in range(1, 16):
            piece(dx, o).start()

        @pl.when(dx != 0)
        def _():
            piece(dx, 0).start()

    def all_pieces():
        most = pl.ds(0, 63 * 8)
        return remote(gp.at[most, :], rb.at[most, :], rs_s.at[0], rs_r.at[0], other)

    last(1)
    last(3)
    for k in range(5):
        core_y(k).wait_send()
        all_out_y(k).wait_send()
    all_back_y().wait_send()
    for buf, axis, n in lines:
        all_line(buf, n).wait_send()
    for src, buf, axis, n in planes:
        all_plane(buf, n).wait_send()
    for part in (1, 3):
        core_b(part).wait_send()
        for stage in range(4):
            all_three(stage, part).wait_send()
    last(0)
    last(2)
    sk1 = finish(1, 1, 3)
    gp[pl.ds(384, 128), :] = gram(sk1, sk1)[0]
    scatter(3)
    sk0 = finish(0, 0, 2)
    first, second = gram(sk0, jnp.concatenate([sk0, sk1], axis=1))
    gp[pl.ds(0, 128), :] = first
    scatter(0)
    gp[pl.ds(128, 128), :] = second
    scatter(1)
    gp[pl.ds(256, 128), :] = second.T
    scatter(2)
    rb[rows((here * 4 + me["x"]) * 8, 8), :] = gp[rows(me["x"] * 128 + here * 8, 8), :]
    for stage in (2, 3):
        for part in (0, 2):
            all_three(stage, part).wait_send()
    all_pieces().wait_recv()
    mine = rows(me["c"] * 128 + here * 8, 8)
    ob[mine, :] = rb[...].reshape(64, 8, 128).sum(0) * (1.0 / (128 * 256))

    def share(o):
        to = {"c": (me["c"] + o // 16) % 2, "y": (me["y"] + o // 4 % 4) % 4, "z": (me["z"] + o % 4) % 4}
        return remote(ob.at[mine, :], ob.at[mine, :], ag_s.at[0], ag_r.at[0], moved(me, **to))

    for o in range(1, 32):
        share(o).start()
    all_pieces().wait_send()
    most = pl.ds(0, 31 * 8)
    shares = remote(rb.at[most, :], ob.at[most, :], ag_s.at[0], ag_r.at[0], other)
    shares.wait_send()
    shares.wait_recv()
    gr_out[...] = ob[pl.ds(0, 128), :] + ob[pl.ds(128, 128), :]


def hand_on(a, b, to_a, to_b):
    to_a[...] = a[...]
    to_b[...] = b[...]


def local(matrix, signs, indices, counts):
    f32, i32 = jnp.float32, jnp.int32
    vmem, smem, dma = pltpu.VMEM, pltpu.SMEM, pltpu.SemaphoreType.DMA
    in_vmem = pl.BlockSpec(memory_space=vmem)
    sketch, gram = pl.pallas_call(
        kernel,
        name="sketch_gram",
        out_shape=(jax.ShapeDtypeStruct((256, 256), f32), jax.ShapeDtypeStruct((128, 128), f32)),
        in_specs=[pl.BlockSpec(memory_space=pl.ANY), in_vmem, in_vmem, pl.BlockSpec(memory_space=smem)],
        out_specs=(in_vmem, in_vmem),
        scratch_shapes=[
            vmem((4096, 128), f32), vmem((2, 2048, 128), f32), vmem((128, 128), f32),
            vmem((4, 1024, 128), f32), vmem((4, 1024, 128), f32), vmem((32, 128), i32), vmem((32, 128), i32),
            vmem((4, 1024, 128), f32), vmem((4096, 128), f32), vmem((256, 128), f32),
            vmem((2, 2048, 128), f32), vmem((2, 2048, 128), f32), vmem((2, 2048, 128), f32),
            vmem((4096, 128), f32), vmem((4096, 128), f32),
            vmem((4, 2048, 128), f32), vmem((4, 2048, 128), f32),
            vmem((4, 512, 128), f32), vmem((4, 512, 128), f32),
            vmem((1024,), i32), vmem((4096,), i32), vmem((4096,), i32),
            vmem((16384,), i32), vmem((16384,), i32), vmem((16384,), i32),
            smem((16384,), i32), smem((16384,), i32), smem((16384,), i32),
            vmem((512, 128), f32), vmem((512, 128), f32), vmem((256, 128), f32),
            dma((2,)), dma((7,)), dma((7,)), dma((6,)), dma((6,)), dma((16,)), dma((16,)),
            dma((5,)), dma((5,)), dma((3,)), dma((1,)), dma((1,)), dma((1,)), dma((1,)),
        ],
        compiler_params=pltpu.CompilerParams(
            collective_id=0, has_side_effects=True, vmem_limit_bytes=56 * 2**20
        ),
    )(matrix, signs.reshape(32, 128), indices, counts)
    sketch, gram = pl.pallas_call(
        hand_on,
        name="hand_on",
        out_shape=(jax.ShapeDtypeStruct((256, 256), f32), jax.ShapeDtypeStruct((128, 128), f32)),
        in_specs=[in_vmem] * 2,
        out_specs=(in_vmem,) * 2,
    )(sketch, gram)
    return sketch, gram[None]


def solution(mesh):
    in_specs = (P(("rx", "ry"), None), P(("rx", "ry")), P(("rx", "ry")), P(("rx", "ry")))
    out_specs = (P(("rx", "ry"), None), P("ry", None, None))
    return jax.shard_map(local, mesh=mesh, in_specs=in_specs, out_specs=out_specs, check_vma=False)
```

```python
import functools

import jax
import jax.numpy as jnp
from jax import lax
from jax.experimental import pallas as pl
from jax.experimental.pallas import tpu as pltpu
from jax.sharding import PartitionSpec as P

MESH = pl.DeviceIdType.MESH
BLK = 128
HALF = 64
FAR = (2, 1, 3)
PARTS = (("y", "x", "z"), ("x", "z", "y"), ("y", "z", "x"), ("z", "x", "y"))


def coords():
    rx = lax.axis_index("rx")
    return {"y": rx // 8, "z": (rx // 2) % 4, "c": rx % 2, "x": lax.axis_index("ry")}


def device(at):
    return ((at["y"] * 4 + at["z"]) * 2 + at["c"], at["x"])


def moved(at, **to):
    return device({**at, **to})


def sign4(a, b):
    odd = (a % 2) * (b % 2) + (a // 2) * (b // 2)
    return (1 - 2 * (odd % 2)).astype(jnp.float32)


def hadamard(n):
    both = lax.broadcasted_iota(jnp.int32, (n, n), 0) & lax.broadcasted_iota(jnp.int32, (n, n), 1)
    both = both ^ (both >> 4)
    both = both ^ (both >> 2)
    both = both ^ (both >> 1)
    return (1 - 2 * (both & 1)).astype(jnp.float32)


def kernel(
    x_hbm, sg, idx, cnt, sk_out, gr_out,
    xm, bo, had, ry, ro, sy, syo, cy, dy, r, a, b, c, d1, d3, e, f, g, h,
    tile, ly, lz, pzy, pxy, pxz, szy, sxy, sxz, gp, rb, co, ob,
    loc_sem, core_s, core_r, y_s, y_r, st_s, st_r, ix_s, ix_r, sm_sem, rs_s, rs_r, ag_s, ag_r,
):
    me = coords()
    done = {1: d1, 3: d3}
    lane = lax.broadcasted_iota(jnp.int32, (1, 128), 1) < HALF
    other = moved(me, c=1 - me["c"])

    def rows(start, size):
        return pl.ds(pl.multiple_of(start, 1024 if size % 1024 == 0 else 8), size)

    def remote(src, dst, send, recv, to):
        return pltpu.make_async_remote_copy(
            src_ref=src, dst_ref=dst, send_sem=send, recv_sem=recv, device_id=to, device_id_type=MESH
        )

    load = pltpu.make_async_copy(x_hbm.at[:, pl.ds(128, 128)], xm, loc_sem.at[0])
    keep = pltpu.make_async_copy(
        x_hbm.at[rows(me["y"] * 1024, 1024), pl.ds(0, 128)], ry.at[me["y"]], loc_sem.at[1]
    )
    load.start()
    keep.start()

    barrier = pltpu.get_barrier_semaphore()

    for axis in "yxz":
        for dist in (1, 2, 3):
            to = moved(me, **{axis: (me[axis] + dist) % 4})
            pl.semaphore_signal(barrier, inc=1, device_id=to, device_id_type=MESH)
    pl.semaphore_signal(barrier, inc=1, device_id=other, device_id_type=MESH)

    had[...] = hadamard(BLK)
    tile[...] = jnp.zeros_like(tile)
    tile[pl.ds(0, 128)] = idx[pl.ds(0, 128)]
    tile[pl.ds(128, 128)] = idx[pl.ds(128, 128)] ^ 2048
    tile[pl.ds(256, 128)] = idx[pl.ds(128, 128)]

    def split(v):
        hi = v.astype(jnp.bfloat16)
        return hi, (v - hi.astype(jnp.float32)).astype(jnp.bfloat16)

    def times(left, v):
        out = jnp.dot(left, jnp.concatenate(split(v), axis=1), preferred_element_type=jnp.float32)
        return out[:, :128] + out[:, 128:]

    def panel1(i, _):
        def block(at):
            left = had[...] * sg[pl.ds(at, 1), :].astype(jnp.float32)
            return times(left.astype(jnp.bfloat16), xm[rows(at * BLK, BLK), :])

        lo, hi = block(i), block(i + 16)
        place = rows(i * BLK, BLK)
        a[0, place, :] = jnp.where(lane, lo, pltpu.roll(hi, HALF, 1))
        a[1, place, :] = jnp.where(lane, pltpu.roll(lo, HALF, 1), hi)
        return 0

    pl.semaphore_wait(barrier, 10)

    def out_y(k, dist):
        at = (me["y"] + dist) % 4
        if k == 4:
            src, dst = sg.at[rows(at * 8, 8), :], sy.at[rows(me["y"] * 8, 8), :]
        else:
            src = x_hbm.at[rows(at * 1024 + k * 256, 256), pl.ds(0, 128)]
            dst = ry.at[me["y"], pl.ds(k * 256, 256), :]
        return remote(src, dst, y_s.at[k], y_r.at[k], moved(me, y=at))

    def all_out_y(k):
        if k == 4:
            return remote(sg.at[pl.ds(0, 24), :], sy.at[pl.ds(0, 24), :], y_s.at[k], y_r.at[k], other)
        return remote(
            x_hbm.at[pl.ds(0, 768), pl.ds(0, 128)], ry.at[0, pl.ds(0, 768), :], y_s.at[k], y_r.at[k], other
        )

    def back_y(k, dist):
        at = (me["y"] + dist) % 4
        return remote(
            cy.at[at, pl.ds(k * 256, 256), :], dy.at[rows(me["y"] * 1024 + k * 256, 256), :],
            y_s.at[5], y_r.at[5], moved(me, y=at),
        )

    def all_back_y():
        return remote(cy.at[pl.ds(0, 3)], ro.at[pl.ds(0, 3)], y_s.at[5], y_r.at[5], other)

    def core_y(k):
        i = 2 + k
        if k == 4:
            return remote(sy, syo, core_s.at[i], core_r.at[i], other)
        place = pl.ds(k * 256, 256)
        return remote(ry.at[:, place, :], ro.at[:, place, :], core_s.at[i], core_r.at[i], other)

    def line(buf, axis, n, dist):
        to = moved(me, **{axis: (me[axis] + dist) % 4})
        return remote(tile, buf.at[rows(me[axis] * 1024, 1024)], ix_s.at[n], ix_r.at[n], to)

    def all_line(buf, n):
        return remote(lines[1 - n][0].at[pl.ds(0, 3072)], buf.at[pl.ds(0, 3072)], ix_s.at[n], ix_r.at[n], other)

    def plane(src, buf, axis, n, dist):
        to = moved(me, **{axis: (me[axis] + dist) % 4})
        return remote(src, buf.at[rows(me[axis] * 4096, 4096)], ix_s.at[2 + n], ix_r.at[2 + n], to)

    def all_plane(buf, n):
        some = pl.ds(0, 12288)
        return remote(planes[(n + 1) % 3][1].at[some], buf.at[some], ix_s.at[2 + n], ix_r.at[2 + n], other)

    lines = ((ly, "y", 0), (lz, "z", 1))
    planes = ((ly, pzy, "z", 0), (ly, pxy, "x", 1), (lz, pxz, "x", 2))

    def exchange(stage, part, dist):
        axis = PARTS[part][max(stage - 1, 0)]
        at = (me[axis] + dist) % 4
        size = 128 if stage == 3 else 512
        i = stage * 4 + part
        src = (a, c, e, g)[stage].at[part // 2 if stage < 2 else part, rows(at * size, size), :]
        mine = rows(me[axis] * size, size)
        if stage == 1:
            dst = done[part].at[mine, :]
        else:
            dst = (b, None, f, h)[stage].at[part // 2 if stage < 2 else part, mine, :]
        return remote(src, dst, st_s.at[i], st_r.at[i], moved(me, **{axis: at}))

    def all_three(stage, part):
        n, i = part // 2 if stage < 2 else part, stage * 4 + part
        three = pl.ds(0, 384 if stage == 3 else 1536)
        dst = done[part].at[three, :] if stage == 1 else (b, None, f, h)[stage].at[n, three, :]
        return remote((a, c, e, g)[stage].at[n, three, :], dst, st_s.at[i], st_r.at[i], other)

    def send(stage, part):
        for dist in FAR:
            exchange(stage, part, dist).start()

    def arrive(stage, part):
        all_three(stage, part).wait_recv()

    def own(axis, size):
        return rows(me[axis] * size, size)

    def core_b(part):
        n = part // 2
        return remote(b.at[n], bo.at[n], core_s.at[n], core_r.at[n], other)

    for dist in FAR:
        out_y(4, dist).start()
    for buf, axis, n in lines:
        for dist in (1, 2, 3):
            line(buf, axis, n, dist).start()
    for dist in FAR:
        out_y(0, dist).start()
    load.wait()
    lax.fori_loop(0, 16, panel1, 0)
    for part in (1, 3):
        send(0, part)
        b[part // 2, own(PARTS[part][0], 512), :] = a[part // 2, own(PARTS[part][0], 512), :]
    for k in range(1, 4):
        for dist in FAR:
            out_y(k, dist).start()
    for buf, axis, n in lines:
        buf[rows(me[axis] * 1024, 1024)] = tile[...]

    sign = (1 - 2 * me["c"]).astype(jnp.float32)

    def mixed(s0, s1, x0, x1):
        hm = had[...]
        left = jnp.concatenate(
            [hm * (s0.astype(jnp.float32) * sign), hm * s1.astype(jnp.float32)], axis=1
        ).astype(jnp.bfloat16)
        return times(left, jnp.concatenate([x0, x1], axis=0))

    def four(v):
        s, t, u, w = v[0] + v[1], v[0] - v[1], v[2] + v[3], v[2] - v[3]
        return s + u, t + w, s - u, t - w

    def panel0(k):
        def step(n, _):
            at = k * 2 + n
            place = rows(at * BLK, BLK)
            v = [
                mixed(sy[pl.ds(q * 8 + at, 1), :], syo[pl.ds(q * 8 + at, 1), :], ry[q, place, :], ro[q, place, :])
                for q in range(4)
            ]
            for q, out in enumerate(four(v)):
                cy[q, place, :] = out
            return 0

        lax.fori_loop(0, 2, step, 0)
        for dist in FAR:
            back_y(k, dist).start()
        dy[rows(me["y"] * 1024 + k * 256, 256), :] = cy[me["y"], pl.ds(k * 256, 256), :]

    def across(k):
        all_out_y(k).wait_recv()
        core_y(k).start()

    def across_b(part):
        arrive(0, part)
        core_b(part).start()

    def whole(part):
        n, axis = part // 2, PARTS[part][0]
        core_b(part).wait_recv()

        def step(i, _):
            places = [rows(q * 512 + i * 32, 32) for q in range(4)]
            for place, out in zip(places, four([b[n, p, :] * sign + bo[n, p, :] for p in places])):
                c[n, place, :] = out
            return 0

        lax.fori_loop(0, 16, step, 0)
        send(1, part)
        done[part][own(axis, 512), :] = c[n, own(axis, 512), :]

    def gather(part, m, dst):
        table, src = {1: szy, 3: sxy}[part], done[part]

        def some(i, _):
            base = (m * 4 + i // 2) * 1024 + (i % 2) * 64
            for u in range(64):
                lo = src[pl.ds(table[base + u], 1), :]
                hi = src[pl.ds(table[base + 128 + u], 1), :]
                dst[part, pl.ds(m * 512 + i * 64 + u, 1), :] = jnp.where(lane, lo, hi)
            return 0

        lax.fori_loop(0, 8, some, 0)

    def turned(part):
        arrive(1, part)

        def turn(i, _):
            done[part][rows(2048 + i * 64, 64), :] = pltpu.roll(done[part][rows(i * 64, 64), :], HALF, 1)
            return 0

        lax.fori_loop(0, 32, turn, 0)

    def pruned(part, dist):
        axis = PARTS[part][1]
        gather(part, (me[axis] + dist) % 4, e if dist else f)
        if dist:
            exchange(2, part, dist).start()

    def far(n):
        return jnp.where(n == 0, 2, jnp.where(n == 1, 1, jnp.where(n == 2, 3, 0)))

    def cells(xs, zs):
        def cell(n, _):
            x = (me["x"] + far(xs[0] + n if len(xs) > 1 else xs[0])) % 4
            z = (me["z"] + far(zs[0] + n if len(zs) > 1 else zs[0])) % 4
            base = (x * 4 + z) * 1024
            table = sxz

            def some(i, _):
                for u in range(32):
                    r[pl.ds(i * 32 + u, 1), :] = dy[pl.ds(table[base + i * 32 + u], 1), :]
                    r[pl.ds(128 + i * 32 + u, 1), :] = dy[pl.ds(table[base + 256 + i * 32 + u], 1), :]
                return 0

            lax.fori_loop(0, 4, some, 0)
            lo, hi = r[pl.ds(0, 128), :], r[pl.ds(128, 128), :]
            e[0, rows(x * 512 + z * 128, 128), :] = jnp.where(lane, lo, pltpu.roll(hi, HALF, 1))
            e[2, rows(z * 512 + x * 128, 128), :] = jnp.where(lane, pltpu.roll(lo, HALF, 1), hi)
            return 0

        lax.fori_loop(0, max(len(xs), len(zs)), cell, 0)

    def pruned_y():
        all_back_y().wait_recv()
        for n, dist in enumerate(FAR):
            cells((n,), range(n, 4))
            exchange(2, 0, dist).start()
            cells(range(n + 1, 4), (n,))
            exchange(2, 2, dist).start()
        cells((3,), (3,))
        for part in (0, 2):
            f[part, own(PARTS[part][1], 512), :] = e[part, own(PARTS[part][1], 512), :]

    def add_up(part, src, size, axis):
        signs = [sign4(me[axis], jnp.int32(q)) for q in range(4)]

        def at(start, count):
            total = src[part, pl.ds(start, count), :]
            for q in range(1, 4):
                total = total + signs[q] * src[part, rows(q * size + start, count), :]
            return total

        return at

    def last(part):
        axis = PARTS[part][2]
        arrive(2, part)
        sums = add_up(part, f, 512, PARTS[part][1])

        def step(i, _):
            start = pl.multiple_of(i * 32, 32)
            g[part, pl.ds(start, 32), :] = sums(start, 32)
            return 0

        lax.fori_loop(0, 16, step, 0)
        send(3, part)
        h[part, own(axis, 128), :] = g[part, own(axis, 128), :]

    def final(part):
        arrive(3, part)
        return add_up(part, h, 128, PARTS[part][2])(0, 128)

    keep.wait()
    all_out_y(4).wait_recv()
    sy[own("y", 8), :] = sg[own("y", 8), :]
    core_y(4).start()
    across(0)
    for buf, axis, n in lines:
        all_line(buf, n).wait_recv()
    for src, buf, axis, n in planes:
        for dist in (1, 2, 3):
            plane(src, buf, axis, n, dist).start()
        buf[rows(me[axis] * 4096, 4096)] = src[...]
    core_y(4).wait_recv()
    core_y(0).wait_recv()
    panel0(0)
    across(1)
    across_b(1)
    across_b(3)
    core_y(1).wait_recv()
    panel0(1)
    whole(1)
    whole(3)
    across(2)
    core_y(2).wait_recv()
    panel0(2)

    def to_smem(i):
        return pltpu.make_async_copy(planes[i][1], (szy, sxy, sxz)[i], sm_sem.at[i])

    for i, (src, buf, axis, n) in enumerate(planes):
        all_plane(buf, n).wait_recv()
        to_smem(i).start()
    across(3)
    core_y(3).wait_recv()
    panel0(3)
    for i in range(3):
        to_smem(i).wait()
    turned(1)
    pruned(1, 2)
    turned(3)
    pruned(3, 2)
    pruned(1, 1)
    pruned(3, 1)
    pruned(1, 3)
    pruned(3, 3)
    pruned(1, 0)
    pruned(3, 0)
    pruned_y()
    scale = 1.0 / (128 * BLK) ** 0.5
    slot = lax.broadcasted_iota(jnp.int32, (128, 1), 0)
    count = cnt[0]

    def finish(panel, lower, upper):
        p0, p1 = final(lower), final(upper)
        cols = pl.ds(panel * 128, 128)
        lo = jnp.where(lane, p0, pltpu.roll(p1, HALF, 1)) * scale
        hi = jnp.where(lane, pltpu.roll(p0, HALF, 1), p1) * scale
        sk_out[pl.ds(0, 128), cols] = jnp.where(slot < count, lo, 0.0)
        sk_out[pl.ds(128, 128), cols] = jnp.where(slot + 128 < count, hi, 0.0)
        return jnp.concatenate(split(sk_out[:, cols]), axis=1)

    here = me["y"] * 4 + me["z"]

    def gram(p, q):
        out = lax.dot_general(p, q, (((0,), (0,)), ((), ())), preferred_element_type=jnp.float32)
        out = out[:128] + out[128:]
        return [out[:, i : i + 128] + out[:, i + 128 : i + 256] for i in range(0, out.shape[1], 256)]

    odd = me["z"] % 2
    nth = me["y"] * 2 + me["z"] // 2

    def piece(dx, o):
        to = {"y": (me["y"] + o // 2) % 4, "z": (me["z"] // 2 + o % 2) % 2 * 2, "x": (me["x"] + dx) % 4}
        src = to["x"] * 128 + (to["y"] * 2 + to["z"] // 2) * 16
        dst = (here * 4 + me["x"]) * 16
        return remote(gp.at[rows(src, 16), :], rb.at[rows(dst, 16), :], rs_s.at[0], rs_r.at[0], moved(me, **to))

    def scatter(n):
        dx = (n - me["x"] + 4) % 4
        for o in range(1, 8):
            piece(dx, o).start()

        @pl.when(dx + odd != 0)
        def _():
            piece(dx, 0).start()

    def pieces(count, of):
        most = pl.ds(0, count * 16)
        return remote(of.at[most, :], rb.at[most, :], rs_s.at[0], rs_r.at[0], other)

    last(1)
    last(3)
    for k in range(5):
        core_y(k).wait_send()
        all_out_y(k).wait_send()
    all_back_y().wait_send()
    for buf, axis, n in lines:
        all_line(buf, n).wait_send()
    for src, buf, axis, n in planes:
        all_plane(buf, n).wait_send()
    for part in (1, 3):
        core_b(part).wait_send()
        for stage in range(4):
            all_three(stage, part).wait_send()
    last(0)
    last(2)
    sk1 = finish(1, 1, 3)
    gp[pl.ds(384, 128), :] = gram(sk1, sk1)[0]
    scatter(3)
    sk0 = finish(0, 0, 2)
    first, second = gram(sk0, jnp.concatenate([sk0, sk1], axis=1))
    gp[pl.ds(0, 128), :] = first
    scatter(0)
    gp[pl.ds(128, 128), :] = second
    scatter(1)
    gp[pl.ds(256, 128), :] = second.T
    scatter(2)
    for stage in (2, 3):
        for part in (0, 2):
            all_three(stage, part).wait_send()
    mine = rows(nth * 16, 16)

    def share(o):
        to = {"y": (me["y"] + o // 4) % 4, "z": (me["z"] + o % 4) % 4}
        return remote(ob.at[mine, :], ob.at[mine, :], ag_s.at[0], ag_r.at[0], moved(me, **to))

    def shares(count):
        most = pl.ds(0, count * 16)
        return remote(rb.at[most, :], ob.at[most, :], ag_s.at[0], ag_r.at[0], other)

    @pl.when(odd == 0)
    def _():
        rb[rows((here * 4 + me["x"]) * 16, 16), :] = gp[rows(me["x"] * 128 + nth * 16, 16), :]
        pieces(63, rb).wait_recv()
        co[pl.ds(0, 16), :] = rb[...].reshape(64, 16, 128).sum(0) * (1.0 / (128 * 256))
        swap = remote(co.at[pl.ds(0, 16), :], co.at[pl.ds(16, 16), :], core_s.at[7], core_r.at[7], other)
        swap.start()
        swap.wait_recv()
        ob[mine, :] = co[pl.ds(0, 16), :] + co[pl.ds(16, 16), :]
        for o in range(1, 16):
            share(o).start()
        swap.wait_send()
        pieces(31, gp).wait_send()
        remote(rb.at[pl.ds(0, 240), :], rb.at[pl.ds(0, 240), :], ag_s.at[0], ag_r.at[0], other).wait_send()
        shares(7).wait_recv()

    @pl.when(odd != 0)
    def _():
        pieces(32, gp).wait_send()
        shares(8).wait_recv()

    gr_out[...] = ob[...]


def hand_on(a, b, to_a, to_b):
    to_a[...] = a[...]
    to_b[...] = b[...]


def local(matrix, signs, indices, counts):
    f32, i32 = jnp.float32, jnp.int32
    vmem, smem, dma = pltpu.VMEM, pltpu.SMEM, pltpu.SemaphoreType.DMA
    in_vmem = pl.BlockSpec(memory_space=vmem)
    sketch, gram = pl.pallas_call(
        kernel,
        name="sketch_gram",
        out_shape=(jax.ShapeDtypeStruct((256, 256), f32), jax.ShapeDtypeStruct((128, 128), f32)),
        in_specs=[pl.BlockSpec(memory_space=pl.ANY), in_vmem, in_vmem, pl.BlockSpec(memory_space=smem)],
        out_specs=(in_vmem, in_vmem),
        scratch_shapes=[
            vmem((4096, 128), f32), vmem((2, 2048, 128), f32), vmem((128, 128), f32),
            vmem((4, 1024, 128), f32), vmem((4, 1024, 128), f32), vmem((32, 128), i32), vmem((32, 128), i32),
            vmem((4, 1024, 128), f32), vmem((4096, 128), f32), vmem((256, 128), f32),
            vmem((2, 2048, 128), f32), vmem((2, 2048, 128), f32), vmem((2, 2048, 128), f32),
            vmem((4096, 128), f32), vmem((4096, 128), f32),
            vmem((4, 2048, 128), f32), vmem((4, 2048, 128), f32),
            vmem((4, 512, 128), f32), vmem((4, 512, 128), f32),
            vmem((1024,), i32), vmem((4096,), i32), vmem((4096,), i32),
            vmem((16384,), i32), vmem((16384,), i32), vmem((16384,), i32),
            smem((16384,), i32), smem((16384,), i32), smem((16384,), i32),
            vmem((512, 128), f32), vmem((1024, 128), f32), vmem((32, 128), f32), vmem((128, 128), f32),
            dma((2,)), dma((8,)), dma((8,)), dma((6,)), dma((6,)), dma((16,)), dma((16,)),
            dma((5,)), dma((5,)), dma((3,)), dma((1,)), dma((1,)), dma((1,)), dma((1,)),
        ],
        compiler_params=pltpu.CompilerParams(
            collective_id=0, has_side_effects=True, vmem_limit_bytes=56 * 2**20
        ),
    )(matrix, signs.reshape(32, 128), indices, counts)
    sketch, gram = pl.pallas_call(
        hand_on,
        name="hand_on",
        out_shape=(jax.ShapeDtypeStruct((256, 256), f32), jax.ShapeDtypeStruct((128, 128), f32)),
        in_specs=[in_vmem] * 2,
        out_specs=(in_vmem,) * 2,
    )(sketch, gram)
    return sketch, gram[None]


def solution(mesh):
    in_specs = (P(("rx", "ry"), None), P(("rx", "ry")), P(("rx", "ry")), P(("rx", "ry")))
    out_specs = (P(("rx", "ry"), None), P("ry", None, None))
    return jax.shard_map(local, mesh=mesh, in_specs=in_specs, out_specs=out_specs, check_vma=False)
```

```python
import functools

import jax
import jax.numpy as jnp
from jax import lax
from jax.experimental import pallas as pl
from jax.experimental.pallas import tpu as pltpu
from jax.sharding import PartitionSpec as P

MESH = pl.DeviceIdType.MESH
BLK = 128
HALF = 64
FAR = (2, 1, 3)
PARTS = (("y", "x", "z"), ("x", "z", "y"), ("y", "z", "x"), ("z", "x", "y"))


def coords():
    rx = lax.axis_index("rx")
    return {"y": rx // 8, "z": (rx // 2) % 4, "c": rx % 2, "x": lax.axis_index("ry")}


def device(at):
    return ((at["y"] * 4 + at["z"]) * 2 + at["c"], at["x"])


def moved(at, **to):
    return device({**at, **to})


def sign4(a, b):
    odd = (a % 2) * (b % 2) + (a // 2) * (b // 2)
    return (1 - 2 * (odd % 2)).astype(jnp.float32)


def hadamard(n):
    both = lax.broadcasted_iota(jnp.int32, (n, n), 0) & lax.broadcasted_iota(jnp.int32, (n, n), 1)
    both = both ^ (both >> 4)
    both = both ^ (both >> 2)
    both = both ^ (both >> 1)
    return (1 - 2 * (both & 1)).astype(jnp.float32)


def kernel(
    x_hbm, sg, idx, cnt, sk_out, gr_out,
    xm, bo, had, ry, ro, sy, syo, cy, dy, r, a, b, c, d1, d3, e, f, g, h,
    tile, ly, lz, pzy, pxy, pxz, szy, sxy, sxz, gp, rb, co, ob,
    loc_sem, core_s, core_r, y_s, y_r, st_s, st_r, ix_s, ix_r, sm_sem, rs_s, rs_r, ag_s, ag_r,
):
    me = coords()
    done = {1: d1, 3: d3}
    lane = lax.broadcasted_iota(jnp.int32, (1, 128), 1) < HALF
    other = moved(me, c=1 - me["c"])

    def rows(start, size):
        return pl.ds(pl.multiple_of(start, 1024 if size % 1024 == 0 else 8), size)

    def remote(src, dst, send, recv, to):
        return pltpu.make_async_remote_copy(
            src_ref=src, dst_ref=dst, send_sem=send, recv_sem=recv, device_id=to, device_id_type=MESH
        )

    load = pltpu.make_async_copy(x_hbm.at[:, pl.ds(128, 128)], xm, loc_sem.at[0])
    keep = pltpu.make_async_copy(
        x_hbm.at[rows(me["y"] * 1024, 1024), pl.ds(0, 128)], ry.at[me["y"]], loc_sem.at[1]
    )
    load.start()
    keep.start()

    barrier = pltpu.get_barrier_semaphore()

    for axis in "yxz":
        for dist in (1, 2, 3):
            to = moved(me, **{axis: (me[axis] + dist) % 4})
            pl.semaphore_signal(barrier, inc=1, device_id=to, device_id_type=MESH)
    pl.semaphore_signal(barrier, inc=1, device_id=other, device_id_type=MESH)

    had[...] = hadamard(BLK)
    tile[...] = jnp.zeros_like(tile)
    tile[pl.ds(0, 128)] = idx[pl.ds(0, 128)]
    tile[pl.ds(128, 128)] = idx[pl.ds(128, 128)] ^ 2048
    tile[pl.ds(256, 128)] = idx[pl.ds(128, 128)]

    def split(v):
        hi = v.astype(jnp.bfloat16)
        return hi, (v - hi.astype(jnp.float32)).astype(jnp.bfloat16)

    def times(left, v):
        out = jnp.dot(left, jnp.concatenate(split(v), axis=1), preferred_element_type=jnp.float32)
        return out[:, :128] + out[:, 128:]

    def panel1(i, _):
        def block(at):
            left = had[...] * sg[pl.ds(at, 1), :].astype(jnp.float32)
            return times(left.astype(jnp.bfloat16), xm[rows(at * BLK, BLK), :])

        lo, hi = block(i), block(i + 16)
        place = rows(i * BLK, BLK)
        a[0, place, :] = jnp.where(lane, lo, pltpu.roll(hi, HALF, 1))
        a[1, place, :] = jnp.where(lane, pltpu.roll(lo, HALF, 1), hi)
        return 0

    pl.semaphore_wait(barrier, 10)

    def out_y(k, dist):
        at = (me["y"] + dist) % 4
        if k == 4:
            src, dst = sg.at[rows(at * 8, 8), :], sy.at[rows(me["y"] * 8, 8), :]
        else:
            src = x_hbm.at[rows(at * 1024 + k * 256, 256), pl.ds(0, 128)]
            dst = ry.at[me["y"], pl.ds(k * 256, 256), :]
        return remote(src, dst, y_s.at[k], y_r.at[k], moved(me, y=at))

    def all_out_y(k):
        if k == 4:
            return remote(sg.at[pl.ds(0, 24), :], sy.at[pl.ds(0, 24), :], y_s.at[k], y_r.at[k], other)
        return remote(
            x_hbm.at[pl.ds(0, 768), pl.ds(0, 128)], ry.at[0, pl.ds(0, 768), :], y_s.at[k], y_r.at[k], other
        )

    def back_y(k, dist):
        at = (me["y"] + dist) % 4
        return remote(
            cy.at[at, pl.ds(k * 256, 256), :], dy.at[rows(me["y"] * 1024 + k * 256, 256), :],
            y_s.at[5], y_r.at[5], moved(me, y=at),
        )

    def all_back_y():
        return remote(cy.at[pl.ds(0, 3)], ro.at[pl.ds(0, 3)], y_s.at[5], y_r.at[5], other)

    def core_y(k):
        i = 2 + k
        if k == 4:
            return remote(sy, syo, core_s.at[i], core_r.at[i], other)
        place = pl.ds(k * 256, 256)
        return remote(ry.at[:, place, :], ro.at[:, place, :], core_s.at[i], core_r.at[i], other)

    def line(buf, axis, n, dist):
        to = moved(me, **{axis: (me[axis] + dist) % 4})
        return remote(tile, buf.at[rows(me[axis] * 1024, 1024)], ix_s.at[n], ix_r.at[n], to)

    def all_line(buf, n):
        return remote(lines[1 - n][0].at[pl.ds(0, 3072)], buf.at[pl.ds(0, 3072)], ix_s.at[n], ix_r.at[n], other)

    def plane(src, buf, axis, n, dist):
        to = moved(me, **{axis: (me[axis] + dist) % 4})
        return remote(src, buf.at[rows(me[axis] * 4096, 4096)], ix_s.at[2 + n], ix_r.at[2 + n], to)

    def all_plane(buf, n):
        some = pl.ds(0, 12288)
        return remote(planes[(n + 1) % 3][1].at[some], buf.at[some], ix_s.at[2 + n], ix_r.at[2 + n], other)

    lines = ((ly, "y", 0), (lz, "z", 1))
    planes = ((ly, pzy, "z", 0), (ly, pxy, "x", 1), (lz, pxz, "x", 2))

    def exchange(stage, part, dist):
        axis = PARTS[part][max(stage - 1, 0)]
        at = (me[axis] + dist) % 4
        size = 128 if stage == 3 else 512
        i = stage * 4 + part
        src = (a, c, e, g)[stage].at[part // 2 if stage < 2 else part, rows(at * size, size), :]
        mine = rows(me[axis] * size, size)
        if stage == 1:
            dst = done[part].at[mine, :]
        else:
            dst = (b, None, f, h)[stage].at[part // 2 if stage < 2 else part, mine, :]
        return remote(src, dst, st_s.at[i], st_r.at[i], moved(me, **{axis: at}))

    def all_three(stage, part):
        n, i = part // 2 if stage < 2 else part, stage * 4 + part
        three = pl.ds(0, 384 if stage == 3 else 1536)
        dst = done[part].at[three, :] if stage == 1 else (b, None, f, h)[stage].at[n, three, :]
        return remote((a, c, e, g)[stage].at[n, three, :], dst, st_s.at[i], st_r.at[i], other)

    def send(stage, part):
        for dist in FAR:
            exchange(stage, part, dist).start()

    def arrive(stage, part):
        all_three(stage, part).wait_recv()

    def own(axis, size):
        return rows(me[axis] * size, size)

    def core_b(part):
        n = part // 2
        return remote(b.at[n], bo.at[n], core_s.at[n], core_r.at[n], other)

    for dist in FAR:
        out_y(4, dist).start()
    for buf, axis, n in lines:
        for dist in (1, 2, 3):
            line(buf, axis, n, dist).start()
    for dist in FAR:
        out_y(0, dist).start()
    load.wait()
    lax.fori_loop(0, 16, panel1, 0)
    for part in (1, 3):
        send(0, part)
        b[part // 2, own(PARTS[part][0], 512), :] = a[part // 2, own(PARTS[part][0], 512), :]
    for k in range(1, 4):
        for dist in FAR:
            out_y(k, dist).start()
    for buf, axis, n in lines:
        buf[rows(me[axis] * 1024, 1024)] = tile[...]

    sign = (1 - 2 * me["c"]).astype(jnp.float32)

    def mixed(s0, s1, x0, x1):
        hm = had[...]
        left = jnp.concatenate(
            [hm * (s0.astype(jnp.float32) * sign), hm * s1.astype(jnp.float32)], axis=1
        ).astype(jnp.bfloat16)
        return times(left, jnp.concatenate([x0, x1], axis=0))

    def four(v):
        s, t, u, w = v[0] + v[1], v[0] - v[1], v[2] + v[3], v[2] - v[3]
        return s + u, t + w, s - u, t - w

    def panel0(k):
        def step(n, _):
            at = k * 2 + n
            place = rows(at * BLK, BLK)
            v = [
                mixed(sy[pl.ds(q * 8 + at, 1), :], syo[pl.ds(q * 8 + at, 1), :], ry[q, place, :], ro[q, place, :])
                for q in range(4)
            ]
            for q, out in enumerate(four(v)):
                cy[q, place, :] = out
            return 0

        lax.fori_loop(0, 2, step, 0)
        for dist in FAR:
            back_y(k, dist).start()
        dy[rows(me["y"] * 1024 + k * 256, 256), :] = cy[me["y"], pl.ds(k * 256, 256), :]

    def across(k):
        all_out_y(k).wait_recv()
        core_y(k).start()

    def across_b(part):
        arrive(0, part)
        core_b(part).start()

    def whole(part):
        n, axis = part // 2, PARTS[part][0]
        core_b(part).wait_recv()

        def step(i, _):
            places = [rows(q * 512 + i * 32, 32) for q in range(4)]
            for place, out in zip(places, four([b[n, p, :] * sign + bo[n, p, :] for p in places])):
                c[n, place, :] = out
            return 0

        lax.fori_loop(0, 16, step, 0)
        send(1, part)
        done[part][own(axis, 512), :] = c[n, own(axis, 512), :]

    def gather(part, m, dst):
        table, src = {1: szy, 3: sxy}[part], done[part]

        def some(i, _):
            base = (m * 4 + i // 2) * 1024 + (i % 2) * 64
            for u in range(64):
                lo = src[pl.ds(table[base + u], 1), :]
                hi = src[pl.ds(table[base + 128 + u], 1), :]
                dst[part, pl.ds(m * 512 + i * 64 + u, 1), :] = jnp.where(lane, lo, hi)
            return 0

        lax.fori_loop(0, 8, some, 0)

    def turned(part):
        arrive(1, part)

        def turn(i, _):
            done[part][rows(2048 + i * 64, 64), :] = pltpu.roll(done[part][rows(i * 64, 64), :], HALF, 1)
            return 0

        lax.fori_loop(0, 32, turn, 0)

    def pruned(part, dist):
        axis = PARTS[part][1]
        gather(part, (me[axis] + dist) % 4, e if dist else f)
        if dist:
            exchange(2, part, dist).start()

    def far(n):
        return jnp.where(n == 0, 2, jnp.where(n == 1, 1, jnp.where(n == 2, 3, 0)))

    def cells(xs, zs):
        def cell(n, _):
            x = (me["x"] + far(xs[0] + n if len(xs) > 1 else xs[0])) % 4
            z = (me["z"] + far(zs[0] + n if len(zs) > 1 else zs[0])) % 4
            base = (x * 4 + z) * 1024
            table = sxz

            def some(i, _):
                for u in range(32):
                    r[pl.ds(i * 32 + u, 1), :] = dy[pl.ds(table[base + i * 32 + u], 1), :]
                    r[pl.ds(128 + i * 32 + u, 1), :] = dy[pl.ds(table[base + 256 + i * 32 + u], 1), :]
                return 0

            lax.fori_loop(0, 4, some, 0)
            lo, hi = r[pl.ds(0, 128), :], r[pl.ds(128, 128), :]
            e[0, rows(x * 512 + z * 128, 128), :] = jnp.where(lane, lo, pltpu.roll(hi, HALF, 1))
            e[2, rows(z * 512 + x * 128, 128), :] = jnp.where(lane, pltpu.roll(lo, HALF, 1), hi)
            return 0

        lax.fori_loop(0, max(len(xs), len(zs)), cell, 0)

    def pruned_y():
        all_back_y().wait_recv()
        for n, dist in enumerate(FAR):
            cells((n,), range(n, 4))
            exchange(2, 0, dist).start()
            cells(range(n + 1, 4), (n,))
            exchange(2, 2, dist).start()
        cells((3,), (3,))
        for part in (0, 2):
            f[part, own(PARTS[part][1], 512), :] = e[part, own(PARTS[part][1], 512), :]

    def add_up(part, src, size, axis):
        signs = [sign4(me[axis], jnp.int32(q)) for q in range(4)]

        def at(start, count):
            total = src[part, pl.ds(start, count), :]
            for q in range(1, 4):
                total = total + signs[q] * src[part, rows(q * size + start, count), :]
            return total

        return at

    def last(part):
        axis = PARTS[part][2]
        arrive(2, part)
        sums = add_up(part, f, 512, PARTS[part][1])

        def step(i, _):
            start = pl.multiple_of(i * 32, 32)
            g[part, pl.ds(start, 32), :] = sums(start, 32)
            return 0

        lax.fori_loop(0, 16, step, 0)
        send(3, part)
        h[part, own(axis, 128), :] = g[part, own(axis, 128), :]

    def final(part):
        arrive(3, part)
        return add_up(part, h, 128, PARTS[part][2])(0, 128)

    keep.wait()
    all_out_y(4).wait_recv()
    sy[own("y", 8), :] = sg[own("y", 8), :]
    core_y(4).start()
    across(0)
    for buf, axis, n in lines:
        all_line(buf, n).wait_recv()
    for src, buf, axis, n in planes:
        for dist in (1, 2, 3):
            plane(src, buf, axis, n, dist).start()
        buf[rows(me[axis] * 4096, 4096)] = src[...]
    core_y(4).wait_recv()
    core_y(0).wait_recv()
    panel0(0)
    across(1)
    across_b(1)
    across_b(3)
    core_y(1).wait_recv()
    panel0(1)
    whole(1)
    whole(3)
    across(2)
    core_y(2).wait_recv()
    panel0(2)

    def to_smem(i):
        return pltpu.make_async_copy(planes[i][1], (szy, sxy, sxz)[i], sm_sem.at[i])

    for i, (src, buf, axis, n) in enumerate(planes):
        all_plane(buf, n).wait_recv()
        to_smem(i).start()
    across(3)
    core_y(3).wait_recv()
    panel0(3)
    for i in range(3):
        to_smem(i).wait()
    turned(1)
    pruned(1, 2)
    turned(3)
    pruned(3, 2)
    pruned(1, 1)
    pruned(3, 1)
    pruned(1, 3)
    pruned(3, 3)
    pruned(1, 0)
    pruned(3, 0)
    pruned_y()
    scale = 1.0 / (128 * BLK) ** 0.5
    slot = lax.broadcasted_iota(jnp.int32, (128, 1), 0)
    count = cnt[0]

    def finish(panel, lower, upper):
        p0, p1 = final(lower), final(upper)
        cols = pl.ds(panel * 128, 128)
        lo = jnp.where(lane, p0, pltpu.roll(p1, HALF, 1)) * scale
        hi = jnp.where(lane, pltpu.roll(p0, HALF, 1), p1) * scale
        sk_out[pl.ds(0, 128), cols] = jnp.where(slot < count, lo, 0.0)
        sk_out[pl.ds(128, 128), cols] = jnp.where(slot + 128 < count, hi, 0.0)
        return jnp.concatenate(split(sk_out[:, cols]), axis=1)

    here = me["y"] * 4 + me["z"]

    def gram(p, q):
        out = lax.dot_general(p, q, (((0,), (0,)), ((), ())), preferred_element_type=jnp.float32)
        out = out[:128] + out[128:]
        return [out[:, i : i + 128] + out[:, i + 128 : i + 256] for i in range(0, out.shape[1], 256)]

    def piece(dx, o):
        to = {"y": (me["y"] + o // 4) % 4, "z": (me["z"] + o % 4) % 4, "x": (me["x"] + dx) % 4}
        src = to["x"] * 128 + (to["y"] * 4 + to["z"]) * 8
        dst = (here * 4 + me["x"]) * 8
        return remote(gp.at[rows(src, 8), :], rb.at[rows(dst, 8), :], rs_s.at[0], rs_r.at[0], moved(me, **to))

    def scatter(n):
        dx = (n - me["x"] + 4) % 4
        for o in range(1, 16):
            piece(dx, o).start()

        @pl.when(dx != 0)
        def _():
            piece(dx, 0).start()

    def all_pieces():
        most = pl.ds(0, 63 * 8)
        return remote(gp.at[most, :], rb.at[most, :], rs_s.at[0], rs_r.at[0], other)

    last(1)
    last(3)
    for k in range(5):
        core_y(k).wait_send()
        all_out_y(k).wait_send()
    all_back_y().wait_send()
    for buf, axis, n in lines:
        all_line(buf, n).wait_send()
    for src, buf, axis, n in planes:
        all_plane(buf, n).wait_send()
    for part in (1, 3):
        core_b(part).wait_send()
        for stage in range(4):
            all_three(stage, part).wait_send()
    last(0)
    last(2)
    sk1 = finish(1, 1, 3)
    gp[pl.ds(384, 128), :] = gram(sk1, sk1)[0]
    scatter(3)
    sk0 = finish(0, 0, 2)
    first, second = gram(sk0, jnp.concatenate([sk0, sk1], axis=1))
    gp[pl.ds(0, 128), :] = first
    scatter(0)
    gp[pl.ds(128, 128), :] = second
    scatter(1)
    gp[pl.ds(256, 128), :] = second.T
    scatter(2)
    rb[rows((here * 4 + me["x"]) * 8, 8), :] = gp[rows(me["x"] * 128 + here * 8, 8), :]
    for stage in (2, 3):
        for part in (0, 2):
            all_three(stage, part).wait_send()
    all_pieces().wait_recv()
    co[pl.ds(0, 8), :] = rb[...].reshape(64, 8, 128).sum(0) * (1.0 / (128 * 256))
    swap = remote(co.at[pl.ds(0, 8), :], co.at[pl.ds(8, 8), :], core_s.at[7], core_r.at[7], other)
    swap.start()
    all_pieces().wait_send()
    swap.wait_recv()
    mine = rows(here * 8, 8)
    ob[mine, :] = co[pl.ds(0, 8), :] + co[pl.ds(8, 8), :]

    def share(o):
        to = {"y": (me["y"] + o // 4) % 4, "z": (me["z"] + o % 4) % 4}
        return remote(ob.at[mine, :], ob.at[mine, :], ag_s.at[0], ag_r.at[0], moved(me, **to))

    for o in range(1, 16):
        share(o).start()
    most = pl.ds(0, 15 * 8)
    shares = remote(rb.at[most, :], ob.at[most, :], ag_s.at[0], ag_r.at[0], other)
    swap.wait_send()
    shares.wait_send()
    shares.wait_recv()
    gr_out[...] = ob[...]


def hand_on(a, b, to_a, to_b):
    to_a[...] = a[...]
    to_b[...] = b[...]


def local(matrix, signs, indices, counts):
    f32, i32 = jnp.float32, jnp.int32
    vmem, smem, dma = pltpu.VMEM, pltpu.SMEM, pltpu.SemaphoreType.DMA
    in_vmem = pl.BlockSpec(memory_space=vmem)
    sketch, gram = pl.pallas_call(
        kernel,
        name="sketch_gram",
        out_shape=(jax.ShapeDtypeStruct((256, 256), f32), jax.ShapeDtypeStruct((128, 128), f32)),
        in_specs=[pl.BlockSpec(memory_space=pl.ANY), in_vmem, in_vmem, pl.BlockSpec(memory_space=smem)],
        out_specs=(in_vmem, in_vmem),
        scratch_shapes=[
            vmem((4096, 128), f32), vmem((2, 2048, 128), f32), vmem((128, 128), f32),
            vmem((4, 1024, 128), f32), vmem((4, 1024, 128), f32), vmem((32, 128), i32), vmem((32, 128), i32),
            vmem((4, 1024, 128), f32), vmem((4096, 128), f32), vmem((256, 128), f32),
            vmem((2, 2048, 128), f32), vmem((2, 2048, 128), f32), vmem((2, 2048, 128), f32),
            vmem((4096, 128), f32), vmem((4096, 128), f32),
            vmem((4, 2048, 128), f32), vmem((4, 2048, 128), f32),
            vmem((4, 512, 128), f32), vmem((4, 512, 128), f32),
            vmem((1024,), i32), vmem((4096,), i32), vmem((4096,), i32),
            vmem((16384,), i32), vmem((16384,), i32), vmem((16384,), i32),
            smem((16384,), i32), smem((16384,), i32), smem((16384,), i32),
            vmem((512, 128), f32), vmem((512, 128), f32), vmem((16, 128), f32), vmem((128, 128), f32),
            dma((2,)), dma((8,)), dma((8,)), dma((6,)), dma((6,)), dma((16,)), dma((16,)),
            dma((5,)), dma((5,)), dma((3,)), dma((1,)), dma((1,)), dma((1,)), dma((1,)),
        ],
        compiler_params=pltpu.CompilerParams(
            collective_id=0, has_side_effects=True, vmem_limit_bytes=56 * 2**20
        ),
    )(matrix, signs.reshape(32, 128), indices, counts)
    sketch, gram = pl.pallas_call(
        hand_on,
        name="hand_on",
        out_shape=(jax.ShapeDtypeStruct((256, 256), f32), jax.ShapeDtypeStruct((128, 128), f32)),
        in_specs=[in_vmem] * 2,
        out_specs=(in_vmem,) * 2,
    )(sketch, gram)
    return sketch, gram[None]


def solution(mesh):
    in_specs = (P(("rx", "ry"), None), P(("rx", "ry")), P(("rx", "ry")), P(("rx", "ry")))
    out_specs = (P(("rx", "ry"), None), P("ry", None, None))
    return jax.shard_map(local, mesh=mesh, in_specs=in_specs, out_specs=out_specs, check_vma=False)
```

```python
import functools

import jax
import jax.numpy as jnp
from jax import lax
from jax.experimental import pallas as pl
from jax.experimental.pallas import tpu as pltpu
from jax.sharding import PartitionSpec as P

MESH = pl.DeviceIdType.MESH
BLK = 128
HALF = 64
FAR = (2, 1, 3)
PARTS = (("y", "x", "z"), ("x", "z", "y"), ("y", "z", "x"), ("z", "x", "y"))


def coords():
    rx = lax.axis_index("rx")
    return {"y": rx // 8, "z": (rx // 2) % 4, "c": rx % 2, "x": lax.axis_index("ry")}


def device(at):
    return ((at["y"] * 4 + at["z"]) * 2 + at["c"], at["x"])


def moved(at, **to):
    return device({**at, **to})


def sign4(a, b):
    odd = (a % 2) * (b % 2) + (a // 2) * (b // 2)
    return (1 - 2 * (odd % 2)).astype(jnp.float32)


def hadamard(n):
    both = lax.broadcasted_iota(jnp.int32, (n, n), 0) & lax.broadcasted_iota(jnp.int32, (n, n), 1)
    both = both ^ (both >> 4)
    both = both ^ (both >> 2)
    both = both ^ (both >> 1)
    return (1 - 2 * (both & 1)).astype(jnp.float32)


def kernel(
    x_hbm, sg, idx, cnt, sk_out, gr_out,
    xm, bo, had, ry, ro, sy, syo, cy, dy, r, a, b, c, d1, d3, e, f, g, h,
    tile, ly, lz, pzy, pxy, pxz, szy, sxy, sxz, gp, rb, co, ob,
    loc_sem, core_s, core_r, y_s, y_r, st_s, st_r, ix_s, ix_r, sm_sem, rs_s, rs_r, ag_s, ag_r,
):
    me = coords()
    done = {1: d1, 3: d3}
    lane = lax.broadcasted_iota(jnp.int32, (1, 128), 1) < HALF
    other = moved(me, c=1 - me["c"])

    def rows(start, size):
        return pl.ds(pl.multiple_of(start, 1024 if size % 1024 == 0 else 8), size)

    def remote(src, dst, send, recv, to):
        return pltpu.make_async_remote_copy(
            src_ref=src, dst_ref=dst, send_sem=send, recv_sem=recv, device_id=to, device_id_type=MESH
        )

    load = pltpu.make_async_copy(x_hbm.at[:, pl.ds(128, 128)], xm, loc_sem.at[0])
    keep = pltpu.make_async_copy(
        x_hbm.at[rows(me["y"] * 1024, 1024), pl.ds(0, 128)], ry.at[me["y"]], loc_sem.at[1]
    )
    load.start()
    keep.start()

    barrier = pltpu.get_barrier_semaphore()

    for axis in "yxz":
        for dist in (1, 2, 3):
            to = moved(me, **{axis: (me[axis] + dist) % 4})
            pl.semaphore_signal(barrier, inc=1, device_id=to, device_id_type=MESH)
    pl.semaphore_signal(barrier, inc=1, device_id=other, device_id_type=MESH)

    had[...] = hadamard(BLK)
    tile[...] = jnp.zeros_like(tile)
    tile[pl.ds(0, 128)] = idx[pl.ds(0, 128)]
    tile[pl.ds(128, 128)] = idx[pl.ds(128, 128)] ^ 2048
    tile[pl.ds(256, 128)] = idx[pl.ds(128, 128)]

    def split(v):
        hi = v.astype(jnp.bfloat16)
        return hi, (v - hi.astype(jnp.float32)).astype(jnp.bfloat16)

    def times(left, v):
        out = jnp.dot(left, jnp.concatenate(split(v), axis=1), preferred_element_type=jnp.float32)
        return out[:, :128] + out[:, 128:]

    def panel1(i, _):
        def block(at):
            left = had[...] * sg[pl.ds(at, 1), :].astype(jnp.float32)
            return times(left.astype(jnp.bfloat16), xm[rows(at * BLK, BLK), :])

        lo, hi = block(i), block(i + 16)
        place = rows(i * BLK, BLK)
        a[0, place, :] = jnp.where(lane, lo, pltpu.roll(hi, HALF, 1))
        a[1, place, :] = jnp.where(lane, pltpu.roll(lo, HALF, 1), hi)
        return 0

    pl.semaphore_wait(barrier, 10)

    def out_y(k, dist):
        at = (me["y"] + dist) % 4
        if k == 4:
            src, dst = sg.at[rows(at * 8, 8), :], sy.at[rows(me["y"] * 8, 8), :]
        else:
            src = x_hbm.at[rows(at * 1024 + k * 256, 256), pl.ds(0, 128)]
            dst = ry.at[me["y"], pl.ds(k * 256, 256), :]
        return remote(src, dst, y_s.at[k], y_r.at[k], moved(me, y=at))

    def all_out_y(k):
        if k == 4:
            return remote(sg.at[pl.ds(0, 24), :], sy.at[pl.ds(0, 24), :], y_s.at[k], y_r.at[k], other)
        return remote(
            x_hbm.at[pl.ds(0, 768), pl.ds(0, 128)], ry.at[0, pl.ds(0, 768), :], y_s.at[k], y_r.at[k], other
        )

    def back_y(k, dist):
        at = (me["y"] + dist) % 4
        return remote(
            cy.at[at, pl.ds(k * 256, 256), :], dy.at[rows(me["y"] * 1024 + k * 256, 256), :],
            y_s.at[5], y_r.at[5], moved(me, y=at),
        )

    def all_back_y():
        return remote(cy.at[pl.ds(0, 3)], ro.at[pl.ds(0, 3)], y_s.at[5], y_r.at[5], other)

    def core_y(k):
        i = 2 + k
        if k == 4:
            return remote(sy, syo, core_s.at[i], core_r.at[i], other)
        place = pl.ds(k * 256, 256)
        return remote(ry.at[:, place, :], ro.at[:, place, :], core_s.at[i], core_r.at[i], other)

    def line(buf, axis, n, dist):
        to = moved(me, **{axis: (me[axis] + dist) % 4})
        return remote(tile, buf.at[rows(me[axis] * 1024, 1024)], ix_s.at[n], ix_r.at[n], to)

    def all_line(buf, n):
        return remote(lines[1 - n][0].at[pl.ds(0, 3072)], buf.at[pl.ds(0, 3072)], ix_s.at[n], ix_r.at[n], other)

    def plane(src, buf, axis, n, dist):
        to = moved(me, **{axis: (me[axis] + dist) % 4})
        return remote(src, buf.at[rows(me[axis] * 4096, 4096)], ix_s.at[2 + n], ix_r.at[2 + n], to)

    def all_plane(buf, n):
        some = pl.ds(0, 12288)
        return remote(planes[(n + 1) % 3][1].at[some], buf.at[some], ix_s.at[2 + n], ix_r.at[2 + n], other)

    lines = ((ly, "y", 0), (lz, "z", 1))
    planes = ((ly, pzy, "z", 0), (ly, pxy, "x", 1), (lz, pxz, "x", 2))

    def exchange(stage, part, dist):
        axis = PARTS[part][max(stage - 1, 0)]
        at = (me[axis] + dist) % 4
        size = 128 if stage == 3 else 512
        i = stage * 4 + part
        src = (a, c, e, g)[stage].at[part // 2 if stage < 2 else part, rows(at * size, size), :]
        mine = rows(me[axis] * size, size)
        if stage == 1:
            dst = done[part].at[mine, :]
        else:
            dst = (b, None, f, h)[stage].at[part // 2 if stage < 2 else part, mine, :]
        return remote(src, dst, st_s.at[i], st_r.at[i], moved(me, **{axis: at}))

    def all_three(stage, part):
        n, i = part // 2 if stage < 2 else part, stage * 4 + part
        three = pl.ds(0, 384 if stage == 3 else 1536)
        dst = done[part].at[three, :] if stage == 1 else (b, None, f, h)[stage].at[n, three, :]
        return remote((a, c, e, g)[stage].at[n, three, :], dst, st_s.at[i], st_r.at[i], other)

    def send(stage, part):
        for dist in FAR:
            exchange(stage, part, dist).start()

    def arrive(stage, part):
        all_three(stage, part).wait_recv()

    def own(axis, size):
        return rows(me[axis] * size, size)

    def core_b(part):
        n = part // 2
        return remote(b.at[n], bo.at[n], core_s.at[n], core_r.at[n], other)

    for dist in FAR:
        out_y(4, dist).start()
    for buf, axis, n in lines:
        for dist in (1, 2, 3):
            line(buf, axis, n, dist).start()
    for dist in FAR:
        out_y(0, dist).start()
    load.wait()
    lax.fori_loop(0, 16, panel1, 0)
    for part in (1, 3):
        send(0, part)
        b[part // 2, own(PARTS[part][0], 512), :] = a[part // 2, own(PARTS[part][0], 512), :]
    for k in range(1, 4):
        for dist in FAR:
            out_y(k, dist).start()
    for buf, axis, n in lines:
        buf[rows(me[axis] * 1024, 1024)] = tile[...]

    sign = (1 - 2 * me["c"]).astype(jnp.float32)

    def mixed(s0, s1, x0, x1):
        hm = had[...]
        left = jnp.concatenate(
            [hm * (s0.astype(jnp.float32) * sign), hm * s1.astype(jnp.float32)], axis=1
        ).astype(jnp.bfloat16)
        return times(left, jnp.concatenate([x0, x1], axis=0))

    def four(v):
        s, t, u, w = v[0] + v[1], v[0] - v[1], v[2] + v[3], v[2] - v[3]
        return s + u, t + w, s - u, t - w

    def panel0(k):
        def step(n, _):
            at = k * 2 + n
            place = rows(at * BLK, BLK)
            v = [
                mixed(sy[pl.ds(q * 8 + at, 1), :], syo[pl.ds(q * 8 + at, 1), :], ry[q, place, :], ro[q, place, :])
                for q in range(4)
            ]
            for q, out in enumerate(four(v)):
                cy[q, place, :] = out
            return 0

        lax.fori_loop(0, 2, step, 0)
        for dist in FAR:
            back_y(k, dist).start()
        dy[rows(me["y"] * 1024 + k * 256, 256), :] = cy[me["y"], pl.ds(k * 256, 256), :]

    def across(k):
        all_out_y(k).wait_recv()
        core_y(k).start()

    def across_b(part):
        arrive(0, part)
        core_b(part).start()

    def whole(part):
        n, axis = part // 2, PARTS[part][0]
        core_b(part).wait_recv()

        def step(i, _):
            places = [rows(q * 512 + i * 32, 32) for q in range(4)]
            for place, out in zip(places, four([b[n, p, :] * sign + bo[n, p, :] for p in places])):
                c[n, place, :] = out
            return 0

        lax.fori_loop(0, 16, step, 0)
        send(1, part)
        done[part][own(axis, 512), :] = c[n, own(axis, 512), :]

    def gather(part, m, dst):
        table, src = {1: szy, 3: sxy}[part], done[part]

        def some(i, _):
            base = (m * 4 + i // 2) * 1024 + (i % 2) * 64
            for u in range(64):
                lo = src[pl.ds(table[base + u], 1), :]
                hi = src[pl.ds(table[base + 128 + u], 1), :]
                dst[part, pl.ds(m * 512 + i * 64 + u, 1), :] = jnp.where(lane, lo, hi)
            return 0

        lax.fori_loop(0, 8, some, 0)

    def turned(part):
        arrive(1, part)

        def turn(i, _):
            done[part][rows(2048 + i * 64, 64), :] = pltpu.roll(done[part][rows(i * 64, 64), :], HALF, 1)
            return 0

        lax.fori_loop(0, 32, turn, 0)

    def pruned(part, dist):
        axis = PARTS[part][1]
        gather(part, (me[axis] + dist) % 4, e if dist else f)
        if dist:
            exchange(2, part, dist).start()

    def far(n):
        return jnp.where(n == 0, 2, jnp.where(n == 1, 1, jnp.where(n == 2, 3, 0)))

    def cells(xs, zs):
        def cell(n, _):
            x = (me["x"] + far(xs[0] + n if len(xs) > 1 else xs[0])) % 4
            z = (me["z"] + far(zs[0] + n if len(zs) > 1 else zs[0])) % 4
            base = (x * 4 + z) * 1024
            table = sxz

            def some(i, _):
                for u in range(32):
                    r[pl.ds(i * 32 + u, 1), :] = dy[pl.ds(table[base + i * 32 + u], 1), :]
                    r[pl.ds(128 + i * 32 + u, 1), :] = dy[pl.ds(table[base + 256 + i * 32 + u], 1), :]
                return 0

            lax.fori_loop(0, 4, some, 0)
            lo, hi = r[pl.ds(0, 128), :], r[pl.ds(128, 128), :]
            e[0, rows(x * 512 + z * 128, 128), :] = jnp.where(lane, lo, pltpu.roll(hi, HALF, 1))
            e[2, rows(z * 512 + x * 128, 128), :] = jnp.where(lane, pltpu.roll(lo, HALF, 1), hi)
            return 0

        lax.fori_loop(0, max(len(xs), len(zs)), cell, 0)

    def pruned_y():
        all_back_y().wait_recv()
        for n, dist in enumerate(FAR):
            cells((n,), range(n, 4))
            exchange(2, 0, dist).start()
            cells(range(n + 1, 4), (n,))
            exchange(2, 2, dist).start()
        cells((3,), (3,))
        for part in (0, 2):
            f[part, own(PARTS[part][1], 512), :] = e[part, own(PARTS[part][1], 512), :]

    def add_up(part, src, size, axis):
        signs = [sign4(me[axis], jnp.int32(q)) for q in range(4)]

        def at(start, count):
            total = src[part, pl.ds(start, count), :]
            for q in range(1, 4):
                total = total + signs[q] * src[part, rows(q * size + start, count), :]
            return total

        return at

    def last(part):
        axis = PARTS[part][2]
        arrive(2, part)
        sums = add_up(part, f, 512, PARTS[part][1])

        def step(i, _):
            start = pl.multiple_of(i * 32, 32)
            g[part, pl.ds(start, 32), :] = sums(start, 32)
            return 0

        lax.fori_loop(0, 16, step, 0)
        send(3, part)
        h[part, own(axis, 128), :] = g[part, own(axis, 128), :]

    def final(part):
        arrive(3, part)
        return add_up(part, h, 128, PARTS[part][2])(0, 128)

    keep.wait()
    all_out_y(4).wait_recv()
    sy[own("y", 8), :] = sg[own("y", 8), :]
    core_y(4).start()
    across(0)
    for buf, axis, n in lines:
        all_line(buf, n).wait_recv()
    for src, buf, axis, n in planes:
        for dist in (1, 2, 3):
            plane(src, buf, axis, n, dist).start()
        buf[rows(me[axis] * 4096, 4096)] = src[...]
    core_y(4).wait_recv()
    core_y(0).wait_recv()
    panel0(0)
    across(1)
    across_b(1)
    across_b(3)
    core_y(1).wait_recv()
    panel0(1)
    whole(1)
    whole(3)
    across(2)
    core_y(2).wait_recv()
    panel0(2)

    def to_smem(i):
        return pltpu.make_async_copy(planes[i][1], (szy, sxy, sxz)[i], sm_sem.at[i])

    for i, (src, buf, axis, n) in enumerate(planes):
        all_plane(buf, n).wait_recv()
        to_smem(i).start()
    across(3)
    core_y(3).wait_recv()
    panel0(3)
    for i in range(3):
        to_smem(i).wait()
    turned(1)
    pruned(1, 2)
    turned(3)
    pruned(3, 2)
    pruned(1, 1)
    pruned(3, 1)
    pruned(1, 3)
    pruned(3, 3)
    pruned(1, 0)
    pruned(3, 0)
    pruned_y()
    scale = 1.0 / (128 * BLK) ** 0.5
    slot = lax.broadcasted_iota(jnp.int32, (128, 1), 0)
    count = cnt[0]

    def finish(panel, lower, upper):
        p0, p1 = final(lower), final(upper)
        cols = pl.ds(panel * 128, 128)
        lo = jnp.where(lane, p0, pltpu.roll(p1, HALF, 1)) * scale
        hi = jnp.where(lane, pltpu.roll(p0, HALF, 1), p1) * scale
        sk_out[pl.ds(0, 128), cols] = jnp.where(slot < count, lo, 0.0)
        sk_out[pl.ds(128, 128), cols] = jnp.where(slot + 128 < count, hi, 0.0)
        return jnp.concatenate(split(sk_out[:, cols]), axis=1)

    here = me["y"] * 4 + me["z"]

    def gram(p, q):
        out = lax.dot_general(p, q, (((0,), (0,)), ((), ())), preferred_element_type=jnp.float32)
        out = out[:128] + out[128:]
        return [out[:, i : i + 128] + out[:, i + 128 : i + 256] for i in range(0, out.shape[1], 256)]

    def piece(dx, o):
        to = {"y": (me["y"] + o // 4) % 4, "z": (me["z"] + o % 4) % 4, "x": (me["x"] + dx) % 4}
        src = to["x"] * 128 + (to["y"] * 4 + to["z"]) * 8
        dst = (here * 4 + me["x"]) * 8
        return remote(gp.at[rows(src, 8), :], rb.at[rows(dst, 8), :], rs_s.at[0], rs_r.at[0], moved(me, **to))

    def scatter(n):
        dx = (n - me["x"] + 4) % 4
        for o in range(1, 16):
            piece(dx, o).start()

        @pl.when(dx != 0)
        def _():
            piece(dx, 0).start()

    def pieces(count, of):
        most = pl.ds(0, count * 8)
        return remote(of.at[most, :], rb.at[most, :], rs_s.at[0], rs_r.at[0], other)

    last(1)
    last(3)
    for k in range(5):
        core_y(k).wait_send()
        all_out_y(k).wait_send()
    all_back_y().wait_send()
    for buf, axis, n in lines:
        all_line(buf, n).wait_send()
    for src, buf, axis, n in planes:
        all_plane(buf, n).wait_send()
    for part in (1, 3):
        core_b(part).wait_send()
        for stage in range(4):
            all_three(stage, part).wait_send()
    sk1 = finish(1, 1, 3)
    gp[pl.ds(384, 128), :] = gram(sk1, sk1)[0]
    scatter(3)
    last(0)
    last(2)
    sk0 = finish(0, 0, 2)
    first, second = gram(sk0, jnp.concatenate([sk0, sk1], axis=1))
    gp[pl.ds(0, 128), :] = first
    scatter(0)
    gp[pl.ds(128, 128), :] = second
    scatter(1)
    rb[rows((here * 4 + me["x"]) * 8, 8), :] = gp[rows(me["x"] * 128 + here * 8, 8), :]
    for stage in (2, 3):
        for part in (0, 2):
            all_three(stage, part).wait_send()
    mine = rows(here * 8, 8)

    def share(o, x):
        to = {"y": (me["y"] + o // 4) % 4, "z": (me["z"] + o % 4) % 4, "x": x}
        return remote(ob.at[mine, :], ob.at[mine, :], ag_s.at[0], ag_r.at[0], moved(me, **to))

    def shares(count):
        most = pl.ds(0, count * 8)
        return remote(rb.at[most, :], ob.at[most, :] if count < 17 else rb.at[most, :], ag_s.at[0], ag_r.at[0], other)

    @pl.when(me["x"] != 2)
    def _():
        pieces(63, rb).wait_recv()
        co[pl.ds(0, 8), :] = rb[...].reshape(64, 8, 128).sum(0) * (1.0 / (128 * 256))
        swap = remote(co.at[pl.ds(0, 8), :], co.at[pl.ds(8, 8), :], core_s.at[7], core_r.at[7], other)
        swap.start()
        pieces(47, gp).wait_send()
        swap.wait_recv()
        ob[mine, :] = co[pl.ds(0, 8), :] + co[pl.ds(8, 8), :]

        @pl.when(me["x"] == 1)
        def _():
            for o in range(16):
                share(o, 2).start()

        for o in range(1, 16):
            share(o, me["x"]).start()
        swap.wait_send()

        @pl.when(me["x"] == 1)
        def _():
            shares(31).wait_send()

        @pl.when(me["x"] != 1)
        def _():
            shares(15).wait_send()

        shares(15).wait_recv()
        gr_out[...] = ob[...]

    @pl.when(me["x"] == 2)
    def _():
        pieces(48, gp).wait_send()
        shares(16).wait_recv()
        gr_out[...] = ob[...].T


def hand_on(a, b, to_a, to_b):
    to_a[...] = a[...]
    to_b[...] = b[...]


def local(matrix, signs, indices, counts):
    f32, i32 = jnp.float32, jnp.int32
    vmem, smem, dma = pltpu.VMEM, pltpu.SMEM, pltpu.SemaphoreType.DMA
    in_vmem = pl.BlockSpec(memory_space=vmem)
    sketch, gram = pl.pallas_call(
        kernel,
        name="sketch_gram",
        out_shape=(jax.ShapeDtypeStruct((256, 256), f32), jax.ShapeDtypeStruct((128, 128), f32)),
        in_specs=[pl.BlockSpec(memory_space=pl.ANY), in_vmem, in_vmem, pl.BlockSpec(memory_space=smem)],
        out_specs=(in_vmem, in_vmem),
        scratch_shapes=[
            vmem((4096, 128), f32), vmem((2, 2048, 128), f32), vmem((128, 128), f32),
            vmem((4, 1024, 128), f32), vmem((4, 1024, 128), f32), vmem((32, 128), i32), vmem((32, 128), i32),
            vmem((4, 1024, 128), f32), vmem((4096, 128), f32), vmem((256, 128), f32),
            vmem((2, 2048, 128), f32), vmem((2, 2048, 128), f32), vmem((2, 2048, 128), f32),
            vmem((4096, 128), f32), vmem((4096, 128), f32),
            vmem((4, 2048, 128), f32), vmem((4, 2048, 128), f32),
            vmem((4, 512, 128), f32), vmem((4, 512, 128), f32),
            vmem((1024,), i32), vmem((4096,), i32), vmem((4096,), i32),
            vmem((16384,), i32), vmem((16384,), i32), vmem((16384,), i32),
            smem((16384,), i32), smem((16384,), i32), smem((16384,), i32),
            vmem((512, 128), f32), vmem((512, 128), f32), vmem((16, 128), f32), vmem((128, 128), f32),
            dma((2,)), dma((8,)), dma((8,)), dma((6,)), dma((6,)), dma((16,)), dma((16,)),
            dma((5,)), dma((5,)), dma((3,)), dma((1,)), dma((1,)), dma((1,)), dma((1,)),
        ],
        compiler_params=pltpu.CompilerParams(
            collective_id=0, has_side_effects=True, vmem_limit_bytes=56 * 2**20
        ),
    )(matrix, signs.reshape(32, 128), indices, counts)
    sketch, gram = pl.pallas_call(
        hand_on,
        name="hand_on",
        out_shape=(jax.ShapeDtypeStruct((256, 256), f32), jax.ShapeDtypeStruct((128, 128), f32)),
        in_specs=[in_vmem] * 2,
        out_specs=(in_vmem,) * 2,
    )(sketch, gram)
    return sketch, gram[None]


def solution(mesh):
    in_specs = (P(("rx", "ry"), None), P(("rx", "ry")), P(("rx", "ry")), P(("rx", "ry")))
    out_specs = (P(("rx", "ry"), None), P("ry", None, None))
    return jax.shard_map(local, mesh=mesh, in_specs=in_specs, out_specs=out_specs, check_vma=False)
```

```python
import functools

import jax
import jax.numpy as jnp
from jax import lax
from jax.experimental import pallas as pl
from jax.experimental.pallas import tpu as pltpu
from jax.sharding import PartitionSpec as P

MESH = pl.DeviceIdType.MESH
BLK = 128
HALF = 64
FAR = (2, 1, 3)
FAR_PLANE = sorted(range(1, 16), key=lambda o: -(2 - abs(o // 4 - 2)) - (2 - abs(o % 4 - 2)))
PARTS = (("y", "x", "z"), ("x", "z", "y"), ("y", "z", "x"), ("z", "x", "y"))


def coords():
    rx = lax.axis_index("rx")
    return {"y": rx // 8, "z": (rx // 2) % 4, "c": rx % 2, "x": lax.axis_index("ry")}


def device(at):
    return ((at["y"] * 4 + at["z"]) * 2 + at["c"], at["x"])


def moved(at, **to):
    return device({**at, **to})


def sign4(a, b):
    odd = (a % 2) * (b % 2) + (a // 2) * (b // 2)
    return (1 - 2 * (odd % 2)).astype(jnp.float32)


def hadamard(n):
    both = lax.broadcasted_iota(jnp.int32, (n, n), 0) & lax.broadcasted_iota(jnp.int32, (n, n), 1)
    both = both ^ (both >> 4)
    both = both ^ (both >> 2)
    both = both ^ (both >> 1)
    return (1 - 2 * (both & 1)).astype(jnp.float32)


def kernel(
    x_hbm, sg, idx, cnt, sk_out, gr_out,
    xm, bo, had, ry, ro, sy, syo, cy, dy, r, a, b, c, d1, d3, e, f, g, h,
    tile, ly, lz, pzy, pxy, pxz, szy, sxy, sxz, gp, rb, co, ob,
    loc_sem, core_s, core_r, y_s, y_r, st_s, st_r, ix_s, ix_r, sm_sem, rs_s, rs_r, ag_s, ag_r,
):
    me = coords()
    done = {1: d1, 3: d3}
    lane = lax.broadcasted_iota(jnp.int32, (1, 128), 1) < HALF
    other = moved(me, c=1 - me["c"])

    def rows(start, size):
        return pl.ds(pl.multiple_of(start, 1024 if size % 1024 == 0 else 8), size)

    def remote(src, dst, send, recv, to):
        return pltpu.make_async_remote_copy(
            src_ref=src, dst_ref=dst, send_sem=send, recv_sem=recv, device_id=to, device_id_type=MESH
        )

    load = pltpu.make_async_copy(x_hbm.at[:, pl.ds(128, 128)], xm, loc_sem.at[0])
    keep = pltpu.make_async_copy(
        x_hbm.at[rows(me["y"] * 1024, 1024), pl.ds(0, 128)], ry.at[me["y"]], loc_sem.at[1]
    )
    load.start()
    keep.start()

    barrier = pltpu.get_barrier_semaphore()

    for axis in "yxz":
        for dist in (1, 2, 3):
            to = moved(me, **{axis: (me[axis] + dist) % 4})
            pl.semaphore_signal(barrier, inc=1, device_id=to, device_id_type=MESH)
    pl.semaphore_signal(barrier, inc=1, device_id=other, device_id_type=MESH)

    had[...] = hadamard(BLK)
    tile[...] = jnp.zeros_like(tile)
    tile[pl.ds(0, 128)] = idx[pl.ds(0, 128)]
    tile[pl.ds(128, 128)] = idx[pl.ds(128, 128)] ^ 2048
    tile[pl.ds(256, 128)] = idx[pl.ds(128, 128)]

    def split(v):
        hi = v.astype(jnp.bfloat16)
        return hi, (v - hi.astype(jnp.float32)).astype(jnp.bfloat16)

    def times(left, v):
        out = jnp.dot(left, jnp.concatenate(split(v), axis=1), preferred_element_type=jnp.float32)
        return out[:, :128] + out[:, 128:]

    def panel1(i, _):
        def block(at):
            left = had[...] * sg[pl.ds(at, 1), :].astype(jnp.float32)
            return times(left.astype(jnp.bfloat16), xm[rows(at * BLK, BLK), :])

        lo, hi = block(i), block(i + 16)
        place = rows(i * BLK, BLK)
        a[0, place, :] = jnp.where(lane, lo, pltpu.roll(hi, HALF, 1))
        a[1, place, :] = jnp.where(lane, pltpu.roll(lo, HALF, 1), hi)
        return 0

    pl.semaphore_wait(barrier, 10)

    def out_y(k, dist):
        at = (me["y"] + dist) % 4
        if k == 4:
            src, dst = sg.at[rows(at * 8, 8), :], sy.at[rows(me["y"] * 8, 8), :]
        else:
            src = x_hbm.at[rows(at * 1024 + k * 256, 256), pl.ds(0, 128)]
            dst = ry.at[me["y"], pl.ds(k * 256, 256), :]
        return remote(src, dst, y_s.at[k], y_r.at[k], moved(me, y=at))

    def all_out_y(k):
        if k == 4:
            return remote(sg.at[pl.ds(0, 24), :], sy.at[pl.ds(0, 24), :], y_s.at[k], y_r.at[k], other)
        return remote(
            x_hbm.at[pl.ds(0, 768), pl.ds(0, 128)], ry.at[0, pl.ds(0, 768), :], y_s.at[k], y_r.at[k], other
        )

    def back_y(k, dist):
        at = (me["y"] + dist) % 4
        return remote(
            cy.at[at, pl.ds(k * 256, 256), :], dy.at[rows(me["y"] * 1024 + k * 256, 256), :],
            y_s.at[5], y_r.at[5], moved(me, y=at),
        )

    def all_back_y():
        return remote(cy.at[pl.ds(0, 3)], ro.at[pl.ds(0, 3)], y_s.at[5], y_r.at[5], other)

    def core_y(k):
        i = 2 + k
        if k == 4:
            return remote(sy, syo, core_s.at[i], core_r.at[i], other)
        place = pl.ds(k * 256, 256)
        return remote(ry.at[:, place, :], ro.at[:, place, :], core_s.at[i], core_r.at[i], other)

    def line(buf, axis, n, dist):
        to = moved(me, **{axis: (me[axis] + dist) % 4})
        return remote(tile, buf.at[rows(me[axis] * 1024, 1024)], ix_s.at[n], ix_r.at[n], to)

    def all_line(buf, n):
        return remote(lines[1 - n][0].at[pl.ds(0, 3072)], buf.at[pl.ds(0, 3072)], ix_s.at[n], ix_r.at[n], other)

    def plane(src, buf, axis, n, dist):
        to = moved(me, **{axis: (me[axis] + dist) % 4})
        return remote(src, buf.at[rows(me[axis] * 4096, 4096)], ix_s.at[2 + n], ix_r.at[2 + n], to)

    def all_plane(buf, n):
        some = pl.ds(0, 12288)
        return remote(planes[(n + 1) % 3][1].at[some], buf.at[some], ix_s.at[2 + n], ix_r.at[2 + n], other)

    lines = ((ly, "y", 0), (lz, "z", 1))
    planes = ((ly, pzy, "z", 0), (ly, pxy, "x", 1), (lz, pxz, "x", 2))

    def exchange(stage, part, dist):
        axis = PARTS[part][max(stage - 1, 0)]
        at = (me[axis] + dist) % 4
        size = 128 if stage == 3 else 512
        i = stage * 4 + part
        src = (a, c, e, g)[stage].at[part // 2 if stage < 2 else part, rows(at * size, size), :]
        mine = rows(me[axis] * size, size)
        if stage == 1:
            dst = done[part].at[mine, :]
        else:
            dst = (b, None, f, h)[stage].at[part // 2 if stage < 2 else part, mine, :]
        return remote(src, dst, st_s.at[i], st_r.at[i], moved(me, **{axis: at}))

    def all_three(stage, part):
        n, i = part // 2 if stage < 2 else part, stage * 4 + part
        three = pl.ds(0, 384 if stage == 3 else 1536)
        dst = done[part].at[three, :] if stage == 1 else (b, None, f, h)[stage].at[n, three, :]
        return remote((a, c, e, g)[stage].at[n, three, :], dst, st_s.at[i], st_r.at[i], other)

    def send(stage, part):
        for dist in FAR:
            exchange(stage, part, dist).start()

    def arrive(stage, part):
        all_three(stage, part).wait_recv()

    def own(axis, size):
        return rows(me[axis] * size, size)

    def core_b(part):
        n = part // 2
        return remote(b.at[n], bo.at[n], core_s.at[n], core_r.at[n], other)

    for dist in FAR:
        out_y(4, dist).start()
    for buf, axis, n in lines:
        for dist in (1, 2, 3):
            line(buf, axis, n, dist).start()
    for dist in FAR:
        out_y(0, dist).start()
    load.wait()
    lax.fori_loop(0, 16, panel1, 0)
    for part in (1, 3):
        send(0, part)
        b[part // 2, own(PARTS[part][0], 512), :] = a[part // 2, own(PARTS[part][0], 512), :]
    for k in range(1, 4):
        for dist in FAR:
            out_y(k, dist).start()
    for buf, axis, n in lines:
        buf[rows(me[axis] * 1024, 1024)] = tile[...]

    sign = (1 - 2 * me["c"]).astype(jnp.float32)

    def mixed(s0, s1, x0, x1):
        hm = had[...]
        left = jnp.concatenate(
            [hm * (s0.astype(jnp.float32) * sign), hm * s1.astype(jnp.float32)], axis=1
        ).astype(jnp.bfloat16)
        return times(left, jnp.concatenate([x0, x1], axis=0))

    def four(v):
        s, t, u, w = v[0] + v[1], v[0] - v[1], v[2] + v[3], v[2] - v[3]
        return s + u, t + w, s - u, t - w

    def panel0(k):
        def step(n, _):
            at = k * 2 + n
            place = rows(at * BLK, BLK)
            v = [
                mixed(sy[pl.ds(q * 8 + at, 1), :], syo[pl.ds(q * 8 + at, 1), :], ry[q, place, :], ro[q, place, :])
                for q in range(4)
            ]
            for q, out in enumerate(four(v)):
                cy[q, place, :] = out
            return 0

        lax.fori_loop(0, 2, step, 0)
        for dist in FAR:
            back_y(k, dist).start()
        dy[rows(me["y"] * 1024 + k * 256, 256), :] = cy[me["y"], pl.ds(k * 256, 256), :]

    def across(k):
        all_out_y(k).wait_recv()
        core_y(k).start()

    def across_b(part):
        arrive(0, part)
        core_b(part).start()

    def whole(part):
        n, axis = part // 2, PARTS[part][0]
        core_b(part).wait_recv()

        def step(i, _):
            places = [rows(q * 512 + i * 32, 32) for q in range(4)]
            for place, out in zip(places, four([b[n, p, :] * sign + bo[n, p, :] for p in places])):
                c[n, place, :] = out
            return 0

        lax.fori_loop(0, 16, step, 0)
        send(1, part)
        done[part][own(axis, 512), :] = c[n, own(axis, 512), :]

    def gather(part, m, dst):
        table, src = {1: szy, 3: sxy}[part], done[part]

        def some(i, _):
            base = (m * 4 + i // 2) * 1024 + (i % 2) * 64
            for u in range(64):
                lo = src[pl.ds(table[base + u], 1), :]
                hi = src[pl.ds(table[base + 128 + u], 1), :]
                dst[part, pl.ds(m * 512 + i * 64 + u, 1), :] = jnp.where(lane, lo, hi)
            return 0

        lax.fori_loop(0, 8, some, 0)

    def turned(part):
        arrive(1, part)

        def turn(i, _):
            done[part][rows(2048 + i * 64, 64), :] = pltpu.roll(done[part][rows(i * 64, 64), :], HALF, 1)
            return 0

        lax.fori_loop(0, 32, turn, 0)

    def pruned(part, dist):
        axis = PARTS[part][1]
        gather(part, (me[axis] + dist) % 4, e if dist else f)
        if dist:
            exchange(2, part, dist).start()

    def far(n):
        return jnp.where(n == 0, 2, jnp.where(n == 1, 1, jnp.where(n == 2, 3, 0)))

    def cells(xs, zs):
        def cell(n, _):
            x = (me["x"] + far(xs[0] + n if len(xs) > 1 else xs[0])) % 4
            z = (me["z"] + far(zs[0] + n if len(zs) > 1 else zs[0])) % 4
            base = (x * 4 + z) * 1024
            table = sxz

            def some(i, _):
                for u in range(32):
                    r[pl.ds(i * 32 + u, 1), :] = dy[pl.ds(table[base + i * 32 + u], 1), :]
                    r[pl.ds(128 + i * 32 + u, 1), :] = dy[pl.ds(table[base + 256 + i * 32 + u], 1), :]
                return 0

            lax.fori_loop(0, 4, some, 0)
            lo, hi = r[pl.ds(0, 128), :], r[pl.ds(128, 128), :]
            e[0, rows(x * 512 + z * 128, 128), :] = jnp.where(lane, lo, pltpu.roll(hi, HALF, 1))
            e[2, rows(z * 512 + x * 128, 128), :] = jnp.where(lane, pltpu.roll(lo, HALF, 1), hi)
            return 0

        lax.fori_loop(0, max(len(xs), len(zs)), cell, 0)

    def pruned_y():
        all_back_y().wait_recv()
        for n, dist in enumerate(FAR):
            cells((n,), range(n, 4))
            exchange(2, 0, dist).start()
            cells(range(n + 1, 4), (n,))
            exchange(2, 2, dist).start()
        cells((3,), (3,))
        for part in (0, 2):
            f[part, own(PARTS[part][1], 512), :] = e[part, own(PARTS[part][1], 512), :]

    def add_up(part, src, size, axis):
        signs = [sign4(me[axis], jnp.int32(q)) for q in range(4)]

        def at(start, count):
            total = src[part, pl.ds(start, count), :]
            for q in range(1, 4):
                total = total + signs[q] * src[part, rows(q * size + start, count), :]
            return total

        return at

    def last(part):
        axis = PARTS[part][2]
        arrive(2, part)
        sums = add_up(part, f, 512, PARTS[part][1])

        def step(i, _):
            start = pl.multiple_of(i * 32, 32)
            g[part, pl.ds(start, 32), :] = sums(start, 32)
            return 0

        lax.fori_loop(0, 16, step, 0)
        send(3, part)
        h[part, own(axis, 128), :] = g[part, own(axis, 128), :]

    def final(part):
        arrive(3, part)
        return add_up(part, h, 128, PARTS[part][2])(0, 128)

    keep.wait()
    all_out_y(4).wait_recv()
    sy[own("y", 8), :] = sg[own("y", 8), :]
    core_y(4).start()
    across(0)
    for buf, axis, n in lines:
        all_line(buf, n).wait_recv()
    for src, buf, axis, n in planes:
        for dist in (1, 2, 3):
            plane(src, buf, axis, n, dist).start()
        buf[rows(me[axis] * 4096, 4096)] = src[...]
    core_y(4).wait_recv()
    core_y(0).wait_recv()
    panel0(0)
    across(1)
    across_b(1)
    across_b(3)
    core_y(1).wait_recv()
    panel0(1)
    whole(1)
    whole(3)
    across(2)
    core_y(2).wait_recv()
    panel0(2)

    def to_smem(i):
        return pltpu.make_async_copy(planes[i][1], (szy, sxy, sxz)[i], sm_sem.at[i])

    for i, (src, buf, axis, n) in enumerate(planes):
        all_plane(buf, n).wait_recv()
        to_smem(i).start()
    across(3)
    core_y(3).wait_recv()
    panel0(3)
    for i in range(3):
        to_smem(i).wait()
    turned(1)
    pruned(1, 2)
    turned(3)
    pruned(3, 2)
    pruned(1, 1)
    pruned(3, 1)
    pruned(1, 3)
    pruned(3, 3)
    pruned(1, 0)
    pruned(3, 0)
    pruned_y()
    scale = 1.0 / (128 * BLK) ** 0.5
    slot = lax.broadcasted_iota(jnp.int32, (128, 1), 0)
    count = cnt[0]

    def finish(panel, lower, upper):
        p0, p1 = final(lower), final(upper)
        cols = pl.ds(panel * 128, 128)
        lo = jnp.where(lane, p0, pltpu.roll(p1, HALF, 1)) * scale
        hi = jnp.where(lane, pltpu.roll(p0, HALF, 1), p1) * scale
        sk_out[pl.ds(0, 128), cols] = jnp.where(slot < count, lo, 0.0)
        sk_out[pl.ds(128, 128), cols] = jnp.where(slot + 128 < count, hi, 0.0)
        return jnp.concatenate(split(sk_out[:, cols]), axis=1)

    here = me["y"] * 4 + me["z"]

    def gram(p, q):
        out = lax.dot_general(p, q, (((0,), (0,)), ((), ())), preferred_element_type=jnp.float32)
        out = out[:128] + out[128:]
        return [out[:, i : i + 128] + out[:, i + 128 : i + 256] for i in range(0, out.shape[1], 256)]

    def piece(dx, o):
        to = {"y": (me["y"] + o // 4) % 4, "z": (me["z"] + o % 4) % 4, "x": (me["x"] + dx) % 4}
        src = to["x"] * 128 + (to["y"] * 4 + to["z"]) * 8
        dst = (here * 4 + me["x"]) * 8
        return remote(gp.at[rows(src, 8), :], rb.at[rows(dst, 8), :], rs_s.at[0], rs_r.at[0], moved(me, **to))

    def scatter(n):
        dx = (n - me["x"] + 4) % 4
        for o in FAR_PLANE:
            piece(dx, o).start()

        @pl.when(dx != 0)
        def _():
            piece(dx, 0).start()

    def pieces(count, of):
        most = pl.ds(0, count * 8)
        return remote(of.at[most, :], rb.at[most, :], rs_s.at[0], rs_r.at[0], other)

    last(1)
    last(3)
    for k in range(5):
        core_y(k).wait_send()
        all_out_y(k).wait_send()
    all_back_y().wait_send()
    for buf, axis, n in lines:
        all_line(buf, n).wait_send()
    for src, buf, axis, n in planes:
        all_plane(buf, n).wait_send()
    for part in (1, 3):
        core_b(part).wait_send()
        for stage in range(4):
            all_three(stage, part).wait_send()
    sk1 = finish(1, 1, 3)
    gp[pl.ds(384, 128), :] = gram(sk1, sk1)[0]
    scatter(3)
    last(0)
    last(2)
    sk0 = finish(0, 0, 2)
    first, second = gram(sk0, jnp.concatenate([sk0, sk1], axis=1))
    gp[pl.ds(0, 128), :] = first
    scatter(0)
    gp[pl.ds(128, 128), :] = second
    scatter(1)
    rb[rows((here * 4 + me["x"]) * 8, 8), :] = gp[rows(me["x"] * 128 + here * 8, 8), :]
    for stage in (2, 3):
        for part in (0, 2):
            all_three(stage, part).wait_send()
    mine = rows(here * 8, 8)

    def share(o, x):
        to = {"y": (me["y"] + o // 4) % 4, "z": (me["z"] + o % 4) % 4, "x": x}
        return remote(ob.at[mine, :], ob.at[mine, :], ag_s.at[0], ag_r.at[0], moved(me, **to))

    def shares(count):
        most = pl.ds(0, count * 8)
        return remote(rb.at[most, :], ob.at[most, :] if count < 17 else rb.at[most, :], ag_s.at[0], ag_r.at[0], other)

    @pl.when(me["x"] != 2)
    def _():
        pieces(63, rb).wait_recv()
        co[pl.ds(0, 8), :] = rb[...].reshape(64, 8, 128).sum(0) * (1.0 / (128 * 256))
        swap = remote(co.at[pl.ds(0, 8), :], co.at[pl.ds(8, 8), :], core_s.at[7], core_r.at[7], other)
        swap.start()
        pieces(47, gp).wait_send()
        swap.wait_recv()
        ob[mine, :] = co[pl.ds(0, 8), :] + co[pl.ds(8, 8), :]

        @pl.when(me["x"] == 1)
        def _():
            for o in (*FAR_PLANE, 0):
                share(o, 2).start()

        for o in FAR_PLANE:
            share(o, me["x"]).start()
        swap.wait_send()

        @pl.when(me["x"] == 1)
        def _():
            shares(31).wait_send()

        @pl.when(me["x"] != 1)
        def _():
            shares(15).wait_send()

        shares(15).wait_recv()
        gr_out[...] = ob[...]

    @pl.when(me["x"] == 2)
    def _():
        pieces(48, gp).wait_send()
        shares(16).wait_recv()
        gr_out[...] = ob[...].T


def hand_on(a, b, to_a, to_b):
    to_a[...] = a[...]
    to_b[...] = b[...]


def local(matrix, signs, indices, counts):
    f32, i32 = jnp.float32, jnp.int32
    vmem, smem, dma = pltpu.VMEM, pltpu.SMEM, pltpu.SemaphoreType.DMA
    in_vmem = pl.BlockSpec(memory_space=vmem)
    sketch, gram = pl.pallas_call(
        kernel,
        name="sketch_gram",
        out_shape=(jax.ShapeDtypeStruct((256, 256), f32), jax.ShapeDtypeStruct((128, 128), f32)),
        in_specs=[pl.BlockSpec(memory_space=pl.ANY), in_vmem, in_vmem, pl.BlockSpec(memory_space=smem)],
        out_specs=(in_vmem, in_vmem),
        scratch_shapes=[
            vmem((4096, 128), f32), vmem((2, 2048, 128), f32), vmem((128, 128), f32),
            vmem((4, 1024, 128), f32), vmem((4, 1024, 128), f32), vmem((32, 128), i32), vmem((32, 128), i32),
            vmem((4, 1024, 128), f32), vmem((4096, 128), f32), vmem((256, 128), f32),
            vmem((2, 2048, 128), f32), vmem((2, 2048, 128), f32), vmem((2, 2048, 128), f32),
            vmem((4096, 128), f32), vmem((4096, 128), f32),
            vmem((4, 2048, 128), f32), vmem((4, 2048, 128), f32),
            vmem((4, 512, 128), f32), vmem((4, 512, 128), f32),
            vmem((1024,), i32), vmem((4096,), i32), vmem((4096,), i32),
            vmem((16384,), i32), vmem((16384,), i32), vmem((16384,), i32),
            smem((16384,), i32), smem((16384,), i32), smem((16384,), i32),
            vmem((512, 128), f32), vmem((512, 128), f32), vmem((16, 128), f32), vmem((128, 128), f32),
            dma((2,)), dma((8,)), dma((8,)), dma((6,)), dma((6,)), dma((16,)), dma((16,)),
            dma((5,)), dma((5,)), dma((3,)), dma((1,)), dma((1,)), dma((1,)), dma((1,)),
        ],
        compiler_params=pltpu.CompilerParams(
            collective_id=0, has_side_effects=True, vmem_limit_bytes=56 * 2**20
        ),
    )(matrix, signs.reshape(32, 128), indices, counts)
    sketch, gram = pl.pallas_call(
        hand_on,
        name="hand_on",
        out_shape=(jax.ShapeDtypeStruct((256, 256), f32), jax.ShapeDtypeStruct((128, 128), f32)),
        in_specs=[in_vmem] * 2,
        out_specs=(in_vmem,) * 2,
    )(sketch, gram)
    return sketch, gram[None]


def solution(mesh):
    in_specs = (P(("rx", "ry"), None), P(("rx", "ry")), P(("rx", "ry")), P(("rx", "ry")))
    out_specs = (P(("rx", "ry"), None), P("ry", None, None))
    return jax.shard_map(local, mesh=mesh, in_specs=in_specs, out_specs=out_specs, check_vma=False)
```
